256 devices in a mesh: chan: 8 (over y_lo, x), lat: 32 (over z, y_hi, core).
Axes of the slice: x: 4, y: 4 (y_hi: 2, y_lo: 2; y = y_hi * 2 + y_lo), z: 8, core: 2. Of those that a mesh axis runs over, the one named last changes fastest.
Arguments:
- source_field: bfloat16 [384, 512, 1440], P('chan', 'lat'), may hold values from -6 to 6
- band_start: int32 [512], P('lat'), may hold values from -2 to 2, as said below
- band_width: int32 [512], P('lat'), may hold values from 1 to 4
- band_coef: bfloat16 [512, 4], P('lat'), may hold values from 0.049804688 to 0.59765625
- mixing_weight: bfloat16 [192, 384, 384], P('lat', 'chan'), may hold values from -0.3125 to 0.3125
- output_grad: bfloat16 [384, 512, 1440], P('chan', 'lat'), may hold values from -6 to 6
Outputs:
- mixed_field: bfloat16 [384, 512, 1440], P('chan', 'lat')
- grad_input: bfloat16 [384, 512, 1440], P('chan', 'lat')
- grad_mixing: float32 [192, 384, 384], P('lat', 'chan')
The draws below stay inside these ranges and needn't reach their ends.
Inputs may be any that keep to these rules, and one draw needn't show every extreme that they name: band_start[i] + band_width[i] <= 3 for every row i.
All inputs are finite; a program needn't handle non-finite values.
Results may differ from the reference program's by a relative error of at most 0.0085.
Values may be sent and summed in bfloat16 or wider, within the bound.
A program may use at most 128 MiB of HBM per device.

```python
import math
import jax
import jax.numpy as jnp
from jax import lax

C = 384
NLAT = 512
NLON = 1440
MMAX = 192
LMAX = 192
HALO = 2
WMAX = 4
N_CHAN = 8


def band_widths(key):
    target_rows = jnp.arange(NLAT, dtype=jnp.int32)
    widths = jax.random.randint(jax.random.fold_in(key, 11), (NLAT,), 1, WMAX + 1)
    widths = jnp.where(target_rows % 5 == 0, WMAX, widths)
    widths = jnp.where(target_rows % 5 == 1, 1, widths)
    return widths.astype(jnp.int32)


def draw_band_width(key, part):
    return band_widths(key)


def draw_band_start(key, part):
    widths = band_widths(key)
    key = jax.random.fold_in(key, 5)
    target_rows = jnp.arange(NLAT, dtype=jnp.int32)
    span = 2 * HALO + 2 - widths
    picked = jax.random.randint(key, (NLAT,), 0, span)
    starts = picked - HALO
    starts = jnp.where(target_rows % 10 == 0, -HALO, starts)
    starts = jnp.where(target_rows % 10 == 1, HALO, starts)
    return starts.astype(jnp.int32)


def block_scale(own_key, dims, split, low, top_value):
    gain, own = 1.0, jax.random.fold_in(own_key, 6)
    for dim, parts in split:
        draws = jnp.exp(jax.random.uniform(jax.random.fold_in(own, dim), (parts,), jnp.float32, low / len(split), top_value / len(split)))
        gain = gain * jnp.repeat(draws, dims[dim] // parts).reshape([-1 if axis == dim else 1 for axis in range(len(dims))])
    return gain


def normal_values(stream_key, extent, spread, reach, pieces=(), kind=jnp.bfloat16):
    factor_of = block_scale(stream_key, extent, pieces, -0.22, 0.18) if pieces else 1.0
    values = jax.random.normal(stream_key, extent, jnp.float32) * spread * factor_of
    return jnp.minimum(jnp.maximum(values, -reach), reach).astype(kind)


def setup_inputs(seed: int = 0) -> dict:
    streams_of = jax.random.split(jax.random.key(seed), 7)
    return {
        "source_field": normal_values(streams_of[0], (C, NLAT, NLON), 1.0, 6.0, ((0, 8), (1, 32))),
        "band_start": draw_band_start(jax.random.fold_in(streams_of[6], 71), 0),
        "band_width": draw_band_width(jax.random.fold_in(streams_of[6], 71), 0),
        "band_coef": jnp.clip(0.049804688 + 0.54785156 * jax.random.uniform(streams_of[3], (NLAT, WMAX), jnp.float32) ** block_scale(streams_of[3], (NLAT, WMAX), ((0, 32),), -0.2, 0.2), 0.049804688, 0.59765625).astype(jnp.bfloat16),
        "mixing_weight": normal_values(streams_of[4], (LMAX, C, C), C ** -0.5, 0.3125, ((0, 32), (1, 8))),
        "output_grad": normal_values(streams_of[5], (C, NLAT, NLON), 1.0, 6.0, ((0, 8), (1, 32))),
    }


def legendre_table(orders, row_count, degree_count):
    theta = math.pi * (jnp.arange(row_count, dtype=jnp.float32) + 0.5) / row_count
    cosine = jnp.cos(theta)
    sine = jnp.sin(theta)
    order = orders[:, None]
    log_sector = 0.5 * (jnp.log((2.0 * order + 1.0) / (4.0 * math.pi)) + lax.lgamma(order + 0.5) - lax.lgamma(order + 1.0) - 0.5 * math.log(math.pi)) + order * jnp.log(sine)[None, :]
    sector = jnp.exp(log_sector)

    def advance(carry, degree):
        previous, earlier = carry
        lower = degree - 1.0
        scale_a = jnp.sqrt(jnp.maximum(4.0 * degree * degree - 1.0, 0.0) / jnp.maximum(degree * degree - order * order, 1.0))
        scale_b = jnp.sqrt(jnp.maximum(lower * lower - order * order, 0.0) / jnp.maximum(4.0 * lower * lower - 1.0, 1.0))
        value = scale_a * (cosine[None, :] * previous - scale_b * earlier)
        value = jnp.where(degree < order, 0.0, jnp.where(degree == order, sector, value))
        return ((value, previous), value)
    initial = jnp.zeros((orders.shape[0], row_count), jnp.float32)
    _, table = lax.scan(advance, (initial, initial), jnp.arange(degree_count, dtype=jnp.float32), unroll=1)
    return (jnp.transpose(table, (1, 2, 0)), sine)

def spectral_tables(orders):
    legendre, sine = legendre_table(orders, NLAT, LMAX)
    quadrature = math.sqrt(NLAT) * math.pi / NLAT * sine
    analysis = (legendre * quadrature[None, :, None]).astype(jnp.bfloat16)
    synthesis = (jnp.transpose(legendre, (0, 2, 1)) * (1.0 / math.sqrt(LMAX))).astype(jnp.bfloat16)
    return (analysis, synthesis)

def fourier_tables():
    longitude = jnp.arange(NLON, dtype=jnp.int32)
    wavenumber = jnp.arange(MMAX, dtype=jnp.int32)
    phase = 2.0 * math.pi / NLON * (longitude[:, None] * wavenumber[None, :] % NLON).astype(jnp.float32)
    paired = jnp.concatenate([jnp.cos(phase), -jnp.sin(phase)], axis=1)
    lon_analysis = (paired * (1.0 / math.sqrt(NLON))).astype(jnp.bfloat16)
    lon_synthesis = (jnp.transpose(paired) * (1.0 / math.sqrt(MMAX))).astype(jnp.bfloat16)
    return (lon_analysis, lon_synthesis)

def reference(source_field, band_start, band_width, band_coef, mixing_weight, output_grad):
    lon_analysis, lon_synthesis = fourier_tables()
    analysis, synthesis = spectral_tables(jnp.arange(MMAX, dtype=jnp.float32))
    weight_degree = jnp.flip(mixing_weight, 0)
    target_rows = jnp.arange(NLAT, dtype=jnp.int32)
    padded = jnp.pad(source_field, ((0, 0), (HALO, HALO), (0, 0)))
    resampled = jnp.zeros(source_field.shape, jnp.float32)
    for offset in range(WMAX):
        position = (target_rows + HALO + band_start + offset).astype(jnp.int32)
        factor = jnp.where(band_width > offset, band_coef[:, offset].astype(jnp.float32), 0.0)
        resampled = resampled + factor[None, :, None] * jnp.take(padded, position, axis=1, mode='clip').astype(jnp.float32)
    resampled = resampled.astype(jnp.bfloat16)
    panels = jnp.dot(resampled.reshape(C * NLAT, NLON), lon_analysis, preferred_element_type=jnp.float32).astype(jnp.bfloat16)
    columns = jnp.transpose(panels.reshape(C, NLAT, 2, MMAX), (3, 2, 0, 1))
    coefficients = jnp.einsum('mrci,mil->mrcl', columns.astype(jnp.float32), analysis.astype(jnp.float32)).astype(jnp.bfloat16)
    group_size = C // N_CHAN
    mixed = jnp.zeros((MMAX, 2, C, LMAX), jnp.float32)
    for member in range(N_CHAN):
        lower = member * group_size
        block = coefficients[:, :, lower:lower + group_size, :].astype(jnp.float32)
        weights = weight_degree[:, lower:lower + group_size, :].astype(jnp.float32)
        partial_sum = jnp.einsum('mrcl,lco->mrol', block, weights).astype(jnp.bfloat16)
        mixed = mixed + lax.optimization_barrier(partial_sum).astype(jnp.float32)
    mixed = mixed.astype(jnp.bfloat16)
    synthesized = jnp.einsum('mrol,mli->mroi', mixed.astype(jnp.float32), synthesis.astype(jnp.float32)).astype(jnp.bfloat16)
    grid_panels = jnp.transpose(synthesized, (2, 3, 1, 0)).reshape(C * NLAT, 2 * MMAX)
    spectral = jnp.dot(grid_panels, lon_synthesis, preferred_element_type=jnp.float32).reshape(C, NLAT, NLON)
    mixed_field = (resampled.astype(jnp.float32) + spectral).astype(jnp.bfloat16)
    back_panels = jnp.dot(output_grad.reshape(C * NLAT, NLON), jnp.transpose(lon_synthesis), preferred_element_type=jnp.float32).astype(jnp.bfloat16)
    back_columns = jnp.transpose(back_panels.reshape(C, NLAT, 2, MMAX), (3, 2, 0, 1))
    back_mixed = jnp.einsum('mroi,mli->mrol', back_columns.astype(jnp.float32), synthesis.astype(jnp.float32)).astype(jnp.bfloat16)
    grad_degree = jnp.einsum('mrcl,mrol->lco', coefficients.astype(jnp.float32), back_mixed.astype(jnp.float32))
    grad_mixing = jnp.flip(grad_degree, 0)
    back_coef = jnp.einsum('mrol,lco->mrcl', back_mixed.astype(jnp.float32), weight_degree.astype(jnp.float32)).astype(jnp.bfloat16)
    back_grid = jnp.einsum('mrcl,mil->mrci', back_coef.astype(jnp.float32), analysis.astype(jnp.float32)).astype(jnp.bfloat16)
    back_grid = jnp.transpose(back_grid, (2, 3, 1, 0)).reshape(C * NLAT, 2 * MMAX)
    back_spectral = jnp.dot(back_grid, jnp.transpose(lon_analysis), preferred_element_type=jnp.float32).reshape(C, NLAT, NLON)
    back_field = (output_grad.astype(jnp.float32) + back_spectral).astype(jnp.bfloat16)
    grad_padded = jnp.zeros((C, NLAT + 2 * HALO, NLON), jnp.float32)
    for offset in range(WMAX):
        position = (target_rows + HALO + band_start + offset).astype(jnp.int32)
        factor = jnp.where(band_width > offset, band_coef[:, offset].astype(jnp.float32), 0.0)
        grad_padded = grad_padded.at[:, position, :].add(factor[None, :, None] * back_field.astype(jnp.float32), mode='drop')
    grad_input = grad_padded[:, HALO:HALO + NLAT, :].astype(jnp.bfloat16)
    return (mixed_field, grad_input, grad_mixing)
```

```python
import math

import jax
import jax.numpy as jnp
import numpy as np
from jax import lax
from jax.experimental import pallas as pl
from jax.experimental.pallas import tpu as pltpu
from jax.sharding import PartitionSpec as P

NLAT = 512
NLON = 1440
MMAX = 192
LMAX = 192
HALO = 2
LAT = 32
CHAN = 8
MODES = MMAX // LAT
ROWS = NLAT // LAT
MESH = pl.DeviceIdType.MESH
VMEM_LIMIT = 48 * 1024 * 1024


def log_norms():
    return np.array(
        [
            0.5
            * (
                math.log((2.0 * m + 1.0) / (4.0 * math.pi))
                + math.lgamma(m + 0.5)
                - math.lgamma(m + 1.0)
                - 0.5 * math.log(math.pi)
            )
            for m in range(MMAX)
        ],
        np.float32,
    )


def fourier_table():
    phase = 2.0 * math.pi / NLON * (np.outer(np.arange(NLON), np.arange(MMAX)) % NLON)
    return np.stack([np.cos(phase), -np.sin(phase)], axis=2).reshape(NLON, MMAX * 2)


def legendre_kernel(order_ref, cosine_ref, sector_ref, out_ref):
    order = jnp.broadcast_to(order_ref[...], (8, NLAT))
    cosine = jnp.broadcast_to(cosine_ref[...], (8, NLAT))
    sector = sector_ref[...]
    order_sq = order * order

    def advance(degree_index, carry):
        previous, earlier = carry
        degree = jnp.full((8, NLAT), degree_index, jnp.int32).astype(jnp.float32)
        lower = degree - 1.0
        scale_a = jnp.sqrt(
            jnp.maximum(4.0 * degree * degree - 1.0, 0.0)
            / jnp.maximum(degree * degree - order_sq, 1.0)
        )
        scale_b = jnp.sqrt(
            jnp.maximum(lower * lower - order_sq, 0.0)
            / jnp.maximum(4.0 * lower * lower - 1.0, 1.0)
        )
        value = scale_a * (cosine * previous - scale_b * earlier)
        value = jnp.where(degree < order, 0.0, jnp.where(degree == order, sector, value))
        out_ref[LMAX - 1 - degree_index] = value
        return value, previous

    zero = sector * 0.0
    lax.fori_loop(0, LMAX, advance, (zero, zero))


def legendre_tables():
    theta = math.pi * (np.arange(NLAT, dtype=np.float64) + 0.5) / NLAT
    cosine = np.cos(theta).astype(np.float32)[None, :]
    sine = np.sin(theta)
    orders = lax.axis_index("lat") * MODES + jnp.arange(8, dtype=jnp.int32)
    norm = jnp.asarray(np.concatenate([log_norms(), np.zeros(2, np.float32)]))
    order = orders.astype(jnp.float32)[:, None]
    own = lax.dynamic_slice(norm, (lax.axis_index("lat") * MODES,), (8,))
    sector = jnp.exp(own[:, None] + order * jnp.asarray(np.log(sine).astype(np.float32))[None, :])
    table = pl.pallas_call(
        legendre_kernel,
        out_shape=jax.ShapeDtypeStruct((LMAX, 8, NLAT), jnp.float32),
        in_specs=[pl.BlockSpec(memory_space=pltpu.VMEM)] * 3,
        out_specs=pl.BlockSpec(memory_space=pltpu.VMEM),
        compiler_params=pltpu.CompilerParams(vmem_limit_bytes=VMEM_LIMIT),
    )(order, jnp.asarray(cosine), sector)
    table = jnp.transpose(table[:, :MODES], (1, 0, 2))
    quadrature = (math.sqrt(NLAT) * math.pi / NLAT * sine).astype(np.float32)
    analysis = (table * jnp.asarray(quadrature)[None, None, :]).astype(jnp.bfloat16)
    synthesis = (table * (1.0 / math.sqrt(LMAX))).astype(jnp.bfloat16)
    return analysis, synthesis


def lat_to(step, lat, chan):
    other = lax.rem(lat + step, LAT)
    return other, chan, other, lat


def spectral_to(step, lat, chan):
    other = lax.rem(lat + step, LAT)
    return other, lax.div(lat, 4), other, lax.rem(lat, 4) * CHAN + chan


def spectral_from(step, lat, chan):
    quarter, group = lax.div(step, CHAN), lax.rem(chan + step, CHAN)
    return chan * 4 + quarter, group, quarter * CHAN + group, lat


def exchange_kernel(sends, receives, x_ref, out_ref, send_sem, recv_sem, own_sem):
    lat, chan = lax.axis_index("lat"), lax.axis_index("chan")
    barrier = pltpu.get_barrier_semaphore()

    def same(pair):
        return (pair[0] == lat) & (pair[1] == chan)

    def greet(step, count):
        source = receives(step, lat, chan)

        @pl.when(jnp.logical_not(same(source)))
        def _():
            pl.semaphore_signal(
                barrier, inc=1, device_id={"lat": source[0], "chan": source[1]},
                device_id_type=MESH,
            )

        return count + jnp.where(same(sends(step, lat, chan)), 0, 1)

    expected = lax.fori_loop(0, LAT, greet, jnp.int32(0))
    pl.semaphore_wait(barrier, expected)

    def remote(step, target):
        return pltpu.make_async_remote_copy(
            src_ref=x_ref.at[target[2]],
            dst_ref=out_ref.at[target[3]],
            send_sem=send_sem.at[target[2]],
            recv_sem=recv_sem.at[target[3]],
            device_id={"lat": target[0], "chan": target[1]},
            device_id_type=MESH,
        )

    def start(step, carry):
        target = sends(step, lat, chan)

        @pl.when(same(target))
        def _():
            pltpu.make_async_copy(x_ref.at[target[2]], out_ref.at[target[3]], own_sem).start()

        @pl.when(jnp.logical_not(same(target)))
        def _():
            remote(step, target).start()

        return carry

    lax.fori_loop(0, LAT, start, 0)

    def finish(step, carry):
        target = sends(step, lat, chan)
        source = receives(step, lat, chan)

        @pl.when(same(target))
        def _():
            pltpu.make_async_copy(x_ref.at[target[2]], out_ref.at[target[3]], own_sem).wait()

        @pl.when(jnp.logical_not(same(target)))
        def _():
            remote(step, target).wait_send()

        @pl.when(jnp.logical_not(same(source)))
        def _():
            pltpu.make_async_remote_copy(
                src_ref=x_ref.at[source[2]],
                dst_ref=out_ref.at[source[2]],
                send_sem=send_sem.at[source[2]],
                recv_sem=recv_sem.at[source[2]],
                device_id={"lat": source[0], "chan": source[1]},
                device_id_type=MESH,
            ).wait_recv()

        return carry

    lax.fori_loop(0, LAT, finish, 0)


def exchange(x, sends, receives, collective_id):
    import functools

    return pl.pallas_call(
        functools.partial(exchange_kernel, sends, receives),
        out_shape=jax.ShapeDtypeStruct(x.shape, x.dtype),
        in_specs=[pl.BlockSpec(memory_space=pl.ANY)],
        out_specs=pl.BlockSpec(memory_space=pl.ANY),
        scratch_shapes=[
            pltpu.SemaphoreType.DMA((LAT,)),
            pltpu.SemaphoreType.DMA((LAT,)),
            pltpu.SemaphoreType.DMA,
        ],
        compiler_params=pltpu.CompilerParams(
            collective_id=collective_id, has_side_effects=True, vmem_limit_bytes=VMEM_LIMIT
        ),
    )(x)


def with_halo(block):
    forward = [(i, i + 1) for i in range(LAT - 1)]
    backward = [(i + 1, i) for i in range(LAT - 1)]
    low = lax.ppermute(block[:, -HALO:], "lat", forward)
    high = lax.ppermute(block[:, :HALO], "lat", backward)
    return jnp.concatenate([low, block, high], axis=1)


def band_matrix(band_start, band_width, band_coef):
    row = jnp.concatenate(
        [
            band_start.astype(jnp.float32)[:, None],
            band_width.astype(jnp.float32)[:, None],
            band_coef.astype(jnp.float32),
        ],
        axis=1,
    )
    rows = lax.all_gather(row, "lat", axis=0, tiled=True)
    start = rows[:, 0:1].astype(jnp.int32)
    width = rows[:, 1:2].astype(jnp.int32)
    target = jnp.arange(NLAT, dtype=jnp.int32)[:, None]
    source = jnp.arange(NLAT, dtype=jnp.int32)[None, :]
    relative = source - target - start
    matrix = jnp.zeros((NLAT, NLAT), jnp.float32)
    for offset in range(4):
        keep = (relative == offset) & (width > offset)
        matrix = matrix + jnp.where(keep, rows[:, 2 + offset : 3 + offset], 0.0)
    return matrix.astype(jnp.bfloat16)


def dot(spec, a, b):
    return jnp.einsum(spec, a, b, preferred_element_type=jnp.float32)


def per_device(source_field, band_start, band_width, band_coef, mixing_weight, output_grad):
    lat = lax.axis_index("lat")
    channels = source_field.shape[0]
    table = fourier_table()
    lon_analysis = jnp.asarray((table / math.sqrt(NLON)).astype(jnp.bfloat16))
    lon_synthesis = jnp.asarray((table / math.sqrt(MMAX)).astype(jnp.bfloat16))

    weight = lax.all_gather(mixing_weight, "chan", axis=1, tiled=True)
    band = band_matrix(band_start, band_width, band_coef)
    padded_band = jnp.pad(band, HALO)
    band_rows = lax.dynamic_slice(padded_band, (lat * ROWS + HALO, lat * ROWS), (ROWS, ROWS + 4))
    band_cols = lax.dynamic_slice(padded_band, (lat * ROWS, lat * ROWS + HALO), (ROWS + 4, ROWS))

    analysis, synthesis = legendre_tables()
    banded = dot("mli,ij->mlj", analysis, band).astype(jnp.bfloat16)

    panels = jnp.stack(
        [
            dot("cin,nk->cik", source_field, lon_analysis).astype(jnp.bfloat16),
            dot("cin,nk->cik", output_grad, lon_synthesis).astype(jnp.bfloat16),
        ]
    )
    panels = panels.reshape(2, channels, ROWS, LAT, 3, 2, 2)
    panels = jnp.transpose(panels, (3, 4, 2, 5, 0, 6, 1)).reshape(LAT, 3, ROWS, 8 * channels)
    columns = exchange(panels, lat_to, lambda k, a, b: lat_to(LAT - k, a, b), 1)

    columns = columns.reshape(LAT, 3, ROWS, 2, 2, 2, channels)
    columns = jnp.transpose(columns, (4, 1, 3, 0, 2, 5, 6)).reshape(2, MODES, NLAT, 2 * channels)
    spectral = jnp.stack(
        [
            dot("mlj,mjk->mlk", banded, columns[0]).astype(jnp.bfloat16),
            dot("mlj,mjk->mlk", synthesis, columns[1]).astype(jnp.bfloat16),
        ]
    )
    message = jnp.transpose(
        spectral.reshape(2, MODES, LAT, 6, 2 * channels), (2, 0, 1, 3, 4)
    ).reshape(LAT, 54, 128)
    message = jnp.pad(message, ((0, 0), (0, 10), (0, 0)))

    def backwards(step, a, b):
        other = spectral_from(step, a, b)
        return other

    received = exchange(message, spectral_to, backwards, 2)
    received = received[:, :54].reshape(4, CHAN, 2, MODES, 6, 2, channels)
    received = jnp.transpose(received, (2, 4, 0, 3, 5, 1, 6)).reshape(2, 6, 48, CHAN * channels)
    coefficients, back_mixed = received[0], received[1]
    grad = dot("lkc,lko->lco", coefficients, back_mixed)
    grad_mixing = lax.psum_scatter(grad, "chan", scatter_dimension=1, tiled=True)
    mixed = dot("lkc,lco->lko", coefficients, weight).astype(jnp.bfloat16)
    back_coef = dot("lko,lco->lkc", back_mixed, weight).astype(jnp.bfloat16)
    reply = jnp.stack([mixed, back_coef]).reshape(2, 6, 4, MODES, 2, CHAN, channels)
    reply = jnp.transpose(reply, (2, 5, 0, 3, 1, 4, 6)).reshape(LAT, 54, 128)
    reply = jnp.pad(reply, ((0, 0), (0, 10), (0, 0)))

    def replies(step, a, b):
        other = lax.rem(a + step, LAT)
        return other, lax.div(a, 4), other, 0

    answers = exchange(reply, spectral_from, replies, 3)
    answers = answers[:, :54].reshape(LAT, 2, MODES, 6, 2 * channels)
    answers = jnp.transpose(answers, (1, 2, 0, 3, 4)).reshape(2, MODES, LMAX, 2 * channels)
    grids = jnp.stack(
        [
            dot("mlj,mlk->mjk", synthesis, answers[0]).astype(jnp.bfloat16),
            dot("mlj,mlk->mjk", banded, answers[1]).astype(jnp.bfloat16),
        ]
    )
    grids = grids.reshape(2, 3, 2, LAT, ROWS, 2, channels)
    grids = jnp.transpose(grids, (3, 1, 4, 2, 0, 5, 6)).reshape(LAT, 3, ROWS, 8 * channels)
    grids = exchange(grids, lat_to, lambda k, a, b: lat_to(LAT - k, a, b), 4)
    grids = grids.reshape(LAT, 3, ROWS, 2, 2, 2, channels)
    grids = jnp.transpose(grids, (4, 6, 2, 0, 1, 3, 5)).reshape(2, channels, ROWS, 2 * MMAX)

    mixed_field = dot("cik,nk->cin", grids[0], lon_synthesis) + dot(
        "ij,cjn->cin", band_rows, with_halo(source_field)
    )
    grad_input = dot("cik,nk->cin", grids[1], lon_analysis) + dot(
        "ji,cjn->cin", band_cols, with_halo(output_grad)
    )
    return (mixed_field.astype(jnp.bfloat16), grad_input.astype(jnp.bfloat16), grad_mixing)


def solution(mesh):
    in_specs = (
        P("chan", "lat", None),
        P("lat"),
        P("lat"),
        P("lat", None),
        P("lat", "chan", None),
        P("chan", "lat", None),
    )
    out_specs = (P("chan", "lat", None), P("chan", "lat", None), P("lat", "chan", None))
    return jax.shard_map(
        per_device, mesh=mesh, in_specs=in_specs, out_specs=out_specs, check_vma=False
    )
```

```python
import functools
import math

import jax
import jax.numpy as jnp
import numpy as np
from jax import lax
from jax.experimental import pallas as pl
from jax.experimental.pallas import tpu as pltpu
from jax.sharding import PartitionSpec as P

NLAT = 512
NLON = 1440
MMAX = 192
LMAX = 192
HALO = 2
LAT = 32
CHAN = 8
MODES = MMAX // LAT
ROWS = NLAT // LAT
MESH = pl.DeviceIdType.MESH
VMEM_LIMIT = 48 * 1024 * 1024


def log_norms():
    return np.array(
        [
            0.5
            * (
                math.log((2.0 * m + 1.0) / (4.0 * math.pi))
                + math.lgamma(m + 0.5)
                - math.lgamma(m + 1.0)
                - 0.5 * math.log(math.pi)
            )
            for m in range(MMAX)
        ],
        np.float32,
    )


def fourier_table():
    phase = 2.0 * math.pi / NLON * (np.outer(np.arange(NLON), np.arange(MMAX)) % NLON)
    return np.stack([np.cos(phase), -np.sin(phase)], axis=2).reshape(NLON, MMAX * 2)


def legendre_kernel(order_ref, cosine_ref, sector_ref, out_ref):
    order = jnp.broadcast_to(order_ref[...], (8, NLAT))
    cosine = jnp.broadcast_to(cosine_ref[...], (8, NLAT))
    sector = sector_ref[...]
    order_sq = order * order

    def advance(degree_index, carry):
        previous, earlier = carry
        degree = jnp.full((8, NLAT), degree_index, jnp.int32).astype(jnp.float32)
        lower = degree - 1.0
        scale_a = jnp.sqrt(
            jnp.maximum(4.0 * degree * degree - 1.0, 0.0)
            / jnp.maximum(degree * degree - order_sq, 1.0)
        )
        scale_b = jnp.sqrt(
            jnp.maximum(lower * lower - order_sq, 0.0)
            / jnp.maximum(4.0 * lower * lower - 1.0, 1.0)
        )
        value = scale_a * (cosine * previous - scale_b * earlier)
        value = jnp.where(degree < order, 0.0, jnp.where(degree == order, sector, value))
        out_ref[LMAX - 1 - degree_index] = value
        return value, previous

    zero = sector * 0.0
    lax.fori_loop(0, LMAX, advance, (zero, zero))


def legendre_tables():
    theta = math.pi * (np.arange(NLAT, dtype=np.float64) + 0.5) / NLAT
    cosine = np.cos(theta).astype(np.float32)[None, :]
    sine = np.sin(theta)
    orders = lax.axis_index("lat") * MODES + jnp.arange(8, dtype=jnp.int32)
    norm = jnp.asarray(np.concatenate([log_norms(), np.zeros(2, np.float32)]))
    order = orders.astype(jnp.float32)[:, None]
    own = lax.dynamic_slice(norm, (lax.axis_index("lat") * MODES,), (8,))
    sector = jnp.exp(own[:, None] + order * jnp.asarray(np.log(sine).astype(np.float32))[None, :])
    table = pl.pallas_call(
        legendre_kernel,
        out_shape=jax.ShapeDtypeStruct((LMAX, 8, NLAT), jnp.float32),
        in_specs=[pl.BlockSpec(memory_space=pltpu.VMEM)] * 3,
        out_specs=pl.BlockSpec(memory_space=pltpu.VMEM),
        compiler_params=pltpu.CompilerParams(vmem_limit_bytes=VMEM_LIMIT),
    )(order, jnp.asarray(cosine), sector)
    table = jnp.transpose(table[:, :MODES], (1, 0, 2))
    quadrature = (math.sqrt(NLAT) * math.pi / NLAT * sine).astype(np.float32)
    analysis = (table * jnp.asarray(quadrature)[None, None, :]).astype(jnp.bfloat16)
    synthesis = (table * (1.0 / math.sqrt(LMAX))).astype(jnp.bfloat16)
    return analysis, synthesis


def lat_to(step, lat, chan):
    other = lax.rem(lat + step, LAT)
    return other, chan, other, lat


def spectral_to(step, lat, chan):
    other = lax.rem(lat + step, LAT)
    return other, lax.div(lat, 4), other, lax.rem(lat, 4) * CHAN + chan


def spectral_from(step, lat, chan):
    quarter, group = lax.div(step, CHAN), lax.rem(chan + step, CHAN)
    return chan * 4 + quarter, group, quarter * CHAN + group, lat


def exchange_kernel(sends, receives, spread, *refs):
    if spread is None:
        x_ref, out_ref, send_sem, recv_sem, own_sem = refs
    else:
        x_ref, side_ref, out_ref, side_out_ref = refs[:4]
        send_sem, recv_sem, own_sem, side_send, side_recv, side_own = refs[4:]
    lat, chan = lax.axis_index("lat"), lax.axis_index("chan")
    barrier = pltpu.get_barrier_semaphore()

    def same(pair):
        return (pair[0] == lat) & (pair[1] == chan)

    def greet(step, count):
        source = receives(step, lat, chan)

        @pl.when(jnp.logical_not(same(source)))
        def _():
            pl.semaphore_signal(
                barrier, inc=1, device_id={"lat": source[0], "chan": source[1]},
                device_id_type=MESH,
            )

        return count + jnp.where(same(sends(step, lat, chan)), 0, 1)

    expected = lax.fori_loop(0, LAT, greet, jnp.int32(0))
    if spread is not None:

        def greet_side(step, count):
            pl.semaphore_signal(
                barrier, inc=1, device_id={"lat": lat, "chan": lax.rem(chan + step, CHAN)},
                device_id_type=MESH,
            )
            return count + 1

        expected = lax.fori_loop(1, CHAN, greet_side, expected)
    pl.semaphore_wait(barrier, expected)

    def remote(target):
        return pltpu.make_async_remote_copy(
            src_ref=x_ref.at[target[2]],
            dst_ref=out_ref.at[target[3]],
            send_sem=send_sem.at[target[2]],
            recv_sem=recv_sem.at[target[3]],
            device_id={"lat": target[0], "chan": target[1]},
            device_id_type=MESH,
        )

    def side(step, source):
        other = lax.rem(chan + step, CHAN)
        return pltpu.make_async_remote_copy(
            src_ref=side_ref.at[other] if spread == "parts" else side_ref,
            dst_ref=side_out_ref.at[other if source else chan],
            send_sem=side_send.at[other],
            recv_sem=side_recv.at[other if source else chan],
            device_id={"lat": lat, "chan": other},
            device_id_type=MESH,
        )

    def side_local():
        source = side_ref.at[chan] if spread == "parts" else side_ref
        return pltpu.make_async_copy(source, side_out_ref.at[chan], side_own)

    def start(step, carry):
        target = sends(step, lat, chan)

        @pl.when(same(target))
        def _():
            pltpu.make_async_copy(x_ref.at[target[2]], out_ref.at[target[3]], own_sem).start()

        @pl.when(jnp.logical_not(same(target)))
        def _():
            remote(target).start()

        return carry

    def start_side(step, carry):
        side(step, False).start()
        return carry

    lax.fori_loop(0, LAT, start, 0)
    if spread is not None:
        side_local().start()
        lax.fori_loop(1, CHAN, start_side, 0)

    def finish(step, carry):
        target = sends(step, lat, chan)
        source = receives(step, lat, chan)

        @pl.when(same(target))
        def _():
            pltpu.make_async_copy(x_ref.at[target[2]], out_ref.at[target[3]], own_sem).wait()

        @pl.when(jnp.logical_not(same(target)))
        def _():
            remote(target).wait_send()

        @pl.when(jnp.logical_not(same(source)))
        def _():
            remote((source[0], source[1], source[2], source[2])).wait_recv()

        return carry

    def finish_side(step, carry):
        side(step, False).wait_send()
        side(step, True).wait_recv()
        return carry

    lax.fori_loop(0, LAT, finish, 0)
    if spread is not None:
        side_local().wait()
        lax.fori_loop(1, CHAN, finish_side, 0)


def exchange(x, sends, receives, collective_id, spread=None, extra=None):
    arrays, shapes = [x], [jax.ShapeDtypeStruct(x.shape, x.dtype)]
    scratch = [
        pltpu.SemaphoreType.DMA((LAT,)),
        pltpu.SemaphoreType.DMA((LAT,)),
        pltpu.SemaphoreType.DMA,
    ]
    if spread is not None:
        shape = extra.shape if spread == "parts" else (CHAN,) + extra.shape
        arrays.append(extra)
        shapes.append(jax.ShapeDtypeStruct(shape, extra.dtype))
        scratch += [
            pltpu.SemaphoreType.DMA((CHAN,)),
            pltpu.SemaphoreType.DMA((CHAN,)),
            pltpu.SemaphoreType.DMA,
        ]
    out = pl.pallas_call(
        functools.partial(exchange_kernel, sends, receives, spread),
        out_shape=shapes,
        in_specs=[pl.BlockSpec(memory_space=pl.ANY)] * len(arrays),
        out_specs=[pl.BlockSpec(memory_space=pl.ANY)] * len(arrays),
        scratch_shapes=scratch,
        compiler_params=pltpu.CompilerParams(
            collective_id=collective_id, has_side_effects=True, vmem_limit_bytes=VMEM_LIMIT
        ),
    )(*arrays)
    return out if spread is not None else out[0]


def with_halo(block):
    forward = [(i, i + 1) for i in range(LAT - 1)]
    backward = [(i + 1, i) for i in range(LAT - 1)]
    low = lax.ppermute(block[:, -HALO:], "lat", forward)
    high = lax.ppermute(block[:, :HALO], "lat", backward)
    return jnp.concatenate([low, block, high], axis=1)


def band_matrix(band_start, band_width, band_coef):
    row = jnp.concatenate(
        [
            band_start.astype(jnp.float32)[:, None],
            band_width.astype(jnp.float32)[:, None],
            band_coef.astype(jnp.float32),
        ],
        axis=1,
    )
    rows = lax.all_gather(row, "lat", axis=0, tiled=True)
    start = rows[:, 0:1].astype(jnp.int32)
    width = rows[:, 1:2].astype(jnp.int32)
    target = jnp.arange(NLAT, dtype=jnp.int32)[:, None]
    source = jnp.arange(NLAT, dtype=jnp.int32)[None, :]
    relative = source - target - start
    matrix = jnp.zeros((NLAT, NLAT), jnp.float32)
    for offset in range(4):
        keep = (relative == offset) & (width > offset)
        matrix = matrix + jnp.where(keep, rows[:, 2 + offset : 3 + offset], 0.0)
    return matrix.astype(jnp.bfloat16)


def dot(spec, a, b):
    return jnp.einsum(spec, a, b, preferred_element_type=jnp.float32)


def per_device(source_field, band_start, band_width, band_coef, mixing_weight, output_grad):
    lat = lax.axis_index("lat")
    channels = source_field.shape[0]
    table = fourier_table()
    lon_analysis = jnp.asarray((table / math.sqrt(NLON)).astype(jnp.bfloat16))
    lon_synthesis = jnp.asarray((table / math.sqrt(MMAX)).astype(jnp.bfloat16))

    band = band_matrix(band_start, band_width, band_coef)
    padded_band = jnp.pad(band, HALO)
    band_rows = lax.dynamic_slice(padded_band, (lat * ROWS + HALO, lat * ROWS), (ROWS, ROWS + 4))
    band_cols = lax.dynamic_slice(padded_band, (lat * ROWS, lat * ROWS + HALO), (ROWS + 4, ROWS))

    analysis, synthesis = legendre_tables()
    banded = dot("mli,ij->mlj", analysis, band).astype(jnp.bfloat16)

    panels = jnp.stack(
        [
            dot("cin,nk->cik", source_field, lon_analysis).astype(jnp.bfloat16),
            dot("cin,nk->cik", output_grad, lon_synthesis).astype(jnp.bfloat16),
        ]
    )
    panels = panels.reshape(2, channels, ROWS, LAT, 3, 2, 2)
    panels = jnp.transpose(panels, (3, 4, 2, 5, 0, 6, 1)).reshape(LAT, 3, ROWS, 8 * channels)
    columns, weight = exchange(
        panels, lat_to, lambda k, a, b: lat_to(LAT - k, a, b), 1, "whole", mixing_weight
    )
    weight = jnp.transpose(weight, (1, 0, 2, 3)).reshape(6, CHAN * channels, CHAN * channels)

    columns = columns.reshape(LAT, 3, ROWS, 2, 2, 2, channels)
    columns = jnp.transpose(columns, (4, 1, 3, 0, 2, 5, 6)).reshape(2, MODES, NLAT, 2 * channels)
    spectral = jnp.stack(
        [
            dot("mlj,mjk->mlk", banded, columns[0]).astype(jnp.bfloat16),
            dot("mlj,mjk->mlk", synthesis, columns[1]).astype(jnp.bfloat16),
        ]
    )
    message = jnp.transpose(
        spectral.reshape(2, MODES, LAT, 6, 2 * channels), (2, 0, 1, 3, 4)
    ).reshape(LAT, 54, 128)
    message = jnp.pad(message, ((0, 0), (0, 10), (0, 0)))

    def backwards(step, a, b):
        other = spectral_from(step, a, b)
        return other

    received = exchange(message, spectral_to, backwards, 2)
    received = received[:, :54].reshape(4, CHAN, 2, MODES, 6, 2, channels)
    received = jnp.transpose(received, (2, 4, 0, 3, 5, 1, 6)).reshape(2, 6, 48, CHAN * channels)
    coefficients, back_mixed = received[0], received[1]
    grad = dot("lkc,lko->lco", coefficients, back_mixed).astype(jnp.bfloat16)
    grad = jnp.transpose(grad.reshape(6, CHAN, channels, CHAN * channels), (1, 0, 2, 3))
    mixed = dot("lkc,lco->lko", coefficients, weight).astype(jnp.bfloat16)
    back_coef = dot("lko,lco->lkc", back_mixed, weight).astype(jnp.bfloat16)
    reply = jnp.stack([mixed, back_coef]).reshape(2, 6, 4, MODES, 2, CHAN, channels)
    reply = jnp.transpose(reply, (2, 5, 0, 3, 1, 4, 6)).reshape(LAT, 54, 128)
    reply = jnp.pad(reply, ((0, 0), (0, 10), (0, 0)))

    def replies(step, a, b):
        other = lax.rem(a + step, LAT)
        return other, lax.div(a, 4), other, 0

    answers = exchange(reply, spectral_from, replies, 3)
    answers = answers[:, :54].reshape(LAT, 2, MODES, 6, 2 * channels)
    answers = jnp.transpose(answers, (1, 2, 0, 3, 4)).reshape(2, MODES, LMAX, 2 * channels)
    grids = jnp.stack(
        [
            dot("mlj,mlk->mjk", synthesis, answers[0]).astype(jnp.bfloat16),
            dot("mlj,mlk->mjk", banded, answers[1]).astype(jnp.bfloat16),
        ]
    )
    grids = grids.reshape(2, 3, 2, LAT, ROWS, 2, channels)
    grids = jnp.transpose(grids, (3, 1, 4, 2, 0, 5, 6)).reshape(LAT, 3, ROWS, 8 * channels)
    grids, grad_parts = exchange(
        grids, lat_to, lambda k, a, b: lat_to(LAT - k, a, b), 4, "parts", grad
    )
    grad_mixing = jnp.sum(grad_parts.astype(jnp.float32), axis=0)
    grids = grids.reshape(LAT, 3, ROWS, 2, 2, 2, channels)
    grids = jnp.transpose(grids, (4, 6, 2, 0, 1, 3, 5)).reshape(2, channels, ROWS, 2 * MMAX)

    mixed_field = dot("cik,nk->cin", grids[0], lon_synthesis) + dot(
        "ij,cjn->cin", band_rows, with_halo(source_field)
    )
    grad_input = dot("cik,nk->cin", grids[1], lon_analysis) + dot(
        "ji,cjn->cin", band_cols, with_halo(output_grad)
    )
    return (mixed_field.astype(jnp.bfloat16), grad_input.astype(jnp.bfloat16), grad_mixing)


def solution(mesh):
    in_specs = (
        P("chan", "lat", None),
        P("lat"),
        P("lat"),
        P("lat", None),
        P("lat", "chan", None),
        P("chan", "lat", None),
    )
    out_specs = (P("chan", "lat", None), P("chan", "lat", None), P("lat", "chan", None))
    return jax.shard_map(
        per_device, mesh=mesh, in_specs=in_specs, out_specs=out_specs, check_vma=False
    )
```

```python
import functools
import math

import jax
import jax.numpy as jnp
import numpy as np
from jax import lax
from jax.experimental import pallas as pl
from jax.experimental.pallas import tpu as pltpu
from jax.sharding import PartitionSpec as P

NLAT = 512
NLON = 1440
MMAX = 192
LMAX = 192
HALO = 2
LAT = 32
CHAN = 8
MODES = MMAX // LAT
ROWS = NLAT // LAT
MESH = pl.DeviceIdType.MESH
VMEM_LIMIT = 48 * 1024 * 1024


def log_norms():
    return np.array(
        [
            0.5
            * (
                math.log((2.0 * m + 1.0) / (4.0 * math.pi))
                + math.lgamma(m + 0.5)
                - math.lgamma(m + 1.0)
                - 0.5 * math.log(math.pi)
            )
            for m in range(MMAX)
        ],
        np.float32,
    )


def fourier_table():
    phase = 2.0 * math.pi / NLON * (np.outer(np.arange(NLON), np.arange(MMAX)) % NLON)
    table = np.zeros((NLON, 2, 256))
    table[:, 0, :MMAX] = np.cos(phase)
    table[:, 1, :MMAX] = -np.sin(phase)
    return table.reshape(NLON, 512)


def dense(a, b, dims=((1,), (0,))):
    return lax.dot_general(a, b, (dims, ((), ())), preferred_element_type=jnp.float32)


def iota(shape, axis):
    return lax.broadcasted_iota(jnp.int32, shape, axis)


def merge_lanes(a, b, c, d):
    lane = iota(a.shape, 1)
    return (
        jnp.where(lane < 96, a, b),
        jnp.where(lane < 64, b, c),
        jnp.where(lane < 32, c, d),
    )


def split_lanes(tiles):
    lane = iota(tiles[0].shape, 1)
    units = []
    for g in range(0, 9, 3):
        t0, t1, t2 = tiles[g : g + 3]
        units += [t0, jnp.where(lane < 64, t1, t0), jnp.where(lane < 32, t2, t1), t2]
    return units


def merge_rows(tiles):
    row = iota(tiles[0].shape, 0) % 8
    out = list(tiles[:8])
    for k in range(3):
        out[k] = jnp.where(row < 6, tiles[k], pltpu.roll(tiles[8], 6 - 2 * k, 0))
    return out


def split_rows(tiles):
    rows = tiles[0].shape[0]
    row = iota(tiles[0].shape, 0) % 8
    back = [pltpu.roll(tiles[k], rows - (6 - 2 * k), 0) for k in range(3)]
    return list(tiles) + [jnp.where(row < 2, back[0], jnp.where(row < 4, back[1], back[2]))]


def store_rows(out_ref, tiles):
    for p in range(4):
        pair = [tiles[2 * p + k].reshape(LAT, 8, 128) for k in range(2)]
        out_ref[:, 16 * p : 16 * p + 16, :] = jnp.concatenate(pair, axis=1).astype(jnp.bfloat16)


def load_rows(in_ref):
    tiles = []
    for p in range(4):
        pair = in_ref[:, 16 * p : 16 * p + 16, :].astype(jnp.float32)
        tiles += [pair[:, :8].reshape(256, 128), pair[:, 8:].reshape(256, 128)]
    return tiles


def spread_kernel(source_ref, grad_ref, band_ref, out_ref, part, rows):
    for f, ref in ((0, source_ref), (1, grad_ref)):
        for k in range(4):
            part[k] = ref[:, 128 * k : 128 * k + 128].astype(jnp.float32)

        def turn(i, carry):
            for half, count in ((0, 128), (1, 64)):
                a = part[half, pl.ds(i, 48, stride=16), :]
                b = part[2 + half, pl.ds(i, 48, stride=16), :]
                block = jnp.concatenate([a, b, a[:32]], axis=0).T
                rows[f, pl.ds(half * 2048 + i, count, stride=16), :] = block[:count]
            return carry

        lax.fori_loop(0, ROWS, turn, 0)

    def send(d, carry):
        units = [
            rows[f, pl.ds(pl.multiple_of((d * 6 + m) * 16, 16), 16), :]
            for f in range(2)
            for m in range(MODES)
        ]
        for g in range(3):
            a, b, c, e = units[4 * g : 4 * g + 4]
            tiles = merge_lanes(a, pltpu.roll(b, 96, 1), pltpu.roll(c, 64, 1), pltpu.roll(e, 32, 1))
            for k in range(3):
                out_ref[d, 3 * g + k] = tiles[k].astype(jnp.bfloat16)
        out_ref[d, 9] = band_ref[...]
        return carry

    lax.fori_loop(0, LAT, send, 0)


def gather_kernel(in_ref, source_ref, grad_ref, part, rows):
    def receive(d, carry):
        tiles = [in_ref[d, k].astype(jnp.float32) for k in range(9)]
        units = split_lanes(tiles)
        for u in range(12):
            if u % 4:
                units[u] = pltpu.roll(units[u], 32 * (u % 4), 1)
            rows[u // 6, pl.ds(pl.multiple_of((d * 6 + u % 6) * 16, 16), 16), :] = units[u]
        return carry

    lax.fori_loop(0, LAT, receive, 0)
    for f, ref in ((0, source_ref), (1, grad_ref)):

        def turn(i, carry):
            block = rows[f, pl.ds(i, MMAX, stride=16), :]
            halves = (block[:128], jnp.concatenate([block[128:], jnp.zeros((64, 128), jnp.float32)], axis=0))
            for half in range(2):
                flat = halves[half].T
                part[half, pl.ds(i, 48, stride=16), :] = flat[:48]
                part[2 + half, pl.ds(i, 48, stride=16), :] = flat[48:96]
            return carry

        lax.fori_loop(0, ROWS, turn, 0)
        for k in range(4):
            ref[:, 128 * k : 128 * k + 128] = part[k].astype(jnp.bfloat16)


def table_kernel(order_ref, cosine_ref, sector_ref, quad_ref, band_ref, near_ref, far_ref, table):
    order = jnp.broadcast_to(order_ref[...], (8, NLAT))
    cosine = jnp.broadcast_to(cosine_ref[...], (8, NLAT))
    sector = sector_ref[...]
    order_sq = order * order
    table[...] = jnp.zeros_like(table)

    def advance(degree_index, carry):
        previous, earlier = carry
        degree = jnp.full((8, NLAT), degree_index, jnp.int32).astype(jnp.float32)
        lower = degree - 1.0
        scale_a = jnp.sqrt(
            jnp.maximum(4.0 * degree * degree - 1.0, 0.0)
            / jnp.maximum(degree * degree - order_sq, 1.0)
        )
        scale_b = jnp.sqrt(
            jnp.maximum(lower * lower - order_sq, 0.0)
            / jnp.maximum(4.0 * lower * lower - 1.0, 1.0)
        )
        value = scale_a * (cosine * previous - scale_b * earlier)
        value = jnp.where(degree < order, 0.0, jnp.where(degree == order, sector, value))
        place = LMAX - 1 - degree_index
        row = place // 6 * 8 + place % 6
        for k in range(4):
            table[k, pl.ds(row, 8, stride=256), :] = value[:, 128 * k : 128 * k + 128]
        return value, previous

    zero = sector * 0.0
    lax.fori_loop(0, LMAX, advance, (zero, zero))

    info = band_ref[...].reshape(NLAT, 128).astype(jnp.float32)
    relative = (iota((NLAT, NLAT), 1) - iota((NLAT, NLAT), 0)).astype(jnp.float32) - info[:, 0:1]
    band = jnp.zeros((NLAT, NLAT), jnp.float32)
    for k in range(4):
        keep = (relative == float(k)) & (info[:, 1:2] > float(k))
        band = band + jnp.where(keep, info[:, 2 + k : 3 + k], 0.0)
    band = band.astype(jnp.bfloat16)
    for m in range(MODES):
        own = jnp.concatenate([table[k, 256 * m : 256 * m + 256, :] for k in range(4)], axis=1)
        analysis = (own * quad_ref[...]).astype(jnp.bfloat16)
        banded = dense(analysis, band)
        synthesis = own * (1.0 / math.sqrt(LMAX))
        near_ref[m] = banded.astype(jnp.bfloat16)
        near_ref[MODES + m] = synthesis.astype(jnp.bfloat16)
        far_ref[m] = synthesis.T.astype(jnp.bfloat16)
        far_ref[MODES + m] = banded.T.astype(jnp.bfloat16)


def analysis_kernel(in_ref, table_ref, out_ref):
    tiles = [in_ref[:, k].reshape(NLAT, 128).astype(jnp.float32) for k in range(9)]
    units = split_lanes(tiles)
    units = [dense(table_ref[u], units[u].astype(jnp.bfloat16)) for u in range(12)]
    packed = []
    for g in range(3):
        packed += merge_lanes(*units[4 * g : 4 * g + 4])
    store_rows(out_ref, merge_rows(packed))


def synthesis_kernel(in_ref, table_ref, out_ref):
    units = split_lanes(split_rows(load_rows(in_ref)))
    units = [dense(table_ref[u], units[u].astype(jnp.bfloat16)) for u in range(12)]
    for g in range(3):
        tiles = merge_lanes(*units[4 * g : 4 * g + 4])
        for k in range(3):
            out_ref[:, 3 * g + k] = tiles[k].reshape(LAT, ROWS, 128).astype(jnp.bfloat16)


def mixing_kernel(in_ref, weight_ref, pick_ref, pick_t_ref, out_ref, grad_ref, before, after):
    units = split_lanes(split_rows(load_rows(in_ref)))
    for u in range(12):
        if u % 4:
            units[u] = pltpu.roll(units[u], 32 * (u % 4), 1)
        f, m = u // 6, u % 6
        before[f, :, 32 * m : 32 * m + 32, :] = units[u].reshape(CHAN, 32, 128)
    after[...] = jnp.zeros_like(after)
    lane = iota((24, 128), 1)

    def degree(l, carry):
        left = []
        for f in range(2):
            columns = []
            for p in range(4):
                a = before[f, 2 * p, pl.ds(l, 24, stride=8), :]
                b = before[f, 2 * p + 1, pl.ds(l, 24, stride=8), :]
                first = jnp.where(lane < 64, a, pltpu.roll(b, 64, 1))
                second = jnp.where(lane < 64, pltpu.roll(a, 80, 1), pltpu.roll(b, 16, 1))
                columns.append(jnp.concatenate([first, second], axis=0))
            left.append(jnp.concatenate(columns, axis=1).astype(jnp.bfloat16))
        rows = []
        for e in range(CHAN):
            rows += [weight_ref[e, l], jnp.zeros((16, 384), jnp.bfloat16)]
        weight = dense(jnp.concatenate(rows, axis=0), pick_ref[...]).astype(jnp.bfloat16)
        mixed = dense(left[0], weight)
        back = dense(left[1], weight, ((1,), (1,)))
        dense_back = dense(left[1], pick_t_ref[...]).astype(jnp.bfloat16)
        grad = dense(left[0], dense_back, ((0,), (0,)))
        for e in range(CHAN):
            grad_ref[e, l] = grad[64 * e : 64 * e + 48].astype(jnp.bfloat16)
            for f, value in ((0, mixed), (1, back)):
                tile = value[:, 128 * (e // 2) : 128 * (e // 2) + 128]
                first, second = tile[:24], tile[24:]
                if e % 2:
                    first = pltpu.roll(first, 64, 1)
                second = pltpu.roll(second, 112 if e % 2 else 48, 1)
                after[f, e, pl.ds(l, 24, stride=8), :] = jnp.where(lane < 48, first, second)
        return carry

    lax.fori_loop(0, 6, degree, 0)
    units = [after[u // 6, :, 32 * (u % 6) : 32 * (u % 6) + 32, :].reshape(256, 128) for u in range(12)]
    packed = []
    for g in range(3):
        a, b, c, d = units[4 * g : 4 * g + 4]
        packed += merge_lanes(a, pltpu.roll(b, 96, 1), pltpu.roll(c, 64, 1), pltpu.roll(d, 32, 1))
    store_rows(out_ref, merge_rows(packed))


def local(kernel, shapes, scratch, *arrays):
    single = not isinstance(shapes, list)
    spec = pl.BlockSpec(memory_space=pltpu.VMEM)
    return pl.pallas_call(
        kernel,
        out_shape=shapes,
        in_specs=[spec] * len(arrays),
        out_specs=spec if single else [spec] * len(shapes),
        scratch_shapes=scratch,
        compiler_params=pltpu.CompilerParams(vmem_limit_bytes=VMEM_LIMIT),
    )(*arrays)


def bf16(*shape):
    return jax.ShapeDtypeStruct(shape, jnp.bfloat16)


def legendre_tables(band_rows):
    theta = math.pi * (np.arange(NLAT, dtype=np.float64) + 0.5) / NLAT
    cosine = np.cos(theta).astype(np.float32)[None, :]
    sine = np.sin(theta)
    orders = lax.axis_index("lat") * MODES + jnp.arange(8, dtype=jnp.int32)
    norm = jnp.asarray(np.concatenate([log_norms(), np.zeros(2, np.float32)]))
    order = orders.astype(jnp.float32)[:, None]
    own = lax.dynamic_slice(norm, (lax.axis_index("lat") * MODES,), (8,))
    sector = jnp.exp(own[:, None] + order * jnp.asarray(np.log(sine).astype(np.float32))[None, :])
    quadrature = (math.sqrt(NLAT) * math.pi / NLAT * sine).astype(np.float32)[None, :]
    return local(
        table_kernel,
        [bf16(12, 256, NLAT), bf16(12, NLAT, 256)],
        [pltpu.VMEM((4, 2048, 128), jnp.float32)],
        order,
        jnp.asarray(cosine),
        sector,
        jnp.asarray(quadrature),
        band_rows,
    )


def lat_to(step, lat, chan):
    other = lax.rem(lat + step, LAT)
    return other, chan, other, lat


def spectral_to(step, lat, chan):
    other = lax.rem(lat + step, LAT)
    group = 2 * lax.rem(lat, 4) + lax.rem(lax.div(lat, 4), 2)
    return other, group, other, chan * 4 + lax.div(lat, 8)


def spectral_from(step, lat, chan):
    part = lax.rem(step + lat, 4)
    group = lax.rem(lax.div(step, 4) + chan, CHAN)
    other = (2 * part + lax.rem(chan, 2)) * 4 + lax.div(chan, 2)
    return other, group, group * 4 + part, lat


def degree_owner(step, lat, chan):
    other = lax.rem(lat + LAT - step, LAT)
    group = 2 * lax.rem(lat, 4) + lax.rem(lax.div(lat, 4), 2)
    return other, group, other, 0


def exchange_kernel(sends, receives, spread, *refs):
    if spread is None:
        x_ref, out_ref, send_sem, recv_sem, own_sem = refs
    else:
        x_ref, side_ref, out_ref, side_out_ref = refs[:4]
        send_sem, recv_sem, own_sem, side_send, side_recv, side_own = refs[4:]
    lat, chan = lax.axis_index("lat"), lax.axis_index("chan")
    barrier = pltpu.get_barrier_semaphore()

    def same(pair):
        return (pair[0] == lat) & (pair[1] == chan)

    def greet(step, count):
        source = receives(step, lat, chan)

        @pl.when(jnp.logical_not(same(source)))
        def _():
            pl.semaphore_signal(
                barrier, inc=1, device_id={"lat": source[0], "chan": source[1]},
                device_id_type=MESH,
            )

        return count + jnp.where(same(sends(step, lat, chan)), 0, 1)

    expected = lax.fori_loop(0, LAT, greet, jnp.int32(0))
    if spread is not None:

        def greet_side(step, count):
            pl.semaphore_signal(
                barrier, inc=1, device_id={"lat": lat, "chan": lax.rem(chan + step, CHAN)},
                device_id_type=MESH,
            )
            return count + 1

        expected = lax.fori_loop(1, CHAN, greet_side, expected)
    pl.semaphore_wait(barrier, expected)

    def remote(target):
        return pltpu.make_async_remote_copy(
            src_ref=x_ref.at[target[2]],
            dst_ref=out_ref.at[target[3]],
            send_sem=send_sem.at[target[2]],
            recv_sem=recv_sem.at[target[3]],
            device_id={"lat": target[0], "chan": target[1]},
            device_id_type=MESH,
        )

    def side(step, source):
        other = lax.rem(chan + step, CHAN)
        return pltpu.make_async_remote_copy(
            src_ref=side_ref.at[other] if spread == "parts" else side_ref,
            dst_ref=side_out_ref.at[other if source else chan],
            send_sem=side_send.at[other],
            recv_sem=side_recv.at[other if source else chan],
            device_id={"lat": lat, "chan": other},
            device_id_type=MESH,
        )

    def side_local():
        source = side_ref.at[chan] if spread == "parts" else side_ref
        return pltpu.make_async_copy(source, side_out_ref.at[chan], side_own)

    def start(step, carry):
        target = sends(step, lat, chan)

        @pl.when(same(target))
        def _():
            pltpu.make_async_copy(x_ref.at[target[2]], out_ref.at[target[3]], own_sem).start()

        @pl.when(jnp.logical_not(same(target)))
        def _():
            remote(target).start()

        return carry

    def start_side(step, carry):
        side(step, False).start()
        return carry

    lax.fori_loop(0, LAT, start, 0)
    if spread is not None:
        side_local().start()
        lax.fori_loop(1, CHAN, start_side, 0)

    def finish(step, carry):
        target = sends(step, lat, chan)
        source = receives(step, lat, chan)

        @pl.when(same(target))
        def _():
            pltpu.make_async_copy(x_ref.at[target[2]], out_ref.at[target[3]], own_sem).wait()

        @pl.when(jnp.logical_not(same(target)))
        def _():
            remote(target).wait_send()

        @pl.when(jnp.logical_not(same(source)))
        def _():
            remote((source[0], source[1], source[2], source[2])).wait_recv()

        return carry

    def finish_side(step, carry):
        side(step, False).wait_send()
        side(step, True).wait_recv()
        return carry

    lax.fori_loop(0, LAT, finish, 0)
    if spread is not None:
        side_local().wait()
        lax.fori_loop(1, CHAN, finish_side, 0)


def exchange(x, sends, receives, collective_id, spread=None, extra=None):
    arrays, shapes = [x], [jax.ShapeDtypeStruct(x.shape, x.dtype)]
    scratch = [
        pltpu.SemaphoreType.DMA((LAT,)),
        pltpu.SemaphoreType.DMA((LAT,)),
        pltpu.SemaphoreType.DMA,
    ]
    if spread is not None:
        shape = extra.shape if spread == "parts" else (CHAN,) + extra.shape
        arrays.append(extra)
        shapes.append(jax.ShapeDtypeStruct(shape, extra.dtype))
        scratch += [
            pltpu.SemaphoreType.DMA((CHAN,)),
            pltpu.SemaphoreType.DMA((CHAN,)),
            pltpu.SemaphoreType.DMA,
        ]
    out = pl.pallas_call(
        functools.partial(exchange_kernel, sends, receives, spread),
        out_shape=shapes,
        in_specs=[pl.BlockSpec(memory_space=pl.ANY)] * len(arrays),
        out_specs=[pl.BlockSpec(memory_space=pl.ANY)] * len(arrays),
        scratch_shapes=scratch,
        compiler_params=pltpu.CompilerParams(
            collective_id=collective_id, has_side_effects=True, vmem_limit_bytes=VMEM_LIMIT
        ),
    )(*arrays)
    return out if spread is not None else out[0]


def with_halo(block):
    forward = [(i, i + 1) for i in range(LAT - 1)]
    backward = [(i + 1, i) for i in range(LAT - 1)]
    low = lax.ppermute(block[:, -HALO:], "lat", forward)
    high = lax.ppermute(block[:, :HALO], "lat", backward)
    return jnp.concatenate([low, block, high], axis=1)


def dot(spec, a, b):
    return jnp.einsum(spec, a, b, preferred_element_type=jnp.float32)


def local_band(start, width, coef, low):
    count = start.shape[0]
    target = jnp.arange(count, dtype=jnp.int32)[:, None]
    source = jnp.arange(ROWS + 4 if low else ROWS, dtype=jnp.int32)[None, :]
    relative = source - target - (HALO if low else -HALO) - start[:, None]
    matrix = jnp.zeros(relative.shape, jnp.float32)
    for offset in range(4):
        keep = (relative == offset) & (width[:, None] > offset)
        matrix = matrix + jnp.where(keep, coef[:, offset : offset + 1], 0.0)
    return matrix.astype(jnp.bfloat16)


def per_device(source_field, band_start, band_width, band_coef, mixing_weight, output_grad):
    lat = lax.axis_index("lat")
    channels = source_field.shape[0]
    table = fourier_table()
    lon_analysis = jnp.asarray((table / math.sqrt(NLON)).astype(jnp.bfloat16))
    lon_synthesis = jnp.asarray((table / math.sqrt(MMAX)).astype(jnp.bfloat16))
    flat = channels * ROWS

    info = jnp.concatenate(
        [
            band_start.astype(jnp.bfloat16)[:, None],
            band_width.astype(jnp.bfloat16)[:, None],
            band_coef,
            jnp.zeros((ROWS, 122), jnp.bfloat16),
        ],
        axis=1,
    )
    message = local(
        spread_kernel,
        bf16(LAT, 10, ROWS, 128),
        [pltpu.VMEM((4, flat, 128), jnp.float32), pltpu.VMEM((2, MMAX * ROWS, 128), jnp.float32)],
        dot("ik,kn->in", source_field.reshape(flat, NLON), lon_analysis).astype(jnp.bfloat16),
        dot("ik,kn->in", output_grad.reshape(flat, NLON), lon_synthesis).astype(jnp.bfloat16),
        info,
    )
    columns, weight = exchange(
        message, lat_to, lambda k, a, b: lat_to(LAT - k, a, b), 1, "whole", mixing_weight
    )
    band_rows = columns[:, 9]
    near, far = legendre_tables(band_rows)
    message = local(analysis_kernel, bf16(LAT, 64, 128), [], columns, near)
    received = exchange(message, spectral_to, spectral_from, 2)

    pick = np.zeros((CHAN, channels, CHAN, 64), np.float32)
    for e in range(CHAN):
        pick[e, :, e, :channels] = np.eye(channels)
    pick = pick.reshape(CHAN * channels, 512)
    panel = pltpu.VMEM((2, CHAN, 192, 128), jnp.float32)
    reply, grad = local(
        mixing_kernel,
        [bf16(LAT, 64, 128), bf16(CHAN, 6, channels, CHAN * channels)],
        [panel, panel],
        received,
        weight,
        jnp.asarray(pick.astype(jnp.bfloat16)),
        jnp.asarray(pick.T.astype(jnp.bfloat16)),
    )
    answers = exchange(reply, spectral_from, degree_owner, 3)
    message = local(synthesis_kernel, bf16(LAT, 9, ROWS, 128), [], answers, far)
    grids, grad_parts = exchange(
        message, lat_to, lambda k, a, b: lat_to(LAT - k, a, b), 4, "parts", grad
    )
    grad_mixing = jnp.sum(grad_parts.astype(jnp.float32), axis=0)
    forward, backward = local(
        gather_kernel,
        [bf16(flat, 512), bf16(flat, 512)],
        [pltpu.VMEM((4, flat, 128), jnp.float32), pltpu.VMEM((2, MMAX * ROWS, 128), jnp.float32)],
        grids,
    )

    rows = jnp.pad(band_rows.reshape(NLAT, 128), ((HALO, HALO), (0, 0)))
    rows = lax.dynamic_slice(rows, (lat * ROWS, 0), (ROWS + 4, 128)).astype(jnp.float32)
    start, width, coef = rows[:, 0].astype(jnp.int32), rows[:, 1].astype(jnp.int32), rows[:, 2:6]
    own = slice(HALO, HALO + ROWS)
    band_ahead = local_band(start[own], width[own], coef[own], True)
    band_back = local_band(start, width, coef, False)
    mixed_field = dot("ik,nk->in", forward, lon_synthesis).reshape(channels, ROWS, NLON) + dot(
        "ij,cjn->cin", band_ahead, with_halo(source_field)
    )
    grad_input = dot("ik,nk->in", backward, lon_analysis).reshape(channels, ROWS, NLON) + dot(
        "ji,cjn->cin", band_back, with_halo(output_grad)
    )
    return (mixed_field.astype(jnp.bfloat16), grad_input.astype(jnp.bfloat16), grad_mixing)


def solution(mesh):
    in_specs = (
        P("chan", "lat", None),
        P("lat"),
        P("lat"),
        P("lat", None),
        P("lat", "chan", None),
        P("chan", "lat", None),
    )
    out_specs = (P("chan", "lat", None), P("chan", "lat", None), P("lat", "chan", None))
    return jax.shard_map(
        per_device, mesh=mesh, in_specs=in_specs, out_specs=out_specs, check_vma=False
    )
```

```python
import functools
import math

import jax
import jax.numpy as jnp
import numpy as np
from jax import lax
from jax.experimental import pallas as pl
from jax.experimental.pallas import tpu as pltpu
from jax.sharding import PartitionSpec as P

NLAT = 512
NLON = 1440
MMAX = 192
LMAX = 192
HALO = 2
LAT = 32
CHAN = 8
MODES = MMAX // LAT
ROWS = NLAT // LAT
MESH = pl.DeviceIdType.MESH
VMEM_LIMIT = 48 * 1024 * 1024


def log_norms():
    return np.array(
        [
            0.5
            * (
                math.log((2.0 * m + 1.0) / (4.0 * math.pi))
                + math.lgamma(m + 0.5)
                - math.lgamma(m + 1.0)
                - 0.5 * math.log(math.pi)
            )
            for m in range(MMAX)
        ],
        np.float32,
    )


def fourier_table():
    phase = 2.0 * math.pi / NLON * (np.outer(np.arange(NLON), np.arange(MMAX)) % NLON)
    table = np.zeros((NLON, 2, 256))
    table[:, 0, :MMAX] = np.cos(phase)
    table[:, 1, :MMAX] = -np.sin(phase)
    return table.reshape(NLON, 512)


def dense(a, b, dims=((1,), (0,))):
    return lax.dot_general(a, b, (dims, ((), ())), preferred_element_type=jnp.float32)


def iota(shape, axis):
    return lax.broadcasted_iota(jnp.int32, shape, axis)


def merge_lanes(a, b, c, d):
    lane = iota(a.shape, 1)
    return (
        jnp.where(lane < 96, a, b),
        jnp.where(lane < 64, b, c),
        jnp.where(lane < 32, c, d),
    )


def split_lanes(tiles):
    lane = iota(tiles[0].shape, 1)
    units = []
    for g in range(0, 9, 3):
        t0, t1, t2 = tiles[g : g + 3]
        units += [t0, jnp.where(lane < 64, t1, t0), jnp.where(lane < 32, t2, t1), t2]
    return units


def merge_rows(tiles):
    row = iota(tiles[0].shape, 0) % 8
    out = list(tiles[:8])
    for k in range(3):
        out[k] = jnp.where(row < 6, tiles[k], pltpu.roll(tiles[8], 6 - 2 * k, 0))
    return out


def split_rows(tiles):
    rows = tiles[0].shape[0]
    row = iota(tiles[0].shape, 0) % 8
    back = [pltpu.roll(tiles[k], rows - (6 - 2 * k), 0) for k in range(3)]
    return list(tiles) + [jnp.where(row < 2, back[0], jnp.where(row < 4, back[1], back[2]))]


def store_rows(out_ref, tiles):
    for p in range(4):
        pair = [tiles[2 * p + k].reshape(LAT, 8, 128) for k in range(2)]
        out_ref[:, 16 * p : 16 * p + 16, :] = jnp.concatenate(pair, axis=1).astype(jnp.bfloat16)


def load_rows(in_ref, live):
    tiles = []
    for p in range(4):
        pair = in_ref[:, 16 * p : 16 * p + 16, :].astype(jnp.float32)
        pair = jnp.where(live, pair, 0.0)
        tiles += [pair[:, :8].reshape(256, 128), pair[:, 8:].reshape(256, 128)]
    return tiles


def spread_kernel(source_ref, grad_ref, out_ref, part, rows, link):
    for f, ref in ((0, source_ref), (1, grad_ref)):
        for k in range(4):
            part[k] = ref[:, 128 * k : 128 * k + 128].astype(jnp.float32)

        def turn(i, carry):
            for half, count in ((0, 128), (1, 64)):
                a = part[half, pl.ds(i, 48, stride=16), :]
                b = part[2 + half, pl.ds(i, 48, stride=16), :]
                block = jnp.concatenate([a, b, a[:32]], axis=0).T
                rows[f, pl.ds(half * 2048 + i, count, stride=16), :] = block[:count]
            return carry

        lax.fori_loop(0, ROWS, turn, 0)

    def send(step, carry):
        d = lax.rem(link.lat + step, LAT)
        units = [
            rows[f, pl.ds(pl.multiple_of((d * 6 + m) * 16, 16), 16), :]
            for f in range(2)
            for m in range(MODES)
        ]
        for g in range(3):
            a, b, c, e = units[4 * g : 4 * g + 4]
            tiles = merge_lanes(a, pltpu.roll(b, 96, 1), pltpu.roll(c, 64, 1), pltpu.roll(e, 32, 1))
            for k in range(3):
                out_ref[d, 3 * g + k] = tiles[k].astype(jnp.bfloat16)
        link.start(step)
        return carry

    lax.fori_loop(0, LAT, send, 0)


def gather_kernel(in_ref, source_ref, grad_ref, part, rows):
    def receive(d, carry):
        tiles = [in_ref[d, k].astype(jnp.float32) for k in range(9)]
        units = split_lanes(tiles)
        for u in range(12):
            if u % 4:
                units[u] = pltpu.roll(units[u], 32 * (u % 4), 1)
            rows[u // 6, pl.ds(pl.multiple_of((d * 6 + u % 6) * 16, 16), 16), :] = units[u]
        return carry

    lax.fori_loop(0, LAT, receive, 0)
    for f, ref in ((0, source_ref), (1, grad_ref)):

        def turn(i, carry):
            block = rows[f, pl.ds(i, MMAX, stride=16), :]
            halves = (block[:128], jnp.concatenate([block[128:], jnp.zeros((64, 128), jnp.float32)], axis=0))
            for half in range(2):
                flat = halves[half].T
                part[half, pl.ds(i, 48, stride=16), :] = flat[:48]
                part[2 + half, pl.ds(i, 48, stride=16), :] = flat[48:96]
            return carry

        lax.fori_loop(0, ROWS, turn, 0)
        for k in range(4):
            ref[:, 128 * k : 128 * k + 128] = part[k].astype(jnp.bfloat16)


def recurrence(order_ref, cosine_ref, sector_ref, table):
    order = jnp.broadcast_to(order_ref[...], (8, NLAT))
    cosine = jnp.broadcast_to(cosine_ref[...], (8, NLAT))
    sector = sector_ref[...]
    order_sq = order * order
    table[...] = jnp.zeros_like(table)

    def advance(degree_index, carry):
        previous, earlier = carry
        degree = jnp.full((8, NLAT), degree_index, jnp.int32).astype(jnp.float32)
        lower = degree - 1.0
        scale_a = jnp.sqrt(
            jnp.maximum(4.0 * degree * degree - 1.0, 0.0)
            / jnp.maximum(degree * degree - order_sq, 1.0)
        )
        scale_b = jnp.sqrt(
            jnp.maximum(lower * lower - order_sq, 0.0)
            / jnp.maximum(4.0 * lower * lower - 1.0, 1.0)
        )
        value = scale_a * (cosine * previous - scale_b * earlier)
        value = jnp.where(degree < order, 0.0, jnp.where(degree == order, sector, value))
        place = LMAX - 1 - degree_index
        row = place // 6 * 8 + place % 6
        for k in range(4):
            table[k, pl.ds(row, 8, stride=256), :] = value[:, 128 * k : 128 * k + 128]
        return value, previous

    zero = sector * 0.0
    lax.fori_loop(0, LMAX, advance, (zero, zero))


def finish_tables(quad_ref, band_ref, near_ref, far_ref, table):
    info = band_ref[...].reshape(NLAT, 128).astype(jnp.float32)
    relative = (iota((NLAT, NLAT), 1) - iota((NLAT, NLAT), 0)).astype(jnp.float32) - info[:, 0:1]
    band = jnp.zeros((NLAT, NLAT), jnp.float32)
    for k in range(4):
        keep = (relative == float(k)) & (info[:, 1:2] > float(k))
        band = band + jnp.where(keep, info[:, 2 + k : 3 + k], 0.0)
    band = band.astype(jnp.bfloat16)
    for m in range(MODES):
        own = jnp.concatenate([table[k, 256 * m : 256 * m + 256, :] for k in range(4)], axis=1)
        analysis = (own * quad_ref[...]).astype(jnp.bfloat16)
        banded = dense(analysis, band)
        synthesis = own * (1.0 / math.sqrt(LMAX))
        near_ref[m] = banded.astype(jnp.bfloat16)
        near_ref[MODES + m] = synthesis.astype(jnp.bfloat16)
        far_ref[m] = synthesis.T.astype(jnp.bfloat16)
        far_ref[MODES + m] = banded.T.astype(jnp.bfloat16)


def analysis_kernel(in_ref, table_ref, out_ref):
    tiles = [in_ref[:, k].reshape(NLAT, 128).astype(jnp.float32) for k in range(9)]
    units = split_lanes(tiles)
    units = [dense(table_ref[u], units[u].astype(jnp.bfloat16)) for u in range(12)]
    packed = []
    for g in range(3):
        packed += merge_lanes(*units[4 * g : 4 * g + 4])
    store_rows(out_ref, merge_rows(packed))


def synthesis_kernel(in_ref, table_ref, out_ref):
    live = iota((LAT, 16, 128), 0) + lax.axis_index("lat") < LAT
    units = split_lanes(split_rows(load_rows(in_ref, live)))
    units = [dense(table_ref[u], units[u].astype(jnp.bfloat16)) for u in range(12)]
    for g in range(3):
        tiles = merge_lanes(*units[4 * g : 4 * g + 4])
        for k in range(3):
            out_ref[:, 3 * g + k] = tiles[k].reshape(LAT, ROWS, 128).astype(jnp.bfloat16)


def mixing_kernel(in_ref, weight_ref, pick_ref, pick_t_ref, out_ref, grad_ref, before, after):
    lat, chan = lax.axis_index("lat"), lax.axis_index("chan")
    slot = iota((LAT, 16, 128), 0)
    other = (2 * (slot % 4) + lax.rem(chan, 2)) * 4 + lax.div(chan, 2)
    units = split_lanes(split_rows(load_rows(in_ref, other + lat < LAT)))
    for u in range(12):
        if u % 4:
            units[u] = pltpu.roll(units[u], 32 * (u % 4), 1)
        f, m = u // 6, u % 6
        before[f, :, 32 * m : 32 * m + 32, :] = units[u].reshape(CHAN, 32, 128)
    after[...] = jnp.zeros_like(after)
    lane = iota((24, 128), 1)

    def degree(l, carry):
        left = []
        for f in range(2):
            columns = []
            for p in range(4):
                a = before[f, 2 * p, pl.ds(l, 24, stride=8), :]
                b = before[f, 2 * p + 1, pl.ds(l, 24, stride=8), :]
                first = jnp.where(lane < 64, a, pltpu.roll(b, 64, 1))
                second = jnp.where(lane < 64, pltpu.roll(a, 80, 1), pltpu.roll(b, 16, 1))
                columns.append(jnp.concatenate([first, second], axis=0))
            left.append(jnp.concatenate(columns, axis=1).astype(jnp.bfloat16))
        rows = []
        for e in range(CHAN):
            rows += [weight_ref[e, l], jnp.zeros((16, 384), jnp.bfloat16)]
        weight = dense(jnp.concatenate(rows, axis=0), pick_ref[...]).astype(jnp.bfloat16)
        mixed = dense(left[0], weight)
        back = dense(left[1], weight, ((1,), (1,)))
        dense_back = dense(left[1], pick_t_ref[...]).astype(jnp.bfloat16)
        grad = dense(left[0], dense_back, ((0,), (0,)))
        for e in range(CHAN):
            grad_ref[e, l] = grad[64 * e : 64 * e + 48].astype(jnp.bfloat16)
            for f, value in ((0, mixed), (1, back)):
                tile = value[:, 128 * (e // 2) : 128 * (e // 2) + 128]
                first, second = tile[:24], tile[24:]
                if e % 2:
                    first = pltpu.roll(first, 64, 1)
                second = pltpu.roll(second, 112 if e % 2 else 48, 1)
                after[f, e, pl.ds(l, 24, stride=8), :] = jnp.where(lane < 48, first, second)
        return carry

    lax.fori_loop(0, 6, degree, 0)
    units = [after[u // 6, :, 32 * (u % 6) : 32 * (u % 6) + 32, :].reshape(256, 128) for u in range(12)]
    packed = []
    for g in range(3):
        a, b, c, d = units[4 * g : 4 * g + 4]
        packed += merge_lanes(a, pltpu.roll(b, 96, 1), pltpu.roll(c, 64, 1), pltpu.roll(d, 32, 1))
    store_rows(out_ref, merge_rows(packed))


def local(kernel, shapes, scratch, *arrays):
    single = not isinstance(shapes, list)
    spec = pl.BlockSpec(memory_space=pltpu.VMEM)
    return pl.pallas_call(
        kernel,
        out_shape=shapes,
        in_specs=[spec] * len(arrays),
        out_specs=spec if single else [spec] * len(shapes),
        scratch_shapes=scratch,
        compiler_params=pltpu.CompilerParams(vmem_limit_bytes=VMEM_LIMIT),
    )(*arrays)


def bf16(*shape):
    return jax.ShapeDtypeStruct(shape, jnp.bfloat16)


def legendre_inputs():
    theta = math.pi * (np.arange(NLAT, dtype=np.float64) + 0.5) / NLAT
    cosine = np.cos(theta).astype(np.float32)[None, :]
    sine = np.sin(theta)
    orders = lax.axis_index("lat") * MODES + jnp.arange(8, dtype=jnp.int32)
    norm = jnp.asarray(np.concatenate([log_norms(), np.zeros(2, np.float32)]))
    order = orders.astype(jnp.float32)[:, None]
    own = lax.dynamic_slice(norm, (lax.axis_index("lat") * MODES,), (8,))
    sector = jnp.exp(own[:, None] + order * jnp.asarray(np.log(sine).astype(np.float32))[None, :])
    quadrature = (math.sqrt(NLAT) * math.pi / NLAT * sine).astype(np.float32)[None, :]
    return order, jnp.asarray(cosine), sector, jnp.asarray(quadrature)


def lat_to(step, lat, chan):
    other = lax.rem(lat + step, LAT)
    return other, chan, other, lat


def spectral_to(step, lat, chan):
    other = lax.rem(lat + step, LAT)
    group = 2 * lax.rem(lat, 4) + lax.rem(lax.div(lat, 4), 2)
    return other, group, other, chan * 4 + lax.div(lat, 8)


def spectral_from(step, lat, chan):
    part = lax.rem(step + lat, 4)
    group = lax.rem(lax.div(step, 4) + chan, CHAN)
    other = (2 * part + lax.rem(chan, 2)) * 4 + lax.div(chan, 2)
    return other, group, group * 4 + part, lat


def degree_owner(step, lat, chan):
    other = lax.rem(lat + LAT - step, LAT)
    group = 2 * lax.rem(lat, 4) + lax.rem(lax.div(lat, 4), 2)
    return other, group, other, 0


class Wire:
    def __init__(self, sends, receives, skip, source, target, sems):
        self.lat, self.chan = lax.axis_index("lat"), lax.axis_index("chan")
        self.sends, self.receives, self.skip = sends, receives, skip
        self.source, self.target = source, target
        self.send_sem, self.recv_sem, self.own_sem = sems

    def live(self, pair):
        if self.skip:
            return self.lat + pair[0] < LAT
        return pair[0] >= 0

    def own(self, pair):
        return (pair[0] == self.lat) & (pair[1] == self.chan) & self.live(pair)

    def far(self, pair):
        return jnp.logical_not((pair[0] == self.lat) & (pair[1] == self.chan)) & self.live(pair)

    def greet(self, barrier, total):
        def step_fn(step, count):
            source = self.receives(step, self.lat, self.chan)

            @pl.when(self.far(source))
            def _():
                pl.semaphore_signal(
                    barrier, inc=1, device_id={"lat": source[0], "chan": source[1]},
                    device_id_type=MESH,
                )

            return count + jnp.where(self.far(self.sends(step, self.lat, self.chan)), 1, 0)

        return lax.fori_loop(0, LAT, step_fn, total)

    def remote(self, pair, slot):
        return pltpu.make_async_remote_copy(
            src_ref=self.source.at[pair[2]],
            dst_ref=self.target.at[slot],
            send_sem=self.send_sem.at[pair[2]],
            recv_sem=self.recv_sem.at[slot],
            device_id={"lat": pair[0], "chan": pair[1]},
            device_id_type=MESH,
        )

    def local(self, pair):
        return pltpu.make_async_copy(
            self.source.at[pair[2]], self.target.at[pair[3]], self.own_sem
        )

    def start(self, step):
        pair = self.sends(step, self.lat, self.chan)

        @pl.when(self.own(pair))
        def _():
            self.local(pair).start()

        @pl.when(self.far(pair))
        def _():
            self.remote(pair, pair[3]).start()

    def start_all(self):
        def step_fn(step, carry):
            self.start(step)
            return carry

        lax.fori_loop(0, LAT, step_fn, 0)

    def arrive(self):
        def step_fn(step, carry):
            target = self.sends(step, self.lat, self.chan)
            source = self.receives(step, self.lat, self.chan)

            @pl.when(self.own(target))
            def _():
                self.local(target).wait()

            @pl.when(self.far(source))
            def _():
                self.remote(source, source[2]).wait_recv()

            return carry

        lax.fori_loop(0, LAT, step_fn, 0)

    def leave(self):
        def step_fn(step, carry):
            target = self.sends(step, self.lat, self.chan)

            @pl.when(self.far(target))
            def _():
                self.remote(target, target[3]).wait_send()

            return carry

        lax.fori_loop(0, LAT, step_fn, 0)


class Side:
    def __init__(self, parts, source, target, sems):
        self.lat, self.chan = lax.axis_index("lat"), lax.axis_index("chan")
        self.parts, self.source, self.target = parts, source, target
        self.send_sem, self.recv_sem, self.own_sem = sems

    def greet(self, barrier, total):
        def step_fn(step, count):
            pl.semaphore_signal(
                barrier, inc=1,
                device_id={"lat": self.lat, "chan": lax.rem(self.chan + step, CHAN)},
                device_id_type=MESH,
            )
            return count + 1

        return lax.fori_loop(1, CHAN, step_fn, total)

    def remote(self, step, incoming):
        other = lax.rem(self.chan + step, CHAN)
        slot = other if incoming else self.chan
        return pltpu.make_async_remote_copy(
            src_ref=self.source.at[other] if self.parts else self.source,
            dst_ref=self.target.at[slot],
            send_sem=self.send_sem.at[other],
            recv_sem=self.recv_sem.at[slot],
            device_id={"lat": self.lat, "chan": other},
            device_id_type=MESH,
        )

    def local(self):
        source = self.source.at[self.chan] if self.parts else self.source
        return pltpu.make_async_copy(source, self.target.at[self.chan], self.own_sem)

    def start(self):
        self.local().start()

        def step_fn(step, carry):
            self.remote(step, False).start()
            return carry

        lax.fori_loop(1, CHAN, step_fn, 0)

    def finish(self):
        self.local().wait()

        def step_fn(step, carry):
            self.remote(step, False).wait_send()
            self.remote(step, True).wait_recv()
            return carry

        lax.fori_loop(1, CHAN, step_fn, 0)


def lat_from(step, lat, chan):
    return lat_to(LAT - step, lat, chan)


def whole_to(step, lat, chan):
    other = lax.rem(lat + step, LAT)
    return other, chan, 0, lat


def whole_from(step, lat, chan):
    other = lax.rem(lat + LAT - step, LAT)
    return other, chan, other, lat


class Whole(Wire):
    def remote(self, pair, slot):
        return pltpu.make_async_remote_copy(
            src_ref=self.source,
            dst_ref=self.target.at[slot],
            send_sem=self.send_sem.at[pair[0]],
            recv_sem=self.recv_sem.at[slot],
            device_id={"lat": pair[0], "chan": pair[1]},
            device_id_type=MESH,
        )

    def local(self, pair):
        return pltpu.make_async_copy(self.source, self.target.at[pair[3]], self.own_sem)


def meet(links):
    barrier = pltpu.get_barrier_semaphore()
    total = jnp.int32(0)
    for link in links:
        total = link.greet(barrier, total)
    pl.semaphore_wait(barrier, total)


def front_kernel(
    source_ref, grad_ref, info_ref, weight_ref, order_ref, cosine_ref, sector_ref, quad_ref,
    out_ref, weights_ref, bands_ref, far_ref,
    part, rows, table, near, message, landing, bands, spectral, *sems
):
    panels = Wire(lat_to, lat_from, False, message, landing, sems[0:3])
    degrees = Wire(spectral_to, spectral_from, True, spectral, out_ref, sems[3:6])
    info = Whole(whole_to, whole_from, False, info_ref, bands, sems[6:9])
    side = Side(False, weight_ref, weights_ref, sems[9:12])
    meet([panels, degrees, info, side])
    side.start()
    info.start_all()
    spread_kernel(source_ref, grad_ref, message, part, rows, panels)
    recurrence(order_ref, cosine_ref, sector_ref, table)
    info.arrive()
    finish_tables(quad_ref, bands, near, far_ref, table)
    bands_ref[...] = bands[...]
    panels.arrive()
    analysis_kernel(landing, near, spectral)
    degrees.start_all()
    info.leave()
    panels.leave()
    degrees.arrive()
    degrees.leave()
    side.finish()


def back_kernel(
    reply_ref, grad_ref, table_ref, parts_ref, forward_ref, backward_ref,
    answers, message, landing, part, rows, *sems
):
    degrees = Wire(spectral_from, degree_owner, True, reply_ref, answers, sems[0:3])
    panels = Wire(lat_to, lat_from, False, message, landing, sems[3:6])
    side = Side(True, grad_ref, parts_ref, sems[6:9])
    meet([degrees, panels, side])
    degrees.start_all()
    side.start()
    degrees.arrive()
    synthesis_kernel(answers, table_ref, message)
    panels.start_all()
    degrees.leave()
    panels.arrive()
    gather_kernel(landing, forward_ref, backward_ref, part, rows)
    panels.leave()
    side.finish()


def link_sems(counts):
    out = []
    for count in counts:
        out += [pltpu.SemaphoreType.DMA((count,))] * 2 + [pltpu.SemaphoreType.DMA]
    return out


def linked(kernel, collective_id, shapes, out_spaces, scratch, spaces, arrays):
    def spec(space):
        return pl.BlockSpec(memory_space=space)

    return pl.pallas_call(
        kernel,
        out_shape=shapes,
        in_specs=[spec(space) for space in spaces],
        out_specs=[spec(space) for space in out_spaces],
        scratch_shapes=scratch,
        compiler_params=pltpu.CompilerParams(
            collective_id=collective_id, has_side_effects=True, vmem_limit_bytes=VMEM_LIMIT
        ),
    )(*arrays)


def with_halo(block):
    forward = [(i, i + 1) for i in range(LAT - 1)]
    backward = [(i + 1, i) for i in range(LAT - 1)]
    low = lax.ppermute(block[:, -HALO:], "lat", forward)
    high = lax.ppermute(block[:, :HALO], "lat", backward)
    return jnp.concatenate([low, block, high], axis=1)


def dot(spec, a, b):
    return jnp.einsum(spec, a, b, preferred_element_type=jnp.float32)


def local_band(start, width, coef, low):
    count = start.shape[0]
    target = jnp.arange(count, dtype=jnp.int32)[:, None]
    source = jnp.arange(ROWS + 4 if low else ROWS, dtype=jnp.int32)[None, :]
    relative = source - target - (HALO if low else -HALO) - start[:, None]
    matrix = jnp.zeros(relative.shape, jnp.float32)
    for offset in range(4):
        keep = (relative == offset) & (width[:, None] > offset)
        matrix = matrix + jnp.where(keep, coef[:, offset : offset + 1], 0.0)
    return matrix.astype(jnp.bfloat16)


def per_device(source_field, band_start, band_width, band_coef, mixing_weight, output_grad):
    lat = lax.axis_index("lat")
    channels = source_field.shape[0]
    table = fourier_table()
    lon_analysis = jnp.asarray((table / math.sqrt(NLON)).astype(jnp.bfloat16))
    lon_synthesis = jnp.asarray((table / math.sqrt(MMAX)).astype(jnp.bfloat16))
    flat = channels * ROWS

    info = jnp.concatenate(
        [
            band_start.astype(jnp.bfloat16)[:, None],
            band_width.astype(jnp.bfloat16)[:, None],
            band_coef,
            jnp.zeros((ROWS, 122), jnp.bfloat16),
        ],
        axis=1,
    )
    vmem, anywhere = pltpu.VMEM, pl.ANY
    work = [vmem((4, flat, 128), jnp.float32), vmem((2, MMAX * ROWS, 128), jnp.float32)]
    received, weight, band_rows, far = linked(
        front_kernel,
        1,
        [
            bf16(LAT, 64, 128),
            bf16(CHAN, 6, channels, CHAN * channels),
            bf16(LAT, ROWS, 128),
            bf16(12, NLAT, 256),
        ],
        [anywhere, anywhere, vmem, vmem],
        work
        + [
            vmem((4, 2048, 128), jnp.float32),
            vmem((12, 256, NLAT), jnp.bfloat16),
            vmem((LAT, 9, ROWS, 128), jnp.bfloat16),
            vmem((LAT, 9, ROWS, 128), jnp.bfloat16),
            vmem((LAT, ROWS, 128), jnp.bfloat16),
            vmem((LAT, 64, 128), jnp.bfloat16),
        ]
        + link_sems([LAT, LAT, LAT, CHAN]),
        [vmem, vmem, vmem, anywhere] + [vmem] * 4,
        [
            dot("ik,kn->in", source_field.reshape(flat, NLON), lon_analysis).astype(jnp.bfloat16),
            dot("ik,kn->in", output_grad.reshape(flat, NLON), lon_synthesis).astype(jnp.bfloat16),
            info,
            mixing_weight,
            *legendre_inputs(),
        ],
    )

    pick = np.zeros((CHAN, channels, CHAN, 64), np.float32)
    for e in range(CHAN):
        pick[e, :, e, :channels] = np.eye(channels)
    pick = pick.reshape(CHAN * channels, 512)
    panel = pltpu.VMEM((2, CHAN, 192, 128), jnp.float32)
    reply, grad = local(
        mixing_kernel,
        [bf16(LAT, 64, 128), bf16(CHAN, 6, channels, CHAN * channels)],
        [panel, panel],
        received,
        weight,
        jnp.asarray(pick.astype(jnp.bfloat16)),
        jnp.asarray(pick.T.astype(jnp.bfloat16)),
    )
    grad_parts, forward, backward = linked(
        back_kernel,
        2,
        [bf16(CHAN, 6, channels, CHAN * channels), bf16(flat, 512), bf16(flat, 512)],
        [anywhere, vmem, vmem],
        [
            vmem((LAT, 64, 128), jnp.bfloat16),
            vmem((LAT, 9, ROWS, 128), jnp.bfloat16),
            vmem((LAT, 9, ROWS, 128), jnp.bfloat16),
        ]
        + work
        + link_sems([LAT, LAT, CHAN]),
        [anywhere, anywhere, vmem],
        [reply, grad, far],
    )
    grad_mixing = jnp.sum(grad_parts.astype(jnp.float32), axis=0)

    rows = jnp.pad(band_rows.reshape(NLAT, 128), ((HALO, HALO), (0, 0)))
    rows = lax.dynamic_slice(rows, (lat * ROWS, 0), (ROWS + 4, 128)).astype(jnp.float32)
    start, width, coef = rows[:, 0].astype(jnp.int32), rows[:, 1].astype(jnp.int32), rows[:, 2:6]
    own = slice(HALO, HALO + ROWS)
    band_ahead = local_band(start[own], width[own], coef[own], True)
    band_back = local_band(start, width, coef, False)
    mixed_field = dot("ik,nk->in", forward, lon_synthesis).reshape(channels, ROWS, NLON) + dot(
        "ij,cjn->cin", band_ahead, with_halo(source_field)
    )
    grad_input = dot("ik,nk->in", backward, lon_analysis).reshape(channels, ROWS, NLON) + dot(
        "ji,cjn->cin", band_back, with_halo(output_grad)
    )
    return (mixed_field.astype(jnp.bfloat16), grad_input.astype(jnp.bfloat16), grad_mixing)


def solution(mesh):
    in_specs = (
        P("chan", "lat", None),
        P("lat"),
        P("lat"),
        P("lat", None),
        P("lat", "chan", None),
        P("chan", "lat", None),
    )
    out_specs = (P("chan", "lat", None), P("chan", "lat", None), P("lat", "chan", None))
    return jax.shard_map(
        per_device, mesh=mesh, in_specs=in_specs, out_specs=out_specs, check_vma=False
    )
```

```python
import functools
import math

import jax
import jax.numpy as jnp
import numpy as np
from jax import lax
from jax.experimental import pallas as pl
from jax.experimental.pallas import tpu as pltpu
from jax.sharding import PartitionSpec as P

NLAT = 512
NLON = 1440
MMAX = 192
LMAX = 192
HALO = 2
LAT = 32
CHAN = 8
MODES = MMAX // LAT
ROWS = NLAT // LAT
MESH = pl.DeviceIdType.MESH
VMEM_LIMIT = 48 * 1024 * 1024


def log_norms():
    return np.array(
        [
            0.5
            * (
                math.log((2.0 * m + 1.0) / (4.0 * math.pi))
                + math.lgamma(m + 0.5)
                - math.lgamma(m + 1.0)
                - 0.5 * math.log(math.pi)
            )
            for m in range(MMAX)
        ],
        np.float32,
    )


def fourier_table():
    phase = 2.0 * math.pi / NLON * (np.outer(np.arange(NLON), np.arange(MMAX)) % NLON)
    table = np.zeros((NLON, 2, 256))
    table[:, 0, :MMAX] = np.cos(phase)
    table[:, 1, :MMAX] = -np.sin(phase)
    return table.reshape(NLON, 512)


def dense(a, b, dims=((1,), (0,))):
    return lax.dot_general(a, b, (dims, ((), ())), preferred_element_type=jnp.float32)


def iota(shape, axis):
    return lax.broadcasted_iota(jnp.int32, shape, axis)


def merge_lanes(a, b, c, d):
    lane = iota(a.shape, 1)
    return (
        jnp.where(lane < 96, a, b),
        jnp.where(lane < 64, b, c),
        jnp.where(lane < 32, c, d),
    )


def split_lanes(tiles):
    lane = iota(tiles[0].shape, 1)
    units = []
    for g in range(0, 9, 3):
        t0, t1, t2 = tiles[g : g + 3]
        units += [t0, jnp.where(lane < 64, t1, t0), jnp.where(lane < 32, t2, t1), t2]
    return units


def merge_rows(tiles):
    row = iota(tiles[0].shape, 0) % 8
    out = list(tiles[:8])
    for k in range(3):
        out[k] = jnp.where(row < 6, tiles[k], pltpu.roll(tiles[8], 6 - 2 * k, 0))
    return out


def split_rows(tiles):
    rows = tiles[0].shape[0]
    row = iota(tiles[0].shape, 0) % 8
    back = [pltpu.roll(tiles[k], rows - (6 - 2 * k), 0) for k in range(3)]
    return list(tiles) + [jnp.where(row < 2, back[0], jnp.where(row < 4, back[1], back[2]))]


def store_rows(out_ref, tiles):
    for p in range(4):
        pair = [tiles[2 * p + k].reshape(LAT, 8, 128) for k in range(2)]
        out_ref[:, 16 * p : 16 * p + 16, :] = jnp.concatenate(pair, axis=1).astype(jnp.bfloat16)


def load_rows(in_ref, live):
    tiles = []
    for p in range(4):
        pair = in_ref[:, 16 * p : 16 * p + 16, :].astype(jnp.float32)
        pair = jnp.where(live, pair, 0.0)
        tiles += [pair[:, :8].reshape(256, 128), pair[:, 8:].reshape(256, 128)]
    return tiles


def spread_kernel(source_ref, grad_ref, out_ref, part, rows, link):
    for f, ref in ((0, source_ref), (1, grad_ref)):
        for k in range(4):
            part[k] = ref[:, 128 * k : 128 * k + 128].astype(jnp.float32)

        def turn(i, carry):
            for half, count in ((0, 128), (1, 64)):
                a = part[half, pl.ds(i, 48, stride=16), :]
                b = part[2 + half, pl.ds(i, 48, stride=16), :]
                block = jnp.concatenate([a, b, a[:32]], axis=0).T
                rows[f, pl.ds(half * 2048 + i, count, stride=16), :] = block[:count]
            return carry

        lax.fori_loop(0, ROWS, turn, 0)

    def send(step, carry):
        d = wrap(link.lat + step, LAT)
        units = [
            rows[f, pl.ds(pl.multiple_of((d * 6 + m) * 16, 16), 16), :]
            for f in range(2)
            for m in range(MODES)
        ]
        for g in range(3):
            a, b, c, e = units[4 * g : 4 * g + 4]
            tiles = merge_lanes(a, pltpu.roll(b, 96, 1), pltpu.roll(c, 64, 1), pltpu.roll(e, 32, 1))
            for k in range(3):
                out_ref[d, 3 * g + k] = tiles[k].astype(jnp.bfloat16)
        link.start(step)
        return carry

    lax.fori_loop(0, LAT, send, 0)


def gather_kernel(in_ref, source_ref, grad_ref, part, rows):
    def receive(d, carry):
        tiles = [in_ref[d, k].astype(jnp.float32) for k in range(9)]
        units = split_lanes(tiles)
        for u in range(12):
            if u % 4:
                units[u] = pltpu.roll(units[u], 32 * (u % 4), 1)
            rows[u // 6, pl.ds(pl.multiple_of((d * 6 + u % 6) * 16, 16), 16), :] = units[u]
        return carry

    lax.fori_loop(0, LAT, receive, 0)
    for f, ref in ((0, source_ref), (1, grad_ref)):

        def turn(i, carry):
            block = rows[f, pl.ds(i, MMAX, stride=16), :]
            halves = (block[:128], jnp.concatenate([block[128:], jnp.zeros((64, 128), jnp.float32)], axis=0))
            for half in range(2):
                flat = halves[half].T
                part[half, pl.ds(i, 48, stride=16), :] = flat[:48]
                part[2 + half, pl.ds(i, 48, stride=16), :] = flat[48:96]
            return carry

        lax.fori_loop(0, ROWS, turn, 0)
        for k in range(4):
            ref[:, 128 * k : 128 * k + 128] = part[k].astype(jnp.bfloat16)


def recurrence(order_ref, cosine_ref, sector_ref, table):
    order = jnp.broadcast_to(order_ref[...], (8, NLAT))
    cosine = jnp.broadcast_to(cosine_ref[...], (8, NLAT))
    sector = sector_ref[...]
    order_sq = order * order
    table[...] = jnp.zeros_like(table)

    def advance(degree_index, carry):
        previous, earlier = carry
        degree = jnp.full((8, NLAT), degree_index, jnp.int32).astype(jnp.float32)
        lower = degree - 1.0
        scale_a = jnp.sqrt(
            jnp.maximum(4.0 * degree * degree - 1.0, 0.0)
            / jnp.maximum(degree * degree - order_sq, 1.0)
        )
        scale_b = jnp.sqrt(
            jnp.maximum(lower * lower - order_sq, 0.0)
            / jnp.maximum(4.0 * lower * lower - 1.0, 1.0)
        )
        value = scale_a * (cosine * previous - scale_b * earlier)
        value = jnp.where(degree < order, 0.0, jnp.where(degree == order, sector, value))
        place = LMAX - 1 - degree_index
        row = place // 6 * 8 + place % 6
        for k in range(4):
            table[k, pl.ds(row, 8, stride=256), :] = value[:, 128 * k : 128 * k + 128]
        return value, previous

    zero = sector * 0.0
    lax.fori_loop(0, LMAX, advance, (zero, zero))


def finish_tables(quad_ref, band_ref, near_ref, far_ref, table):
    info = band_ref[...].reshape(NLAT, 128).astype(jnp.float32)
    relative = (iota((NLAT, NLAT), 1) - iota((NLAT, NLAT), 0)).astype(jnp.float32) - info[:, 0:1]
    band = jnp.zeros((NLAT, NLAT), jnp.float32)
    for k in range(4):
        keep = (relative == float(k)) & (info[:, 1:2] > float(k))
        band = band + jnp.where(keep, info[:, 2 + k : 3 + k], 0.0)
    band = band.astype(jnp.bfloat16)
    for m in range(MODES):
        own = jnp.concatenate([table[k, 256 * m : 256 * m + 256, :] for k in range(4)], axis=1)
        analysis = (own * quad_ref[...]).astype(jnp.bfloat16)
        banded = dense(analysis, band)
        synthesis = own * (1.0 / math.sqrt(LMAX))
        near_ref[m] = banded.astype(jnp.bfloat16)
        near_ref[MODES + m] = synthesis.astype(jnp.bfloat16)
        far_ref[m] = synthesis.T.astype(jnp.bfloat16)
        far_ref[MODES + m] = banded.T.astype(jnp.bfloat16)


def analysis_kernel(in_ref, table_ref, out_ref):
    tiles = [in_ref[:, k].reshape(NLAT, 128).astype(jnp.float32) for k in range(9)]
    units = split_lanes(tiles)
    units = [dense(table_ref[u], units[u].astype(jnp.bfloat16)) for u in range(12)]
    packed = []
    for g in range(3):
        packed += merge_lanes(*units[4 * g : 4 * g + 4])
    store_rows(out_ref, merge_rows(packed))


def synthesis_kernel(in_ref, table_ref, out_ref):
    live = iota((LAT, 16, 128), 0) + lax.axis_index("lat") < LAT
    units = split_lanes(split_rows(load_rows(in_ref, live)))
    units = [dense(table_ref[u], units[u].astype(jnp.bfloat16)) for u in range(12)]
    for g in range(3):
        tiles = merge_lanes(*units[4 * g : 4 * g + 4])
        for k in range(3):
            out_ref[:, 3 * g + k] = tiles[k].reshape(LAT, ROWS, 128).astype(jnp.bfloat16)


def mixing_kernel(in_ref, weight_ref, pick_ref, pick_t_ref, out_ref, grad_ref, before, after):
    lat, chan = lax.axis_index("lat"), lax.axis_index("chan")
    slot = iota((LAT, 16, 128), 0)
    other = (2 * (slot % 4) + lax.rem(chan, 2)) * 4 + lax.div(chan, 2)
    units = split_lanes(split_rows(load_rows(in_ref, other + lat < LAT)))
    for u in range(12):
        if u % 4:
            units[u] = pltpu.roll(units[u], 32 * (u % 4), 1)
        f, m = u // 6, u % 6
        before[f, :, 32 * m : 32 * m + 32, :] = units[u].reshape(CHAN, 32, 128)
    after[...] = jnp.zeros_like(after)
    lane = iota((24, 128), 1)

    def degree(l, carry):
        left = []
        for f in range(2):
            columns = []
            for p in range(4):
                a = before[f, 2 * p, pl.ds(l, 24, stride=8), :]
                b = before[f, 2 * p + 1, pl.ds(l, 24, stride=8), :]
                first = jnp.where(lane < 64, a, pltpu.roll(b, 64, 1))
                second = jnp.where(lane < 64, pltpu.roll(a, 80, 1), pltpu.roll(b, 16, 1))
                columns.append(jnp.concatenate([first, second], axis=0))
            left.append(jnp.concatenate(columns, axis=1).astype(jnp.bfloat16))
        rows = []
        for e in range(CHAN):
            rows += [weight_ref[e, l], jnp.zeros((16, 384), jnp.bfloat16)]
        weight = dense(jnp.concatenate(rows, axis=0), pick_ref[...]).astype(jnp.bfloat16)
        mixed = dense(left[0], weight)
        back = dense(left[1], weight, ((1,), (1,)))
        dense_back = dense(left[1], pick_t_ref[...]).astype(jnp.bfloat16)
        grad = dense(left[0], dense_back, ((0,), (0,)))
        for e in range(CHAN):
            grad_ref[e, l] = grad[64 * e : 64 * e + 48].astype(jnp.bfloat16)
            for f, value in ((0, mixed), (1, back)):
                tile = value[:, 128 * (e // 2) : 128 * (e // 2) + 128]
                first, second = tile[:24], tile[24:]
                if e % 2:
                    first = pltpu.roll(first, 64, 1)
                second = pltpu.roll(second, 112 if e % 2 else 48, 1)
                after[f, e, pl.ds(l, 24, stride=8), :] = jnp.where(lane < 48, first, second)
        return carry

    lax.fori_loop(0, 6, degree, 0)
    units = [after[u // 6, :, 32 * (u % 6) : 32 * (u % 6) + 32, :].reshape(256, 128) for u in range(12)]
    packed = []
    for g in range(3):
        a, b, c, d = units[4 * g : 4 * g + 4]
        packed += merge_lanes(a, pltpu.roll(b, 96, 1), pltpu.roll(c, 64, 1), pltpu.roll(d, 32, 1))
    store_rows(out_ref, merge_rows(packed))


def local(kernel, shapes, scratch, *arrays):
    single = not isinstance(shapes, list)
    spec = pl.BlockSpec(memory_space=pltpu.VMEM)
    return pl.pallas_call(
        kernel,
        out_shape=shapes,
        in_specs=[spec] * len(arrays),
        out_specs=spec if single else [spec] * len(shapes),
        scratch_shapes=scratch,
        compiler_params=pltpu.CompilerParams(vmem_limit_bytes=VMEM_LIMIT),
    )(*arrays)


def bf16(*shape):
    return jax.ShapeDtypeStruct(shape, jnp.bfloat16)


def legendre_inputs():
    theta = math.pi * (np.arange(NLAT, dtype=np.float64) + 0.5) / NLAT
    cosine = np.cos(theta).astype(np.float32)[None, :]
    sine = np.sin(theta)
    orders = lax.axis_index("lat") * MODES + jnp.arange(8, dtype=jnp.int32)
    norm = jnp.asarray(np.concatenate([log_norms(), np.zeros(2, np.float32)]))
    order = orders.astype(jnp.float32)[:, None]
    own = lax.dynamic_slice(norm, (lax.axis_index("lat") * MODES,), (8,))
    sector = jnp.exp(own[:, None] + order * jnp.asarray(np.log(sine).astype(np.float32))[None, :])
    quadrature = (math.sqrt(NLAT) * math.pi / NLAT * sine).astype(np.float32)[None, :]
    return order, jnp.asarray(cosine), sector, jnp.asarray(quadrature)


def wrap(value, size):
    return value - jnp.where(value >= size, size, 0)


def lat_to(step, lat, chan):
    other = wrap(lat + step, LAT)
    return other, chan, other, lat


def spectral_to(step, lat, chan):
    other = wrap(lat + step, LAT)
    group = 2 * lax.rem(lat, 4) + lax.rem(lax.div(lat, 4), 2)
    return other, group, other, chan * 4 + lax.div(lat, 8)


def spectral_from(step, lat, chan):
    part = lax.rem(step + lat, 4)
    group = lax.rem(lax.div(step, 4) + chan, CHAN)
    other = (2 * part + lax.rem(chan, 2)) * 4 + lax.div(chan, 2)
    return other, group, group * 4 + part, lat


def degree_owner(step, lat, chan):
    other = wrap(lat + LAT - step, LAT)
    group = 2 * lax.rem(lat, 4) + lax.rem(lax.div(lat, 4), 2)
    return other, group, other, 0


class Wire:
    def __init__(self, sends, receives, skip, source, target, sems):
        self.lat, self.chan = lax.axis_index("lat"), lax.axis_index("chan")
        self.sends, self.receives, self.skip = sends, receives, skip
        self.source, self.target = source, target
        self.send_sem, self.recv_sem, self.own_sem = sems

    def live(self, pair):
        if self.skip:
            return self.lat + pair[0] < LAT
        return pair[0] >= 0

    def own(self, pair):
        return (pair[0] == self.lat) & (pair[1] == self.chan) & self.live(pair)

    def far(self, pair):
        return jnp.logical_not((pair[0] == self.lat) & (pair[1] == self.chan)) & self.live(pair)

    def greet(self, barrier, total):
        def step_fn(step, count):
            source = self.receives(step, self.lat, self.chan)

            @pl.when(self.far(source))
            def _():
                pl.semaphore_signal(
                    barrier, inc=1, device_id={"lat": source[0], "chan": source[1]},
                    device_id_type=MESH,
                )

            return count + jnp.where(self.far(self.sends(step, self.lat, self.chan)), 1, 0)

        return lax.fori_loop(0, LAT, step_fn, total)

    def remote(self, pair, slot):
        return pltpu.make_async_remote_copy(
            src_ref=self.source.at[pair[2]],
            dst_ref=self.target.at[slot],
            send_sem=self.send_sem.at[pair[2]],
            recv_sem=self.recv_sem.at[slot],
            device_id={"lat": pair[0], "chan": pair[1]},
            device_id_type=MESH,
        )

    def local(self, pair):
        return pltpu.make_async_copy(
            self.source.at[pair[2]], self.target.at[pair[3]], self.own_sem
        )

    def start(self, step):
        pair = self.sends(step, self.lat, self.chan)

        @pl.when(self.own(pair))
        def _():
            self.local(pair).start()

        @pl.when(self.far(pair))
        def _():
            self.remote(pair, pair[3]).start()

    def start_all(self):
        def step_fn(step, carry):
            self.start(step)
            return carry

        lax.fori_loop(0, LAT, step_fn, 0)

    def arrive(self):
        def step_fn(step, carry):
            target = self.sends(step, self.lat, self.chan)
            source = self.receives(step, self.lat, self.chan)

            @pl.when(self.own(target))
            def _():
                self.local(target).wait()

            @pl.when(self.far(source))
            def _():
                self.remote(source, source[2]).wait_recv()

            return carry

        lax.fori_loop(0, LAT, step_fn, 0)

    def leave(self):
        def step_fn(step, carry):
            target = self.sends(step, self.lat, self.chan)

            @pl.when(self.far(target))
            def _():
                self.remote(target, target[3]).wait_send()

            return carry

        lax.fori_loop(0, LAT, step_fn, 0)


class Side:
    def __init__(self, parts, source, target, sems):
        self.lat, self.chan = lax.axis_index("lat"), lax.axis_index("chan")
        self.parts, self.source, self.target = parts, source, target
        self.send_sem, self.recv_sem, self.own_sem = sems

    def greet(self, barrier, total):
        def step_fn(step, count):
            pl.semaphore_signal(
                barrier, inc=1,
                device_id={"lat": self.lat, "chan": lax.rem(self.chan + step, CHAN)},
                device_id_type=MESH,
            )
            return count + 1

        return lax.fori_loop(1, CHAN, step_fn, total)

    def remote(self, step, incoming):
        other = lax.rem(self.chan + step, CHAN)
        slot = other if incoming else self.chan
        return pltpu.make_async_remote_copy(
            src_ref=self.source.at[other] if self.parts else self.source,
            dst_ref=self.target.at[slot],
            send_sem=self.send_sem.at[other],
            recv_sem=self.recv_sem.at[slot],
            device_id={"lat": self.lat, "chan": other},
            device_id_type=MESH,
        )

    def local(self):
        source = self.source.at[self.chan] if self.parts else self.source
        return pltpu.make_async_copy(source, self.target.at[self.chan], self.own_sem)

    def start(self):
        self.local().start()

        def step_fn(step, carry):
            self.remote(step, False).start()
            return carry

        lax.fori_loop(1, CHAN, step_fn, 0)

    def finish(self):
        self.local().wait()

        def step_fn(step, carry):
            self.remote(step, False).wait_send()
            self.remote(step, True).wait_recv()
            return carry

        lax.fori_loop(1, CHAN, step_fn, 0)


def lat_from(step, lat, chan):
    return lat_to(LAT - step, lat, chan)


def whole_to(step, lat, chan):
    other = wrap(lat + step, LAT)
    return other, chan, 0, lat


def whole_from(step, lat, chan):
    other = wrap(lat + LAT - step, LAT)
    return other, chan, other, lat


class Bulk(Wire):
    def remote(self, pair, slot):
        return pltpu.make_async_remote_copy(
            src_ref=self.source.at[pair[2]],
            dst_ref=self.target.at[slot],
            send_sem=self.send_sem,
            recv_sem=self.recv_sem,
            device_id={"lat": pair[0], "chan": pair[1]},
            device_id_type=MESH,
        )

    def local(self, pair):
        return pltpu.make_async_copy(
            self.source.at[pair[2]], self.target.at[pair[3]], self.recv_sem
        )

    def arrive(self):
        pltpu.make_async_copy(self.target, self.target, self.recv_sem).wait()

    def leave(self):
        sent = self.target.at[pl.ds(0, LAT - 1)]
        pltpu.make_async_copy(sent, sent, self.send_sem).wait()


class Whole(Bulk):
    def remote(self, pair, slot):
        return pltpu.make_async_remote_copy(
            src_ref=self.source,
            dst_ref=self.target.at[slot],
            send_sem=self.send_sem,
            recv_sem=self.recv_sem,
            device_id={"lat": pair[0], "chan": pair[1]},
            device_id_type=MESH,
        )

    def local(self, pair):
        return pltpu.make_async_copy(self.source, self.target.at[pair[3]], self.recv_sem)


class Halo:
    def __init__(self, source, target, send_sem, recv_sem):
        self.lat, self.chan = lax.axis_index("lat"), lax.axis_index("chan")
        self.source, self.target = source, target
        self.send_sem, self.recv_sem = send_sem, recv_sem
        self.up, self.down = self.lat < LAT - 1, self.lat > 0

    def copy(self, way):
        step = jnp.where(self.up, 1, -1) if way == 0 else jnp.where(self.down, -1, 1)
        other = self.lat + step
        return pltpu.make_async_remote_copy(
            src_ref=self.source.at[way],
            dst_ref=self.target.at[way],
            send_sem=self.send_sem.at[way],
            recv_sem=self.recv_sem.at[way],
            device_id={"lat": other, "chan": self.chan},
            device_id_type=MESH,
        )

    def start(self):
        pl.when(self.up)(lambda: self.copy(0).start())
        pl.when(self.down)(lambda: self.copy(1).start())

    def arrive(self):
        pl.when(self.down)(lambda: self.copy(0).wait_recv())
        pl.when(self.up)(lambda: self.copy(1).wait_recv())

    def leave(self):
        pl.when(self.up)(lambda: self.copy(0).wait_send())
        pl.when(self.down)(lambda: self.copy(1).wait_send())


CHUNKS = [(k * 128, min(128, NLON - k * 128)) for k in range(12)]
EDGES = (14, 15, 0, 1)


def edge_rows(f, field, part, out_ref):
    for k, (low, size) in enumerate(CHUNKS):
        slot = k % 4
        part[slot, :, :size] = field[:, low : low + size].astype(jnp.float32)
        for r, i in enumerate(EDGES):
            row = part[slot, pl.ds(i, 48, stride=16), :]
            out_ref[r // 2, f, r % 2, :, low : low + size] = row[:, :size].astype(jnp.bfloat16)


def band_block(info, target, source, same):
    relative = (source - target).astype(jnp.float32) - info[:, 0:1]
    total = jnp.zeros(relative.shape, jnp.float32)
    for k in range(4):
        keep = (relative == float(k)) & (info[:, 1:2] > float(k)) & same
        total = total + jnp.where(keep, info[:, 2 + k : 3 + k], 0.0)
    return total


def halo_place(index):
    edge = index // 16
    return jnp.where(edge < 2, edge - HALO, edge + ROWS - HALO)


def residuals(fields, edges, bands, outs):
    lat = lax.axis_index("lat")
    own = bands[lat].astype(jnp.float32)
    below = bands[jnp.maximum(lat - 1, 0)].astype(jnp.float32)
    above = bands[jnp.minimum(lat + 1, LAT - 1)].astype(jnp.float32)
    own = jnp.concatenate([own] * 16, axis=0)
    near = [below[14:15], below[15:16], above[0:1], above[1:2]]
    near = jnp.concatenate([jnp.broadcast_to(x, (16, 128)) for x in near], axis=0)

    row, column = iota((256, 256), 0), iota((256, 256), 1)
    inner = band_block(own, row % 16, column % 16, row // 16 == column // 16)
    row, column = iota((256, 64), 0), iota((256, 64), 1)
    outer = band_block(own, row % 16, halo_place(column), row // 16 == column % 16)
    row, column = iota((64, 256), 0), iota((64, 256), 1)
    outer_back = band_block(near, halo_place(row), column % 16, row % 16 == column // 16)
    left = (
        (inner.astype(jnp.bfloat16), outer.astype(jnp.bfloat16)),
        (inner.T.astype(jnp.bfloat16), outer_back.T.astype(jnp.bfloat16)),
    )
    for low, size in ((0, 512), (512, 512), (1024, 416)):
        live = (lat > 0, lat < LAT - 1)
        for b in range(3):
            for f in range(2):
                rim = [
                    jnp.where(live[r // 2], edges[r // 2, f, r % 2, 16 * b : 16 * b + 16, low : low + size].astype(jnp.float32), 0.0)
                    for r in range(4)
                ]
                rim = jnp.concatenate(rim, axis=0).astype(jnp.bfloat16)
                rows = slice(256 * b, 256 * b + 256)
                value = dense(left[f][0], fields[f][rows, low : low + size]) + dense(left[f][1], rim)
                outs[f][rows, low : low + size] = value.astype(jnp.bfloat16)


def meet(links):
    barrier = pltpu.get_barrier_semaphore()
    total = jnp.int32(0)
    for link in links:
        total = link.greet(barrier, total)
    pl.semaphore_wait(barrier, total)


def front_kernel(
    source_ref, grad_ref, info_ref, weight_ref, source_hbm, grad_hbm,
    order_ref, cosine_ref, sector_ref, quad_ref,
    out_ref, weights_ref, ahead_ref, behind_ref, far_ref,
    part, rows, table, near, message, landing, bands, spectral,
    fields, sums, edges, rim, field_sem, sum_sem, edge_send, edge_recv,
    info_send, info_recv, panel_send, panel_recv, *sems
):
    panels = Bulk(lat_to, lat_from, False, message, landing, (panel_send, panel_recv, None))
    degrees = Wire(spectral_to, spectral_from, True, spectral, out_ref, sems[0:3])
    info = Whole(whole_to, whole_from, False, info_ref, bands, (info_send, info_recv, None))
    side = Side(False, weight_ref, weights_ref, sems[3:6])
    halo = Halo(edges, rim, edge_send, edge_recv)
    loads = [
        pltpu.make_async_copy(ref, fields.at[f], field_sem.at[f])
        for f, ref in ((0, source_hbm), (1, grad_hbm))
    ]
    stores = [
        pltpu.make_async_copy(sums.at[f], ref, sum_sem.at[f])
        for f, ref in ((0, ahead_ref), (1, behind_ref))
    ]
    for load in loads:
        load.start()
    meet([panels, degrees, side])
    info.start_all()
    side.start()
    spread_kernel(source_ref, grad_ref, message, part, rows, panels)
    for f in range(2):
        loads[f].wait()
        edge_rows(f, fields.at[f], part, edges)
    halo.start()
    recurrence(order_ref, cosine_ref, sector_ref, table)
    info.arrive()
    finish_tables(quad_ref, bands, near, far_ref, table)
    halo.arrive()
    residuals([fields.at[0], fields.at[1]], rim, bands, [sums.at[0], sums.at[1]])
    for store in stores:
        store.start()
    panels.arrive()
    analysis_kernel(landing, near, spectral)
    degrees.start_all()
    info.leave()
    panels.leave()
    halo.leave()
    degrees.arrive()
    degrees.leave()
    side.finish()
    for store in stores:
        store.wait()


def back_kernel(
    reply_ref, grad_ref, table_ref, parts_ref, forward_ref, backward_ref,
    answers, message, landing, part, rows, panel_send, panel_recv, *sems
):
    degrees = Wire(spectral_from, degree_owner, True, reply_ref, answers, sems[0:3])
    panels = Bulk(lat_to, lat_from, False, message, landing, (panel_send, panel_recv, None))
    side = Side(True, grad_ref, parts_ref, sems[3:6])
    meet([degrees, panels, side])
    degrees.start_all()
    side.start()
    degrees.arrive()
    synthesis_kernel(answers, table_ref, message)
    panels.start_all()
    degrees.leave()
    panels.arrive()
    gather_kernel(landing, forward_ref, backward_ref, part, rows)
    panels.leave()
    side.finish()


def link_sems(counts):
    out = []
    for count in counts:
        out += [pltpu.SemaphoreType.DMA((count,))] * 2 + [pltpu.SemaphoreType.DMA]
    return out


def linked(kernel, collective_id, shapes, out_spaces, scratch, spaces, arrays):
    def spec(space):
        return pl.BlockSpec(memory_space=space)

    return pl.pallas_call(
        kernel,
        out_shape=shapes,
        in_specs=[spec(space) for space in spaces],
        out_specs=[spec(space) for space in out_spaces],
        scratch_shapes=scratch,
        compiler_params=pltpu.CompilerParams(
            collective_id=collective_id, has_side_effects=True, vmem_limit_bytes=VMEM_LIMIT
        ),
    )(*arrays)


def dot(spec, a, b):
    return jnp.einsum(spec, a, b, preferred_element_type=jnp.float32)


def per_device(source_field, band_start, band_width, band_coef, mixing_weight, output_grad):
    channels = source_field.shape[0]
    table = fourier_table()
    lon_analysis = jnp.asarray((table / math.sqrt(NLON)).astype(jnp.bfloat16))
    lon_synthesis = jnp.asarray((table / math.sqrt(MMAX)).astype(jnp.bfloat16))
    flat = channels * ROWS

    info = jnp.concatenate(
        [
            band_start.astype(jnp.bfloat16)[:, None],
            band_width.astype(jnp.bfloat16)[:, None],
            band_coef,
            jnp.zeros((ROWS, 122), jnp.bfloat16),
        ],
        axis=1,
    )
    vmem, anywhere = pltpu.VMEM, pl.ANY
    work = [vmem((4, flat, 128), jnp.float32), vmem((2, MMAX * ROWS, 128), jnp.float32)]
    received, weight, ahead, behind, far = linked(
        front_kernel,
        1,
        [
            bf16(LAT, 64, 128),
            bf16(CHAN, 6, channels, CHAN * channels),
            bf16(flat, NLON),
            bf16(flat, NLON),
            bf16(12, NLAT, 256),
        ],
        [anywhere] * 4 + [vmem],
        work
        + [
            vmem((4, 2048, 128), jnp.float32),
            vmem((12, 256, NLAT), jnp.bfloat16),
            vmem((LAT, 9, ROWS, 128), jnp.bfloat16),
            vmem((LAT, 9, ROWS, 128), jnp.bfloat16),
            vmem((LAT, ROWS, 128), jnp.bfloat16),
            vmem((LAT, 64, 128), jnp.bfloat16),
            vmem((2, flat, NLON), jnp.bfloat16),
            vmem((2, flat, NLON), jnp.bfloat16),
            vmem((2, 2, 2, channels, NLON), jnp.bfloat16),
            vmem((2, 2, 2, channels, NLON), jnp.bfloat16),
        ]
        + [pltpu.SemaphoreType.DMA((2,))] * 4
        + [pltpu.SemaphoreType.DMA] * 4
        + link_sems([LAT, CHAN]),
        [vmem, vmem, vmem] + [anywhere] * 3 + [vmem] * 4,
        [
            dot("ik,kn->in", source_field.reshape(flat, NLON), lon_analysis).astype(jnp.bfloat16),
            dot("ik,kn->in", output_grad.reshape(flat, NLON), lon_synthesis).astype(jnp.bfloat16),
            info,
            mixing_weight,
            source_field.reshape(flat, NLON),
            output_grad.reshape(flat, NLON),
            *legendre_inputs(),
        ],
    )

    pick = np.zeros((CHAN, channels, CHAN, 64), np.float32)
    for e in range(CHAN):
        pick[e, :, e, :channels] = np.eye(channels)
    pick = pick.reshape(CHAN * channels, 512)
    panel = pltpu.VMEM((2, CHAN, 192, 128), jnp.float32)
    reply, grad = local(
        mixing_kernel,
        [bf16(LAT, 64, 128), bf16(CHAN, 6, channels, CHAN * channels)],
        [panel, panel],
        received,
        weight,
        jnp.asarray(pick.astype(jnp.bfloat16)),
        jnp.asarray(pick.T.astype(jnp.bfloat16)),
    )
    grad_parts, forward, backward = linked(
        back_kernel,
        2,
        [bf16(CHAN, 6, channels, CHAN * channels), bf16(flat, 512), bf16(flat, 512)],
        [anywhere, vmem, vmem],
        [
            vmem((LAT, 64, 128), jnp.bfloat16),
            vmem((LAT, 9, ROWS, 128), jnp.bfloat16),
            vmem((LAT, 9, ROWS, 128), jnp.bfloat16),
        ]
        + work
        + [pltpu.SemaphoreType.DMA] * 2
        + link_sems([LAT, CHAN]),
        [anywhere, anywhere, vmem],
        [reply, grad, far],
    )
    grad_mixing = jnp.sum(grad_parts.astype(jnp.float32), axis=0)

    shape = (channels, ROWS, NLON)
    mixed_field = dot("ik,nk->in", forward, lon_synthesis) + ahead.astype(jnp.float32)
    grad_input = dot("ik,nk->in", backward, lon_analysis) + behind.astype(jnp.float32)
    return (
        mixed_field.astype(jnp.bfloat16).reshape(shape),
        grad_input.astype(jnp.bfloat16).reshape(shape),
        grad_mixing,
    )


def solution(mesh):
    in_specs = (
        P("chan", "lat", None),
        P("lat"),
        P("lat"),
        P("lat", None),
        P("lat", "chan", None),
        P("chan", "lat", None),
    )
    out_specs = (P("chan", "lat", None), P("chan", "lat", None), P("lat", "chan", None))
    return jax.shard_map(
        per_device, mesh=mesh, in_specs=in_specs, out_specs=out_specs, check_vma=False
    )
```

```python
import functools
import math

import jax
import jax.numpy as jnp
import numpy as np
from jax import lax
from jax.experimental import pallas as pl
from jax.experimental.pallas import tpu as pltpu
from jax.sharding import PartitionSpec as P

NLAT = 512
NLON = 1440
MMAX = 192
LMAX = 192
HALO = 2
LAT = 32
CHAN = 8
MODES = MMAX // LAT
ROWS = NLAT // LAT
MESH = pl.DeviceIdType.MESH
VMEM_LIMIT = 58 * 1024 * 1024


def log_norms():
    return np.array(
        [
            0.5
            * (
                math.log((2.0 * m + 1.0) / (4.0 * math.pi))
                + math.lgamma(m + 0.5)
                - math.lgamma(m + 1.0)
                - 0.5 * math.log(math.pi)
            )
            for m in range(MMAX)
        ],
        np.float32,
    )


def fourier_table():
    phase = 2.0 * math.pi / NLON * (np.outer(np.arange(NLON), np.arange(MMAX)) % NLON)
    table = np.zeros((NLON, 2, 256))
    table[:, 0, :MMAX] = np.cos(phase)
    table[:, 1, :MMAX] = -np.sin(phase)
    return table.reshape(NLON, 512)


def dense(a, b, dims=((1,), (0,))):
    return lax.dot_general(a, b, (dims, ((), ())), preferred_element_type=jnp.float32)


def iota(shape, axis):
    return lax.broadcasted_iota(jnp.int32, shape, axis)


def merge_lanes(a, b, c, d):
    lane = iota(a.shape, 1)
    return (
        jnp.where(lane < 96, a, b),
        jnp.where(lane < 64, b, c),
        jnp.where(lane < 32, c, d),
    )


def split_lanes(tiles):
    lane = iota(tiles[0].shape, 1)
    units = []
    for g in range(0, 9, 3):
        t0, t1, t2 = tiles[g : g + 3]
        units += [t0, jnp.where(lane < 64, t1, t0), jnp.where(lane < 32, t2, t1), t2]
    return units


def merge_rows(tiles):
    row = iota(tiles[0].shape, 0) % 8
    out = list(tiles[:8])
    for k in range(3):
        out[k] = jnp.where(row < 6, tiles[k], pltpu.roll(tiles[8], 6 - 2 * k, 0))
    return out


def split_rows(tiles):
    rows = tiles[0].shape[0]
    row = iota(tiles[0].shape, 0) % 8
    back = [pltpu.roll(tiles[k], rows - (6 - 2 * k), 0) for k in range(3)]
    return list(tiles) + [jnp.where(row < 2, back[0], jnp.where(row < 4, back[1], back[2]))]


def store_rows(out_ref, tiles):
    for p in range(4):
        pair = [tiles[2 * p + k].reshape(LAT, 8, 128) for k in range(2)]
        out_ref[:, 16 * p : 16 * p + 16, :] = jnp.concatenate(pair, axis=1).astype(jnp.bfloat16)


def load_rows(in_ref, live):
    tiles = []
    for p in range(4):
        pair = in_ref[:, 16 * p : 16 * p + 16, :].astype(jnp.float32)
        pair = jnp.where(live, pair, 0.0)
        tiles += [pair[:, :8].reshape(256, 128), pair[:, 8:].reshape(256, 128)]
    return tiles


def spread_kernel(source_ref, grad_ref, out_ref, part, rows, link):
    for f, ref in ((0, source_ref), (1, grad_ref)):
        for k in range(4):
            part[k] = ref[:, 128 * k : 128 * k + 128].astype(jnp.float32)

        def turn(i, carry):
            for half, count in ((0, 128), (1, 64)):
                a = part[half, pl.ds(i, 48, stride=16), :]
                b = part[2 + half, pl.ds(i, 48, stride=16), :]
                block = jnp.concatenate([a, b, a[:32]], axis=0).T
                rows[f, pl.ds(half * 2048 + i, count, stride=16), :] = block[:count]
            return carry

        lax.fori_loop(0, ROWS, turn, 0)

    def send(step, carry):
        d = wrap(link.lat + step, LAT)
        units = [
            rows[f, pl.ds(pl.multiple_of((d * 6 + m) * 16, 16), 16), :]
            for f in range(2)
            for m in range(MODES)
        ]
        for g in range(3):
            a, b, c, e = units[4 * g : 4 * g + 4]
            tiles = merge_lanes(a, pltpu.roll(b, 96, 1), pltpu.roll(c, 64, 1), pltpu.roll(e, 32, 1))
            for k in range(3):
                out_ref[d, 3 * g + k] = tiles[k].astype(jnp.bfloat16)
        link.start(step)
        return carry

    lax.fori_loop(0, LAT, send, 0)


def gather_kernel(in_ref, source_ref, grad_ref, part, rows):
    def receive(d, carry):
        tiles = [in_ref[d, k].astype(jnp.float32) for k in range(9)]
        units = split_lanes(tiles)
        for u in range(12):
            if u % 4:
                units[u] = pltpu.roll(units[u], 32 * (u % 4), 1)
            rows[u // 6, pl.ds(pl.multiple_of((d * 6 + u % 6) * 16, 16), 16), :] = units[u]
        return carry

    lax.fori_loop(0, LAT, receive, 0)
    for f, ref in ((0, source_ref), (1, grad_ref)):

        def turn(i, carry):
            block = rows[f, pl.ds(i, MMAX, stride=16), :]
            halves = (block[:128], jnp.concatenate([block[128:], jnp.zeros((64, 128), jnp.float32)], axis=0))
            for half in range(2):
                flat = halves[half].T
                part[half, pl.ds(i, 48, stride=16), :] = flat[:48]
                part[2 + half, pl.ds(i, 48, stride=16), :] = flat[48:96]
            return carry

        lax.fori_loop(0, ROWS, turn, 0)
        for k in range(4):
            ref[:, 128 * k : 128 * k + 128] = part[k].astype(jnp.bfloat16)


def recurrence(order_ref, cosine_ref, sector_ref, table):
    order = jnp.broadcast_to(order_ref[...], (8, NLAT))
    cosine = jnp.broadcast_to(cosine_ref[...], (8, NLAT))
    sector = sector_ref[...]
    order_sq = order * order
    table[...] = jnp.zeros_like(table)

    def advance(degree_index, carry):
        previous, earlier = carry
        degree = jnp.full((8, NLAT), degree_index, jnp.int32).astype(jnp.float32)
        lower = degree - 1.0
        scale_a = jnp.sqrt(
            jnp.maximum(4.0 * degree * degree - 1.0, 0.0)
            / jnp.maximum(degree * degree - order_sq, 1.0)
        )
        scale_b = jnp.sqrt(
            jnp.maximum(lower * lower - order_sq, 0.0)
            / jnp.maximum(4.0 * lower * lower - 1.0, 1.0)
        )
        value = scale_a * (cosine * previous - scale_b * earlier)
        value = jnp.where(degree < order, 0.0, jnp.where(degree == order, sector, value))
        place = LMAX - 1 - degree_index
        row = place // 6 * 8 + place % 6
        for k in range(4):
            table[k, pl.ds(row, 8, stride=256), :] = value[:, 128 * k : 128 * k + 128]
        return value, previous

    zero = sector * 0.0
    lax.fori_loop(0, LMAX, advance, (zero, zero))


def finish_tables(quad_ref, band_ref, near_ref, far_ref, table):
    info = band_ref[...].reshape(NLAT, 128).astype(jnp.float32)
    relative = (iota((NLAT, NLAT), 1) - iota((NLAT, NLAT), 0)).astype(jnp.float32) - info[:, 0:1]
    band = jnp.zeros((NLAT, NLAT), jnp.float32)
    for k in range(4):
        keep = (relative == float(k)) & (info[:, 1:2] > float(k))
        band = band + jnp.where(keep, info[:, 2 + k : 3 + k], 0.0)
    band = band.astype(jnp.bfloat16)
    for m in range(MODES):
        own = jnp.concatenate([table[k, 256 * m : 256 * m + 256, :] for k in range(4)], axis=1)
        analysis = (own * quad_ref[...]).astype(jnp.bfloat16)
        banded = dense(analysis, band)
        synthesis = own * (1.0 / math.sqrt(LMAX))
        near_ref[m] = banded.astype(jnp.bfloat16)
        near_ref[MODES + m] = synthesis.astype(jnp.bfloat16)
        far_ref[m] = synthesis.T.astype(jnp.bfloat16)
        far_ref[MODES + m] = banded.T.astype(jnp.bfloat16)


def analysis_kernel(in_ref, table_ref, out_ref):
    tiles = [in_ref[:, k].reshape(NLAT, 128).astype(jnp.float32) for k in range(9)]
    units = split_lanes(tiles)
    units = [dense(table_ref[u], units[u].astype(jnp.bfloat16)) for u in range(12)]
    packed = []
    for g in range(3):
        packed += merge_lanes(*units[4 * g : 4 * g + 4])
    store_rows(out_ref, merge_rows(packed))


def synthesis_kernel(in_ref, table_ref, out_ref):
    live = iota((LAT, 16, 128), 0) + lax.axis_index("lat") < LAT
    units = split_lanes(split_rows(load_rows(in_ref, live)))
    units = [dense(table_ref[u], units[u].astype(jnp.bfloat16)) for u in range(12)]
    for g in range(3):
        tiles = merge_lanes(*units[4 * g : 4 * g + 4])
        for k in range(3):
            out_ref[:, 3 * g + k] = tiles[k].reshape(LAT, ROWS, 128).astype(jnp.bfloat16)


def widen(weight_ref, pick_ref, wide):
    def degree(l, carry):
        rows = []
        for e in range(CHAN):
            rows += [weight_ref[e, l], jnp.zeros((16, 384), jnp.bfloat16)]
        wide[l] = dense(jnp.concatenate(rows, axis=0), pick_ref[...]).astype(jnp.bfloat16)
        return carry

    lax.fori_loop(0, 6, degree, 0)


def mixing_kernel(in_ref, wide, pick_t_ref, out_ref, grad_ref, before, after):
    lat, chan = lax.axis_index("lat"), lax.axis_index("chan")
    slot = iota((LAT, 16, 128), 0)
    other = (2 * (slot % 4) + lax.rem(chan, 2)) * 4 + lax.div(chan, 2)
    units = split_lanes(split_rows(load_rows(in_ref, other + lat < LAT)))
    for u in range(12):
        if u % 4:
            units[u] = pltpu.roll(units[u], 32 * (u % 4), 1)
        f, m = u // 6, u % 6
        before[f, :, 32 * m : 32 * m + 32, :] = units[u].reshape(CHAN, 32, 128)
    after[...] = jnp.zeros_like(after)
    lane = iota((24, 128), 1)

    def degree(l, carry):
        left = []
        for f in range(2):
            columns = []
            for p in range(4):
                a = before[f, 2 * p, pl.ds(l, 24, stride=8), :]
                b = before[f, 2 * p + 1, pl.ds(l, 24, stride=8), :]
                first = jnp.where(lane < 64, a, pltpu.roll(b, 64, 1))
                second = jnp.where(lane < 64, pltpu.roll(a, 80, 1), pltpu.roll(b, 16, 1))
                columns.append(jnp.concatenate([first, second], axis=0))
            left.append(jnp.concatenate(columns, axis=1).astype(jnp.bfloat16))
        weight = wide[l]
        mixed = dense(left[0], weight)
        back = dense(left[1], weight, ((1,), (1,)))
        dense_back = dense(left[1], pick_t_ref[...]).astype(jnp.bfloat16)
        grad = dense(left[0], dense_back, ((0,), (0,)))
        for e in range(CHAN):
            grad_ref[e, l] = grad[64 * e : 64 * e + 48].astype(jnp.bfloat16)
            for f, value in ((0, mixed), (1, back)):
                tile = value[:, 128 * (e // 2) : 128 * (e // 2) + 128]
                first, second = tile[:24], tile[24:]
                if e % 2:
                    first = pltpu.roll(first, 64, 1)
                second = pltpu.roll(second, 112 if e % 2 else 48, 1)
                after[f, e, pl.ds(l, 24, stride=8), :] = jnp.where(lane < 48, first, second)
        return carry

    lax.fori_loop(0, 6, degree, 0)
    units = [after[u // 6, :, 32 * (u % 6) : 32 * (u % 6) + 32, :].reshape(256, 128) for u in range(12)]
    packed = []
    for g in range(3):
        a, b, c, d = units[4 * g : 4 * g + 4]
        packed += merge_lanes(a, pltpu.roll(b, 96, 1), pltpu.roll(c, 64, 1), pltpu.roll(d, 32, 1))
    store_rows(out_ref, merge_rows(packed))


def bf16(*shape):
    return jax.ShapeDtypeStruct(shape, jnp.bfloat16)


def legendre_inputs():
    theta = math.pi * (np.arange(NLAT, dtype=np.float64) + 0.5) / NLAT
    cosine = np.cos(theta).astype(np.float32)[None, :]
    sine = np.sin(theta)
    orders = lax.axis_index("lat") * MODES + jnp.arange(8, dtype=jnp.int32)
    norm = jnp.asarray(np.concatenate([log_norms(), np.zeros(2, np.float32)]))
    order = orders.astype(jnp.float32)[:, None]
    own = lax.dynamic_slice(norm, (lax.axis_index("lat") * MODES,), (8,))
    sector = jnp.exp(own[:, None] + order * jnp.asarray(np.log(sine).astype(np.float32))[None, :])
    quadrature = (math.sqrt(NLAT) * math.pi / NLAT * sine).astype(np.float32)[None, :]
    return order, jnp.asarray(cosine), sector, jnp.asarray(quadrature)


def wrap(value, size):
    return value - jnp.where(value >= size, size, 0)


def lat_to(step, lat, chan):
    other = wrap(lat + step, LAT)
    return other, chan, other, lat


def spectral_to(step, lat, chan):
    other = wrap(lat + step, LAT)
    group = 2 * lax.rem(lat, 4) + lax.rem(lax.div(lat, 4), 2)
    return other, group, other, chan * 4 + lax.div(lat, 8)


def spectral_from(step, lat, chan):
    part = lax.rem(step + lat, 4)
    group = lax.rem(lax.div(step, 4) + chan, CHAN)
    other = (2 * part + lax.rem(chan, 2)) * 4 + lax.div(chan, 2)
    return other, group, group * 4 + part, lat


def degree_owner(step, lat, chan):
    other = wrap(lat + LAT - step, LAT)
    group = 2 * lax.rem(lat, 4) + lax.rem(lax.div(lat, 4), 2)
    return other, group, other, 0


class Wire:
    def __init__(self, sends, receives, skip, source, target, sems):
        self.lat, self.chan = lax.axis_index("lat"), lax.axis_index("chan")
        self.sends, self.receives, self.skip = sends, receives, skip
        self.source, self.target = source, target
        self.send_sem, self.recv_sem, self.own_sem = sems

    def live(self, pair):
        if self.skip:
            return self.lat + pair[0] < LAT
        return pair[0] >= 0

    def own(self, pair):
        return (pair[0] == self.lat) & (pair[1] == self.chan) & self.live(pair)

    def far(self, pair):
        return jnp.logical_not((pair[0] == self.lat) & (pair[1] == self.chan)) & self.live(pair)

    def greet(self, barrier, total):
        def step_fn(step, count):
            source = self.receives(step, self.lat, self.chan)

            @pl.when(self.far(source))
            def _():
                pl.semaphore_signal(
                    barrier, inc=1, device_id={"lat": source[0], "chan": source[1]},
                    device_id_type=MESH,
                )

            return count + jnp.where(self.far(self.sends(step, self.lat, self.chan)), 1, 0)

        return lax.fori_loop(0, LAT, step_fn, total)

    def remote(self, pair, slot):
        return pltpu.make_async_remote_copy(
            src_ref=self.source.at[pair[2]],
            dst_ref=self.target.at[slot],
            send_sem=self.send_sem.at[pair[2]],
            recv_sem=self.recv_sem.at[slot],
            device_id={"lat": pair[0], "chan": pair[1]},
            device_id_type=MESH,
        )

    def local(self, pair):
        return pltpu.make_async_copy(
            self.source.at[pair[2]], self.target.at[pair[3]], self.own_sem
        )

    def start(self, step):
        pair = self.sends(step, self.lat, self.chan)

        @pl.when(self.own(pair))
        def _():
            self.local(pair).start()

        @pl.when(self.far(pair))
        def _():
            self.remote(pair, pair[3]).start()

    def start_all(self):
        def step_fn(step, carry):
            self.start(step)
            return carry

        lax.fori_loop(0, LAT, step_fn, 0)

    def arrive(self):
        def step_fn(step, carry):
            target = self.sends(step, self.lat, self.chan)
            source = self.receives(step, self.lat, self.chan)

            @pl.when(self.own(target))
            def _():
                self.local(target).wait()

            @pl.when(self.far(source))
            def _():
                self.remote(source, source[2]).wait_recv()

            return carry

        lax.fori_loop(0, LAT, step_fn, 0)

    def leave(self):
        def step_fn(step, carry):
            target = self.sends(step, self.lat, self.chan)

            @pl.when(self.far(target))
            def _():
                self.remote(target, target[3]).wait_send()

            return carry

        lax.fori_loop(0, LAT, step_fn, 0)


class Side:
    def __init__(self, parts, source, target, sems):
        self.lat, self.chan = lax.axis_index("lat"), lax.axis_index("chan")
        self.parts, self.source, self.target = parts, source, target
        self.send_sem, self.recv_sem, self.own_sem = sems

    def greet(self, barrier, total):
        def step_fn(step, count):
            pl.semaphore_signal(
                barrier, inc=1,
                device_id={"lat": self.lat, "chan": lax.rem(self.chan + step, CHAN)},
                device_id_type=MESH,
            )
            return count + 1

        return lax.fori_loop(1, CHAN, step_fn, total)

    def remote(self, step, incoming):
        other = lax.rem(self.chan + step, CHAN)
        slot = other if incoming else self.chan
        return pltpu.make_async_remote_copy(
            src_ref=self.source.at[other] if self.parts else self.source,
            dst_ref=self.target.at[slot],
            send_sem=self.send_sem.at[other],
            recv_sem=self.recv_sem.at[slot],
            device_id={"lat": self.lat, "chan": other},
            device_id_type=MESH,
        )

    def local(self):
        source = self.source.at[self.chan] if self.parts else self.source
        return pltpu.make_async_copy(source, self.target.at[self.chan], self.own_sem)

    def start(self):
        self.local().start()

        def step_fn(step, carry):
            self.remote(step, False).start()
            return carry

        lax.fori_loop(1, CHAN, step_fn, 0)

    def finish(self):
        self.local().wait()

        def step_fn(step, carry):
            self.remote(step, False).wait_send()
            self.remote(step, True).wait_recv()
            return carry

        lax.fori_loop(1, CHAN, step_fn, 0)


def lat_from(step, lat, chan):
    return lat_to(LAT - step, lat, chan)


def whole_to(step, lat, chan):
    other = wrap(lat + step, LAT)
    return other, chan, 0, lat


def whole_from(step, lat, chan):
    other = wrap(lat + LAT - step, LAT)
    return other, chan, other, lat


class Bulk(Wire):
    def remote(self, pair, slot):
        return pltpu.make_async_remote_copy(
            src_ref=self.source.at[pair[2]],
            dst_ref=self.target.at[slot],
            send_sem=self.send_sem,
            recv_sem=self.recv_sem,
            device_id={"lat": pair[0], "chan": pair[1]},
            device_id_type=MESH,
        )

    def local(self, pair):
        return pltpu.make_async_copy(
            self.source.at[pair[2]], self.target.at[pair[3]], self.recv_sem
        )

    def arrive(self):
        pltpu.make_async_copy(self.target, self.target, self.recv_sem).wait()

    def leave(self):
        sent = self.target.at[pl.ds(0, LAT - 1)]
        pltpu.make_async_copy(sent, sent, self.send_sem).wait()


class Whole(Bulk):
    def remote(self, pair, slot):
        return pltpu.make_async_remote_copy(
            src_ref=self.source,
            dst_ref=self.target.at[slot],
            send_sem=self.send_sem,
            recv_sem=self.recv_sem,
            device_id={"lat": pair[0], "chan": pair[1]},
            device_id_type=MESH,
        )

    def local(self, pair):
        return pltpu.make_async_copy(self.source, self.target.at[pair[3]], self.recv_sem)


class Halo:
    def __init__(self, source, target, send_sem, recv_sem):
        self.lat, self.chan = lax.axis_index("lat"), lax.axis_index("chan")
        self.source, self.target = source, target
        self.send_sem, self.recv_sem = send_sem, recv_sem
        self.up, self.down = self.lat < LAT - 1, self.lat > 0

    def copy(self, way):
        step = jnp.where(self.up, 1, -1) if way == 0 else jnp.where(self.down, -1, 1)
        other = self.lat + step
        return pltpu.make_async_remote_copy(
            src_ref=self.source.at[way],
            dst_ref=self.target.at[way],
            send_sem=self.send_sem.at[way],
            recv_sem=self.recv_sem.at[way],
            device_id={"lat": other, "chan": self.chan},
            device_id_type=MESH,
        )

    def start(self):
        pl.when(self.up)(lambda: self.copy(0).start())
        pl.when(self.down)(lambda: self.copy(1).start())

    def arrive(self):
        pl.when(self.down)(lambda: self.copy(0).wait_recv())
        pl.when(self.up)(lambda: self.copy(1).wait_recv())

    def leave(self):
        pl.when(self.up)(lambda: self.copy(0).wait_send())
        pl.when(self.down)(lambda: self.copy(1).wait_send())


CHUNKS = [(k * 128, min(128, NLON - k * 128)) for k in range(12)]
EDGES = (14, 15, 0, 1)


def edge_rows(f, field, part, out_ref):
    for k, (low, size) in enumerate(CHUNKS):
        slot = k % 4
        part[slot, :, :size] = field[:, low : low + size].astype(jnp.float32)
        for r, i in enumerate(EDGES):
            row = part[slot, pl.ds(i, 48, stride=16), :]
            out_ref[r // 2, f, r % 2, :, low : low + size] = row[:, :size].astype(jnp.bfloat16)


def band_block(info, target, source, same):
    relative = (source - target).astype(jnp.float32) - info[:, 0:1]
    total = jnp.zeros(relative.shape, jnp.float32)
    for k in range(4):
        keep = (relative == float(k)) & (info[:, 1:2] > float(k)) & same
        total = total + jnp.where(keep, info[:, 2 + k : 3 + k], 0.0)
    return total


def halo_place(index):
    edge = index // 16
    return jnp.where(edge < 2, edge - HALO, edge + ROWS - HALO)


def residuals(fields, edges, bands, outs):
    lat = lax.axis_index("lat")
    own = bands[lat].astype(jnp.float32)
    below = bands[jnp.maximum(lat - 1, 0)].astype(jnp.float32)
    above = bands[jnp.minimum(lat + 1, LAT - 1)].astype(jnp.float32)
    own = jnp.concatenate([own] * 16, axis=0)
    near = [below[14:15], below[15:16], above[0:1], above[1:2]]
    near = jnp.concatenate([jnp.broadcast_to(x, (16, 128)) for x in near], axis=0)

    row, column = iota((256, 256), 0), iota((256, 256), 1)
    inner = band_block(own, row % 16, column % 16, row // 16 == column // 16)
    row, column = iota((256, 64), 0), iota((256, 64), 1)
    outer = band_block(own, row % 16, halo_place(column), row // 16 == column % 16)
    row, column = iota((64, 256), 0), iota((64, 256), 1)
    outer_back = band_block(near, halo_place(row), column % 16, row % 16 == column // 16)
    left = (
        (inner.astype(jnp.bfloat16), outer.astype(jnp.bfloat16)),
        (inner.T.astype(jnp.bfloat16), outer_back.T.astype(jnp.bfloat16)),
    )
    for low, size in ((0, 512), (512, 512), (1024, 416)):
        live = (lat > 0, lat < LAT - 1)
        for b in range(3):
            for f in range(2):
                rim = [
                    jnp.where(live[r // 2], edges[r // 2, f, r % 2, 16 * b : 16 * b + 16, low : low + size].astype(jnp.float32), 0.0)
                    for r in range(4)
                ]
                rim = jnp.concatenate(rim, axis=0).astype(jnp.bfloat16)
                rows = slice(256 * b, 256 * b + 256)
                value = dense(left[f][0], fields[f][rows, low : low + size]) + dense(left[f][1], rim)
                outs[f][rows, low : low + size] = value.astype(jnp.bfloat16)


def meet(links):
    barrier = pltpu.get_barrier_semaphore()
    total = jnp.int32(0)
    for link in links:
        total = link.greet(barrier, total)
    pl.semaphore_wait(barrier, total)


def block_kernel(
    source_ref, grad_ref, info_ref, weight_ref, source_hbm, grad_hbm,
    order_ref, cosine_ref, sector_ref, quad_ref, pick_ref, pick_t_ref,
    parts_ref, ahead_ref, behind_ref, forward_ref, backward_ref,
    part, rows, table, near, far, message, landing, bands, spectral, received,
    weights, wide, before, after, reply, grads, answers, grids,
    fields, sums, edges, rim, field_sem, sum_sem, edge_send, edge_recv,
    info_send, info_recv, panel_send, panel_recv, grid_send, grid_recv, *sems
):
    panels = Bulk(lat_to, lat_from, False, message, landing, (panel_send, panel_recv, None))
    grid_panels = Bulk(lat_to, lat_from, False, message, grids, (grid_send, grid_recv, None))
    degrees = Wire(spectral_to, spectral_from, True, spectral, received, sems[0:3])
    replies = Wire(spectral_from, degree_owner, True, reply, answers, sems[3:6])
    info = Whole(whole_to, whole_from, False, info_ref, bands, (info_send, info_recv, None))
    side = Side(False, weight_ref, weights, sems[6:9])
    grad_side = Side(True, grads, parts_ref, sems[9:12])
    halo = Halo(edges, rim, edge_send, edge_recv)
    loads = [
        pltpu.make_async_copy(ref, fields.at[f], field_sem.at[f])
        for f, ref in ((0, source_hbm), (1, grad_hbm))
    ]
    stores = [
        pltpu.make_async_copy(sums.at[f], ref, sum_sem.at[f])
        for f, ref in ((0, ahead_ref), (1, behind_ref))
    ]
    for load in loads:
        load.start()
    meet([panels, degrees, replies, side])
    info.start_all()
    side.start()
    spread_kernel(source_ref, grad_ref, message, part, rows, panels)
    for f in range(2):
        loads[f].wait()
        edge_rows(f, fields.at[f], part, edges)
    halo.start()
    recurrence(order_ref, cosine_ref, sector_ref, table)
    info.arrive()
    finish_tables(quad_ref, bands, near, far, table)
    halo.arrive()
    residuals([fields.at[0], fields.at[1]], rim, bands, [sums.at[0], sums.at[1]])
    for store in stores:
        store.start()
    panels.arrive()
    analysis_kernel(landing, near, spectral)
    degrees.start_all()
    side.finish()
    widen(weights, pick_ref, wide)
    info.leave()
    panels.leave()
    halo.leave()
    degrees.arrive()
    mixing_kernel(received, wide, pick_t_ref, reply, grads, before, after)
    replies.start_all()
    degrees.leave()
    replies.arrive()
    synthesis_kernel(answers, far, message)
    grid_panels.start_all()
    grad_side.start()
    replies.leave()
    grid_panels.arrive()
    gather_kernel(grids, forward_ref, backward_ref, part, rows)
    grid_panels.leave()
    grad_side.finish()
    for store in stores:
        store.wait()


def link_sems(counts):
    out = []
    for count in counts:
        out += [pltpu.SemaphoreType.DMA((count,))] * 2 + [pltpu.SemaphoreType.DMA]
    return out


def linked(kernel, collective_id, shapes, out_spaces, scratch, spaces, arrays):
    def spec(space):
        return pl.BlockSpec(memory_space=space)

    return pl.pallas_call(
        kernel,
        out_shape=shapes,
        in_specs=[spec(space) for space in spaces],
        out_specs=[spec(space) for space in out_spaces],
        scratch_shapes=scratch,
        compiler_params=pltpu.CompilerParams(
            collective_id=collective_id, has_side_effects=True, vmem_limit_bytes=VMEM_LIMIT
        ),
    )(*arrays)


def dot(spec, a, b):
    return jnp.einsum(spec, a, b, preferred_element_type=jnp.float32)


def per_device(source_field, band_start, band_width, band_coef, mixing_weight, output_grad):
    channels = source_field.shape[0]
    table = fourier_table()
    lon_analysis = jnp.asarray((table / math.sqrt(NLON)).astype(jnp.bfloat16))
    lon_synthesis = jnp.asarray((table / math.sqrt(MMAX)).astype(jnp.bfloat16))
    flat = channels * ROWS

    info = jnp.concatenate(
        [
            band_start.astype(jnp.bfloat16)[:, None],
            band_width.astype(jnp.bfloat16)[:, None],
            band_coef,
            jnp.zeros((ROWS, 122), jnp.bfloat16),
        ],
        axis=1,
    )
    vmem, anywhere = pltpu.VMEM, pl.ANY
    pick = np.zeros((CHAN, channels, CHAN, 64), np.float32)
    for e in range(CHAN):
        pick[e, :, e, :channels] = np.eye(channels)
    pick = pick.reshape(CHAN * channels, 512)

    def held(*shape):
        return vmem(shape, jnp.bfloat16)

    def panel(*shape):
        return vmem(shape, jnp.float32)

    grad_parts, ahead, behind, forward, backward = linked(
        block_kernel,
        1,
        [
            bf16(CHAN, 6, channels, CHAN * channels),
            bf16(flat, NLON),
            bf16(flat, NLON),
            bf16(flat, 512),
            bf16(flat, 512),
        ],
        [anywhere] * 3 + [vmem] * 2,
        [
            panel(4, flat, 128),
            panel(2, MMAX * ROWS, 128),
            panel(4, 2048, 128),
            held(12, 256, NLAT),
            held(12, NLAT, 256),
            held(LAT, 9, ROWS, 128),
            held(LAT, 9, ROWS, 128),
            held(LAT, ROWS, 128),
            held(LAT, 64, 128),
            held(LAT, 64, 128),
            held(CHAN, 6, channels, CHAN * channels),
            held(6, 512, 512),
            panel(2, CHAN, 192, 128),
            panel(2, CHAN, 192, 128),
            held(LAT, 64, 128),
            held(CHAN, 6, channels, CHAN * channels),
            held(LAT, 64, 128),
            held(LAT, 9, ROWS, 128),
            held(2, flat, NLON),
            held(2, flat, NLON),
            held(2, 2, 2, channels, NLON),
            held(2, 2, 2, channels, NLON),
        ]
        + [pltpu.SemaphoreType.DMA((2,))] * 4
        + [pltpu.SemaphoreType.DMA] * 6
        + link_sems([LAT, LAT, CHAN, CHAN]),
        [vmem, vmem, vmem] + [anywhere] * 3 + [vmem] * 6,
        [
            dot("ik,kn->in", source_field.reshape(flat, NLON), lon_analysis).astype(jnp.bfloat16),
            dot("ik,kn->in", output_grad.reshape(flat, NLON), lon_synthesis).astype(jnp.bfloat16),
            info,
            mixing_weight,
            source_field.reshape(flat, NLON),
            output_grad.reshape(flat, NLON),
            *legendre_inputs(),
            jnp.asarray(pick.astype(jnp.bfloat16)),
            jnp.asarray(pick.T.astype(jnp.bfloat16)),
        ],
    )
    grad_mixing = jnp.sum(grad_parts.astype(jnp.float32), axis=0)

    shape = (channels, ROWS, NLON)
    mixed_field = dot("ik,nk->in", forward, lon_synthesis) + ahead.astype(jnp.float32)
    grad_input = dot("ik,nk->in", backward, lon_analysis) + behind.astype(jnp.float32)
    return (
        mixed_field.astype(jnp.bfloat16).reshape(shape),
        grad_input.astype(jnp.bfloat16).reshape(shape),
        grad_mixing,
    )


def solution(mesh):
    in_specs = (
        P("chan", "lat", None),
        P("lat"),
        P("lat"),
        P("lat", None),
        P("lat", "chan", None),
        P("chan", "lat", None),
    )
    out_specs = (P("chan", "lat", None), P("chan", "lat", None), P("lat", "chan", None))
    return jax.shard_map(
        per_device, mesh=mesh, in_specs=in_specs, out_specs=out_specs, check_vma=False
    )
```

```python
import functools
import math

import jax
import jax.numpy as jnp
import numpy as np
from jax import lax
from jax.experimental import pallas as pl
from jax.experimental.pallas import tpu as pltpu
from jax.sharding import PartitionSpec as P

NLAT = 512
NLON = 1440
MMAX = 192
LMAX = 192
HALO = 2
LAT = 32
CHAN = 8
MODES = MMAX // LAT
ROWS = NLAT // LAT
MESH = pl.DeviceIdType.MESH
VMEM_LIMIT = 58 * 1024 * 1024


def log_norms():
    return np.array(
        [
            0.5
            * (
                math.log((2.0 * m + 1.0) / (4.0 * math.pi))
                + math.lgamma(m + 0.5)
                - math.lgamma(m + 1.0)
                - 0.5 * math.log(math.pi)
            )
            for m in range(MMAX)
        ],
        np.float32,
    )


def fourier_table(shift):
    phase = 2.0 * math.pi / NLON * (np.outer(np.arange(NLON), np.arange(MMAX)) % NLON)
    table = np.zeros((NLON, 2, 256))
    places = np.concatenate([np.arange(128), np.arange(128, MMAX) + shift])
    table[:, 0, places] = np.cos(phase)
    table[:, 1, places] = -np.sin(phase)
    return table.reshape(NLON, 512)


def dense(a, b, dims=((1,), (0,))):
    return lax.dot_general(a, b, (dims, ((), ())), preferred_element_type=jnp.float32)


def iota(shape, axis):
    return lax.broadcasted_iota(jnp.int32, shape, axis)


def merge_lanes(a, b, c, d):
    lane = iota(a.shape, 1)
    return (
        jnp.where(lane < 96, a, b),
        jnp.where(lane < 64, b, c),
        jnp.where(lane < 32, c, d),
    )


def split_lanes(tiles):
    lane = iota(tiles[0].shape, 1)
    units = []
    for g in range(0, 9, 3):
        t0, t1, t2 = tiles[g : g + 3]
        units += [t0, jnp.where(lane < 64, t1, t0), jnp.where(lane < 32, t2, t1), t2]
    return units


def merge_rows(tiles):
    row = iota(tiles[0].shape, 0) % 8
    out = list(tiles[:8])
    for k in range(3):
        out[k] = jnp.where(row < 6, tiles[k], pltpu.roll(tiles[8], 6 - 2 * k, 0))
    return out


def split_rows(tiles):
    rows = tiles[0].shape[0]
    row = iota(tiles[0].shape, 0) % 8
    back = [pltpu.roll(tiles[k], rows - (6 - 2 * k), 0) for k in range(3)]
    return list(tiles) + [jnp.where(row < 2, back[0], jnp.where(row < 4, back[1], back[2]))]


def store_rows(out_ref, tiles):
    for p in range(4):
        pair = [tiles[2 * p + k].reshape(LAT, 8, 128) for k in range(2)]
        out_ref[:, 16 * p : 16 * p + 16, :] = jnp.concatenate(pair, axis=1).astype(jnp.bfloat16)


def load_rows(in_ref, live):
    tiles = []
    for p in range(4):
        pair = in_ref[:, 16 * p : 16 * p + 16, :].astype(jnp.float32)
        pair = jnp.where(live, pair, 0.0)
        tiles += [pair[:, :8].reshape(256, 128), pair[:, 8:].reshape(256, 128)]
    return tiles


def spread_kernel(fields, tables, loads, out_ref, part, rows, link):
    for f in range(2):
        loads[f].wait()

        def transform(b, carry):
            block = pl.ds(pl.multiple_of(b * 256, 256), 256)
            panel = dense(fields[f, block, :], tables[f][...])
            part[2 * f, block, :] = panel[:, :128]
            part[2 * f + 1, block, :] = panel[:, 256:384]
            for r in range(2):
                half = panel[:, 256 * r + 128 : 256 * r + 256]
                part[4 + r, block, :] = half if f == 0 else part[4 + r, block, :] + half
            return carry

        lax.fori_loop(0, 3, transform, 0)

    def turn(i, carry):
        for k in range(3):
            a = part[2 * k, pl.ds(i, 48, stride=16), :]
            b = part[2 * k + 1, pl.ds(i, 48, stride=16), :]
            block = jnp.concatenate([a, b, a[:32]], axis=0).T
            if k < 2:
                rows[k, pl.ds(i, 128, stride=16), :] = block
            else:
                rows[0, pl.ds(2048 + i, 64, stride=16), :] = block[:64]
                rows[1, pl.ds(2048 + i, 64, stride=16), :] = block[64:]
        return carry

    lax.fori_loop(0, ROWS, turn, 0)

    def send(step, carry):
        d = wrap(link.lat + step, LAT)
        units = [
            rows[f, pl.ds(pl.multiple_of((d * 6 + m) * 16, 16), 16), :]
            for f in range(2)
            for m in range(MODES)
        ]
        for g in range(3):
            a, b, c, e = units[4 * g : 4 * g + 4]
            tiles = merge_lanes(a, pltpu.roll(b, 96, 1), pltpu.roll(c, 64, 1), pltpu.roll(e, 32, 1))
            for k in range(3):
                out_ref[d, 3 * g + k] = tiles[k].astype(jnp.bfloat16)
        link.start(step)
        return carry

    lax.fori_loop(0, LAT, send, 0)


def gather_kernel(in_ref, source_ref, grad_ref, part, rows):
    def receive(d, carry):
        tiles = [in_ref[d, k].astype(jnp.float32) for k in range(9)]
        units = split_lanes(tiles)
        for u in range(12):
            if u % 4:
                units[u] = pltpu.roll(units[u], 32 * (u % 4), 1)
            rows[u // 6, pl.ds(pl.multiple_of((d * 6 + u % 6) * 16, 16), 16), :] = units[u]
        return carry

    lax.fori_loop(0, LAT, receive, 0)

    def turn(i, carry):
        first = rows[0, pl.ds(i, MMAX, stride=16), :]
        second = rows[1, pl.ds(i, MMAX, stride=16), :]
        blocks = (
            first[:128], second[:128], jnp.concatenate([first[128:], second[128:]], axis=0)
        )
        for k in range(3):
            flat = blocks[k].T
            part[2 * k, pl.ds(i, 48, stride=16), :] = flat[:48]
            part[2 * k + 1, pl.ds(i, 48, stride=16), :] = flat[48:96]
        return carry

    lax.fori_loop(0, ROWS, turn, 0)
    for r in range(2):
        low = 256 * r
        half = part[4 + r, :768, :].astype(jnp.bfloat16)
        for f, ref in ((0, source_ref), (1, grad_ref)):
            ref[:, low : low + 128] = part[2 * f + r, :768, :].astype(jnp.bfloat16)
            ref[:, low + 128 : low + 256] = half


def recurrence(norm_ref, cosine_ref, log_sine_ref, table):
    lat = lax.axis_index("lat")
    order = (iota((8, NLAT), 0) + lat * MODES).astype(jnp.float32)
    cosine = jnp.broadcast_to(cosine_ref[...], (8, NLAT))
    sector = jnp.exp(norm_ref[lat][:, 0:1] + order * jnp.broadcast_to(log_sine_ref[...], (8, NLAT)))
    order_sq = order * order
    table[...] = jnp.zeros_like(table)

    def advance(degree_index, carry):
        previous, earlier = carry
        degree = jnp.full((8, NLAT), degree_index, jnp.int32).astype(jnp.float32)
        lower = degree - 1.0
        scale_a = jnp.sqrt(
            jnp.maximum(4.0 * degree * degree - 1.0, 0.0)
            / jnp.maximum(degree * degree - order_sq, 1.0)
        )
        scale_b = jnp.sqrt(
            jnp.maximum(lower * lower - order_sq, 0.0)
            / jnp.maximum(4.0 * lower * lower - 1.0, 1.0)
        )
        value = scale_a * (cosine * previous - scale_b * earlier)
        value = jnp.where(degree < order, 0.0, jnp.where(degree == order, sector, value))
        place = LMAX - 1 - degree_index
        row = place // 6 * 8 + place % 6
        for k in range(4):
            table[k, pl.ds(row, 8, stride=256), :] = value[:, 128 * k : 128 * k + 128]
        return value, previous

    zero = sector * 0.0
    lax.fori_loop(0, LMAX, advance, (zero, zero))


def finish_tables(quad_ref, band_ref, near_ref, far_ref, table):
    info = band_ref[...].reshape(NLAT, 128).astype(jnp.float32)
    relative = (iota((NLAT, NLAT), 1) - iota((NLAT, NLAT), 0)).astype(jnp.float32) - info[:, 0:1]
    band = jnp.zeros((NLAT, NLAT), jnp.float32)
    for k in range(4):
        keep = (relative == float(k)) & (info[:, 1:2] > float(k))
        band = band + jnp.where(keep, info[:, 2 + k : 3 + k], 0.0)
    band = band.astype(jnp.bfloat16)
    for m in range(MODES):
        own = jnp.concatenate([table[k, 256 * m : 256 * m + 256, :] for k in range(4)], axis=1)
        analysis = (own * quad_ref[...]).astype(jnp.bfloat16)
        banded = dense(analysis, band)
        synthesis = own * (1.0 / math.sqrt(LMAX))
        near_ref[m] = banded.astype(jnp.bfloat16)
        near_ref[MODES + m] = synthesis.astype(jnp.bfloat16)
        far_ref[m] = synthesis.T.astype(jnp.bfloat16)
        far_ref[MODES + m] = banded.T.astype(jnp.bfloat16)


def analysis_kernel(in_ref, table_ref, out_ref):
    tiles = [in_ref[:, k].reshape(NLAT, 128).astype(jnp.float32) for k in range(9)]
    units = split_lanes(tiles)
    units = [dense(table_ref[u], units[u].astype(jnp.bfloat16)) for u in range(12)]
    packed = []
    for g in range(3):
        packed += merge_lanes(*units[4 * g : 4 * g + 4])
    store_rows(out_ref, merge_rows(packed))


def synthesis_kernel(in_ref, table_ref, out_ref):
    live = iota((LAT, 16, 128), 0) + lax.axis_index("lat") < LAT
    units = split_lanes(split_rows(load_rows(in_ref, live)))
    units = [dense(table_ref[u], units[u].astype(jnp.bfloat16)) for u in range(12)]
    for g in range(3):
        tiles = merge_lanes(*units[4 * g : 4 * g + 4])
        for k in range(3):
            out_ref[:, 3 * g + k] = tiles[k].reshape(LAT, ROWS, 128).astype(jnp.bfloat16)


def widen(weight_ref, pick_ref, wide):
    def degree(l, carry):
        rows = []
        for e in range(CHAN):
            rows += [weight_ref[e, l], jnp.zeros((16, 384), jnp.bfloat16)]
        wide[l] = dense(jnp.concatenate(rows, axis=0), pick_ref[...]).astype(jnp.bfloat16)
        return carry

    lax.fori_loop(0, 6, degree, 0)


def mixing_kernel(in_ref, wide, pick_t_ref, out_ref, grad_ref, before, after):
    lat, chan = lax.axis_index("lat"), lax.axis_index("chan")
    slot = iota((LAT, 16, 128), 0)
    other = (2 * (slot % 4) + lax.rem(chan, 2)) * 4 + lax.div(chan, 2)
    units = split_lanes(split_rows(load_rows(in_ref, other + lat < LAT)))
    for u in range(12):
        if u % 4:
            units[u] = pltpu.roll(units[u], 32 * (u % 4), 1)
        f, m = u // 6, u % 6
        before[f, :, 32 * m : 32 * m + 32, :] = units[u].reshape(CHAN, 32, 128)
    after[...] = jnp.zeros_like(after)
    lane = iota((24, 128), 1)

    def degree(l, carry):
        left = []
        for f in range(2):
            columns = []
            for p in range(4):
                a = before[f, 2 * p, pl.ds(l, 24, stride=8), :]
                b = before[f, 2 * p + 1, pl.ds(l, 24, stride=8), :]
                first = jnp.where(lane < 64, a, pltpu.roll(b, 64, 1))
                second = jnp.where(lane < 64, pltpu.roll(a, 80, 1), pltpu.roll(b, 16, 1))
                columns.append(jnp.concatenate([first, second], axis=0))
            left.append(jnp.concatenate(columns, axis=1).astype(jnp.bfloat16))
        weight = wide[l]
        mixed = dense(left[0], weight)
        back = dense(left[1], weight, ((1,), (1,)))
        dense_back = dense(left[1], pick_t_ref[...]).astype(jnp.bfloat16)
        grad = dense(left[0], dense_back, ((0,), (0,)))
        for e in range(CHAN):
            grad_ref[e, l] = grad[64 * e : 64 * e + 48].astype(jnp.bfloat16)
            for f, value in ((0, mixed), (1, back)):
                tile = value[:, 128 * (e // 2) : 128 * (e // 2) + 128]
                first, second = tile[:24], tile[24:]
                if e % 2:
                    first = pltpu.roll(first, 64, 1)
                second = pltpu.roll(second, 112 if e % 2 else 48, 1)
                after[f, e, pl.ds(l, 24, stride=8), :] = jnp.where(lane < 48, first, second)
        return carry

    lax.fori_loop(0, 6, degree, 0)
    units = [after[u // 6, :, 32 * (u % 6) : 32 * (u % 6) + 32, :].reshape(256, 128) for u in range(12)]
    packed = []
    for g in range(3):
        a, b, c, d = units[4 * g : 4 * g + 4]
        packed += merge_lanes(a, pltpu.roll(b, 96, 1), pltpu.roll(c, 64, 1), pltpu.roll(d, 32, 1))
    store_rows(out_ref, merge_rows(packed))


def bf16(*shape):
    return jax.ShapeDtypeStruct(shape, jnp.bfloat16)


def legendre_inputs():
    theta = math.pi * (np.arange(NLAT, dtype=np.float64) + 0.5) / NLAT
    sine = np.sin(theta)
    norm = np.zeros((LAT, 8, 128), np.float32)
    norm[:, :MODES] = log_norms().reshape(LAT, MODES, 1)
    quadrature = math.sqrt(NLAT) * math.pi / NLAT * sine
    flat = [np.cos(theta), np.log(sine), quadrature]
    return [jnp.asarray(norm)] + [jnp.asarray(x.astype(np.float32)[None, :]) for x in flat]


def band_info(start_ref, width_ref, coef_ref, out_ref):
    row, lane = iota((ROWS, 128), 0), iota((ROWS, 128), 1)
    coef = coef_ref[...].astype(jnp.float32)
    total = pltpu.roll(jnp.concatenate([coef, jnp.zeros((ROWS, 124), jnp.float32)], axis=1), 2, 1)
    for i in range(ROWS):
        total = jnp.where((row == i) & (lane == 0), start_ref[i].astype(jnp.float32), total)
        total = jnp.where((row == i) & (lane == 1), width_ref[i].astype(jnp.float32), total)
    out_ref[...] = total.astype(jnp.bfloat16)


def wrap(value, size):
    return value - jnp.where(value >= size, size, 0)


def lat_to(step, lat, chan):
    other = wrap(lat + step, LAT)
    return other, chan, other, lat


def spectral_to(step, lat, chan):
    other = wrap(lat + step, LAT)
    group = 2 * lax.rem(lat, 4) + lax.rem(lax.div(lat, 4), 2)
    return other, group, other, chan * 4 + lax.div(lat, 8)


def spectral_from(step, lat, chan):
    part = lax.rem(step + lat, 4)
    group = lax.rem(lax.div(step, 4) + chan, CHAN)
    other = (2 * part + lax.rem(chan, 2)) * 4 + lax.div(chan, 2)
    return other, group, group * 4 + part, lat


def degree_owner(step, lat, chan):
    other = wrap(lat + LAT - step, LAT)
    group = 2 * lax.rem(lat, 4) + lax.rem(lax.div(lat, 4), 2)
    return other, group, other, 0


class Wire:
    def __init__(self, sends, receives, skip, source, target, sems):
        self.lat, self.chan = lax.axis_index("lat"), lax.axis_index("chan")
        self.sends, self.receives, self.skip = sends, receives, skip
        self.source, self.target = source, target
        self.send_sem, self.recv_sem, self.own_sem = sems

    def live(self, pair):
        if self.skip:
            return self.lat + pair[0] < LAT
        return pair[0] >= 0

    def own(self, pair):
        return (pair[0] == self.lat) & (pair[1] == self.chan) & self.live(pair)

    def far(self, pair):
        return jnp.logical_not((pair[0] == self.lat) & (pair[1] == self.chan)) & self.live(pair)

    def greet(self, barrier, total):
        def step_fn(step, count):
            source = self.receives(step, self.lat, self.chan)

            @pl.when(self.far(source))
            def _():
                pl.semaphore_signal(
                    barrier, inc=1, device_id={"lat": source[0], "chan": source[1]},
                    device_id_type=MESH,
                )

            return count + jnp.where(self.far(self.sends(step, self.lat, self.chan)), 1, 0)

        return lax.fori_loop(0, LAT, step_fn, total)

    def remote(self, pair, slot):
        return pltpu.make_async_remote_copy(
            src_ref=self.source.at[pair[2]],
            dst_ref=self.target.at[slot],
            send_sem=self.send_sem.at[pair[2]],
            recv_sem=self.recv_sem.at[slot],
            device_id={"lat": pair[0], "chan": pair[1]},
            device_id_type=MESH,
        )

    def local(self, pair):
        return pltpu.make_async_copy(
            self.source.at[pair[2]], self.target.at[pair[3]], self.own_sem
        )

    def start(self, step):
        pair = self.sends(step, self.lat, self.chan)

        @pl.when(self.own(pair))
        def _():
            self.local(pair).start()

        @pl.when(self.far(pair))
        def _():
            self.remote(pair, pair[3]).start()

    def start_all(self):
        def step_fn(step, carry):
            self.start(step)
            return carry

        lax.fori_loop(0, LAT, step_fn, 0)

    def arrive(self):
        def step_fn(step, carry):
            target = self.sends(step, self.lat, self.chan)
            source = self.receives(step, self.lat, self.chan)

            @pl.when(self.own(target))
            def _():
                self.local(target).wait()

            @pl.when(self.far(source))
            def _():
                self.remote(source, source[2]).wait_recv()

            return carry

        lax.fori_loop(0, LAT, step_fn, 0)

    def leave(self):
        def step_fn(step, carry):
            target = self.sends(step, self.lat, self.chan)

            @pl.when(self.far(target))
            def _():
                self.remote(target, target[3]).wait_send()

            return carry

        lax.fori_loop(0, LAT, step_fn, 0)


class Side:
    def __init__(self, parts, source, target, sems):
        self.lat, self.chan = lax.axis_index("lat"), lax.axis_index("chan")
        self.parts, self.source, self.target = parts, source, target
        self.send_sem, self.recv_sem, self.own_sem = sems

    def greet(self, barrier, total):
        def step_fn(step, count):
            pl.semaphore_signal(
                barrier, inc=1,
                device_id={"lat": self.lat, "chan": lax.rem(self.chan + step, CHAN)},
                device_id_type=MESH,
            )
            return count + 1

        return lax.fori_loop(1, CHAN, step_fn, total)

    def remote(self, step, incoming):
        other = lax.rem(self.chan + step, CHAN)
        slot = other if incoming else self.chan
        return pltpu.make_async_remote_copy(
            src_ref=self.source.at[other] if self.parts else self.source,
            dst_ref=self.target.at[slot],
            send_sem=self.send_sem.at[other],
            recv_sem=self.recv_sem.at[slot],
            device_id={"lat": self.lat, "chan": other},
            device_id_type=MESH,
        )

    def local(self):
        source = self.source.at[self.chan] if self.parts else self.source
        return pltpu.make_async_copy(source, self.target.at[self.chan], self.own_sem)

    def start(self):
        self.local().start()

        def step_fn(step, carry):
            self.remote(step, False).start()
            return carry

        lax.fori_loop(1, CHAN, step_fn, 0)

    def finish(self):
        self.local().wait()

        def step_fn(step, carry):
            self.remote(step, False).wait_send()
            self.remote(step, True).wait_recv()
            return carry

        lax.fori_loop(1, CHAN, step_fn, 0)


def lat_from(step, lat, chan):
    return lat_to(LAT - step, lat, chan)


def whole_to(step, lat, chan):
    other = wrap(lat + step, LAT)
    return other, chan, 0, lat


def whole_from(step, lat, chan):
    other = wrap(lat + LAT - step, LAT)
    return other, chan, other, lat


class Bulk(Wire):
    def remote(self, pair, slot):
        return pltpu.make_async_remote_copy(
            src_ref=self.source.at[pair[2]],
            dst_ref=self.target.at[slot],
            send_sem=self.send_sem,
            recv_sem=self.recv_sem,
            device_id={"lat": pair[0], "chan": pair[1]},
            device_id_type=MESH,
        )

    def local(self, pair):
        return pltpu.make_async_copy(
            self.source.at[pair[2]], self.target.at[pair[3]], self.recv_sem
        )

    def arrive(self):
        pltpu.make_async_copy(self.target, self.target, self.recv_sem).wait()

    def leave(self):
        sent = self.target.at[pl.ds(0, LAT - 1)]
        pltpu.make_async_copy(sent, sent, self.send_sem).wait()


class Whole(Bulk):
    def remote(self, pair, slot):
        return pltpu.make_async_remote_copy(
            src_ref=self.source,
            dst_ref=self.target.at[slot],
            send_sem=self.send_sem,
            recv_sem=self.recv_sem,
            device_id={"lat": pair[0], "chan": pair[1]},
            device_id_type=MESH,
        )

    def local(self, pair):
        return pltpu.make_async_copy(self.source, self.target.at[pair[3]], self.recv_sem)


class Halo:
    def __init__(self, source, target, send_sem, recv_sem):
        self.lat, self.chan = lax.axis_index("lat"), lax.axis_index("chan")
        self.source, self.target = source, target
        self.send_sem, self.recv_sem = send_sem, recv_sem
        self.up, self.down = self.lat < LAT - 1, self.lat > 0

    def copy(self, way):
        step = jnp.where(self.up, 1, -1) if way == 0 else jnp.where(self.down, -1, 1)
        other = self.lat + step
        return pltpu.make_async_remote_copy(
            src_ref=self.source.at[way],
            dst_ref=self.target.at[way],
            send_sem=self.send_sem.at[way],
            recv_sem=self.recv_sem.at[way],
            device_id={"lat": other, "chan": self.chan},
            device_id_type=MESH,
        )

    def start(self):
        pl.when(self.up)(lambda: self.copy(0).start())
        pl.when(self.down)(lambda: self.copy(1).start())

    def arrive(self):
        pl.when(self.down)(lambda: self.copy(0).wait_recv())
        pl.when(self.up)(lambda: self.copy(1).wait_recv())

    def leave(self):
        pl.when(self.up)(lambda: self.copy(0).wait_send())
        pl.when(self.down)(lambda: self.copy(1).wait_send())


CHUNKS = [(k * 128, min(128, NLON - k * 128)) for k in range(12)]
EDGES = (14, 15, 0, 1)


def edge_rows(f, field, part, out_ref):
    for k, (low, size) in enumerate(CHUNKS):
        slot = k % 4
        part[slot, :768, :size] = field[:, low : low + size].astype(jnp.float32)
        for r, i in enumerate(EDGES):
            row = part[slot, pl.ds(i, 48, stride=16), :]
            out_ref[r // 2, f, r % 2, :, low : low + size] = row[:, :size].astype(jnp.bfloat16)


def band_block(info, target, source, same):
    relative = (source - target).astype(jnp.float32) - info[:, 0:1]
    total = jnp.zeros(relative.shape, jnp.float32)
    for k in range(4):
        keep = (relative == float(k)) & (info[:, 1:2] > float(k)) & same
        total = total + jnp.where(keep, info[:, 2 + k : 3 + k], 0.0)
    return total


def halo_place(index):
    edge = index // 16
    return jnp.where(edge < 2, edge - HALO, edge + ROWS - HALO)


def residuals(fields, edges, bands, outs):
    lat = lax.axis_index("lat")
    own = bands[lat].astype(jnp.float32)
    below = bands[jnp.maximum(lat - 1, 0)].astype(jnp.float32)
    above = bands[jnp.minimum(lat + 1, LAT - 1)].astype(jnp.float32)
    own = jnp.concatenate([own] * 16, axis=0)
    near = [below[14:15], below[15:16], above[0:1], above[1:2]]
    near = jnp.concatenate([jnp.broadcast_to(x, (16, 128)) for x in near], axis=0)

    row, column = iota((256, 256), 0), iota((256, 256), 1)
    inner = band_block(own, row % 16, column % 16, row // 16 == column // 16)
    row, column = iota((256, 64), 0), iota((256, 64), 1)
    outer = band_block(own, row % 16, halo_place(column), row // 16 == column % 16)
    row, column = iota((64, 256), 0), iota((64, 256), 1)
    outer_back = band_block(near, halo_place(row), column % 16, row % 16 == column // 16)
    left = (
        (inner.astype(jnp.bfloat16), outer.astype(jnp.bfloat16)),
        (inner.T.astype(jnp.bfloat16), outer_back.T.astype(jnp.bfloat16)),
    )
    for low, size in ((0, 512), (512, 512), (1024, 416)):
        live = (lat > 0, lat < LAT - 1)
        for b in range(3):
            for f in range(2):
                rim = [
                    jnp.where(live[r // 2], edges[r // 2, f, r % 2, 16 * b : 16 * b + 16, low : low + size].astype(jnp.float32), 0.0)
                    for r in range(4)
                ]
                rim = jnp.concatenate(rim, axis=0).astype(jnp.bfloat16)
                rows = slice(256 * b, 256 * b + 256)
                value = dense(left[f][0], fields[f][rows, low : low + size]) + dense(left[f][1], rim)
                outs[f][rows, low : low + size] = value.astype(jnp.bfloat16)


def meet(links):
    barrier = pltpu.get_barrier_semaphore()
    total = jnp.int32(0)
    for link in links:
        total = link.greet(barrier, total)
    pl.semaphore_wait(barrier, total)


def block_kernel(
    start_ref, width_ref, coef_ref, weight_ref, source_hbm, grad_hbm, lon_first, lon_second,
    norm_ref, cosine_ref, log_sine_ref, quad_ref, pick_ref, pick_t_ref,
    parts_ref, ahead_ref, behind_ref, forward_ref, backward_ref,
    part, rows, table, near, far, message, landing, info_ref, bands, spectral, received,
    weights, wide, before, after, reply, grads, answers, grids,
    fields, sums, edges, rim, field_sem, sum_sem, edge_send, edge_recv,
    info_send, info_recv, panel_send, panel_recv, grid_send, grid_recv, *sems
):
    panels = Bulk(lat_to, lat_from, False, message, landing, (panel_send, panel_recv, None))
    grid_panels = Bulk(lat_to, lat_from, False, message, grids, (grid_send, grid_recv, None))
    degrees = Wire(spectral_to, spectral_from, True, spectral, received, sems[0:3])
    replies = Wire(spectral_from, degree_owner, True, reply, answers, sems[3:6])
    info = Whole(whole_to, whole_from, False, info_ref, bands, (info_send, info_recv, None))
    side = Side(False, weight_ref, weights, sems[6:9])
    grad_side = Side(True, grads, parts_ref, sems[9:12])
    halo = Halo(edges, rim, edge_send, edge_recv)
    loads = [
        pltpu.make_async_copy(ref, fields.at[f], field_sem.at[f])
        for f, ref in ((0, source_hbm), (1, grad_hbm))
    ]
    stores = [
        pltpu.make_async_copy(sums.at[f], ref, sum_sem.at[f])
        for f, ref in ((0, ahead_ref), (1, behind_ref))
    ]
    for load in loads:
        load.start()
    band_info(start_ref, width_ref, coef_ref, info_ref)
    meet([panels, degrees, replies, side])
    info.start_all()
    side.start()
    spread_kernel(fields, (lon_first, lon_second), loads, message, part, rows, panels)
    for f in range(2):
        edge_rows(f, fields.at[f], part, edges)
    halo.start()
    recurrence(norm_ref, cosine_ref, log_sine_ref, table)
    info.arrive()
    finish_tables(quad_ref, bands, near, far, table)
    halo.arrive()
    residuals([fields.at[0], fields.at[1]], rim, bands, [sums.at[0], sums.at[1]])
    for store in stores:
        store.start()
    panels.arrive()
    analysis_kernel(landing, near, spectral)
    degrees.start_all()
    side.finish()
    widen(weights, pick_ref, wide)
    info.leave()
    panels.leave()
    halo.leave()
    degrees.arrive()
    mixing_kernel(received, wide, pick_t_ref, reply, grads, before, after)
    replies.start_all()
    degrees.leave()
    replies.arrive()
    synthesis_kernel(answers, far, message)
    grid_panels.start_all()
    grad_side.start()
    replies.leave()
    grid_panels.arrive()
    gather_kernel(grids, forward_ref, backward_ref, part, rows)
    grid_panels.leave()
    grad_side.finish()
    for store in stores:
        store.wait()


def link_sems(counts):
    out = []
    for count in counts:
        out += [pltpu.SemaphoreType.DMA((count,))] * 2 + [pltpu.SemaphoreType.DMA]
    return out


def linked(kernel, collective_id, shapes, out_spaces, scratch, spaces, arrays):
    def spec(space):
        return pl.BlockSpec(memory_space=space)

    return pl.pallas_call(
        kernel,
        out_shape=shapes,
        in_specs=[spec(space) for space in spaces],
        out_specs=[spec(space) for space in out_spaces],
        scratch_shapes=scratch,
        compiler_params=pltpu.CompilerParams(
            collective_id=collective_id, has_side_effects=True, vmem_limit_bytes=VMEM_LIMIT
        ),
    )(*arrays)


def dot(spec, a, b):
    return jnp.einsum(spec, a, b, preferred_element_type=jnp.float32)


def per_device(source_field, band_start, band_width, band_coef, mixing_weight, output_grad):
    channels = source_field.shape[0]
    plain, moved = fourier_table(0), fourier_table(64)
    scales = (1.0 / math.sqrt(NLON), 1.0 / math.sqrt(MMAX))
    analysis, moved_analysis = [jnp.asarray((x * scales[0]).astype(jnp.bfloat16)) for x in (plain, moved)]
    synthesis, moved_synthesis = [jnp.asarray((x * scales[1]).astype(jnp.bfloat16)) for x in (plain, moved)]
    flat = channels * ROWS

    vmem, anywhere = pltpu.VMEM, pl.ANY
    pick = np.zeros((CHAN, channels, CHAN, 64), np.float32)
    for e in range(CHAN):
        pick[e, :, e, :channels] = np.eye(channels)
    pick = pick.reshape(CHAN * channels, 512)

    def held(*shape):
        return vmem(shape, jnp.bfloat16)

    def panel(*shape):
        return vmem(shape, jnp.float32)

    grad_parts, ahead, behind, forward, backward = linked(
        block_kernel,
        1,
        [
            bf16(CHAN, 6, channels, CHAN * channels),
            bf16(flat, NLON),
            bf16(flat, NLON),
            bf16(flat, 512),
            bf16(flat, 512),
        ],
        [anywhere] * 3 + [vmem] * 2,
        [
            panel(6, flat + 16, 128),
            panel(2, MMAX * ROWS + 16, 128),
            panel(4, 2048 + 256, 128),
            held(12, 256, NLAT),
            held(12, NLAT, 256),
            held(LAT, 9, ROWS, 128),
            held(LAT, 9, ROWS, 128),
            held(ROWS, 128),
            held(LAT, ROWS, 128),
            held(LAT, 64, 128),
            held(LAT, 64, 128),
            held(CHAN, 6, channels, CHAN * channels),
            held(6, 512, 512),
            panel(2, CHAN, 192 + 8, 128),
            panel(2, CHAN, 192 + 8, 128),
            held(LAT, 64, 128),
            held(CHAN, 6, channels, CHAN * channels),
            held(LAT, 64, 128),
            held(LAT, 9, ROWS, 128),
            held(2, flat, NLON),
            held(2, flat, NLON),
            held(2, 2, 2, channels, NLON),
            held(2, 2, 2, channels, NLON),
        ]
        + [pltpu.SemaphoreType.DMA((2,))] * 4
        + [pltpu.SemaphoreType.DMA] * 6
        + link_sems([LAT, LAT, CHAN, CHAN]),
        [pltpu.SMEM] * 2 + [vmem] + [anywhere] * 3 + [vmem] * 8,
        [
            band_start,
            band_width,
            band_coef,
            mixing_weight,
            source_field.reshape(flat, NLON),
            output_grad.reshape(flat, NLON),
            analysis,
            moved_synthesis,
            *legendre_inputs(),
            jnp.asarray(pick.astype(jnp.bfloat16)),
            jnp.asarray(pick.T.astype(jnp.bfloat16)),
        ],
    )
    grad_mixing = jnp.sum(grad_parts.astype(jnp.float32), axis=0)

    shape = (channels, ROWS, NLON)
    mixed_field = dot("ik,nk->in", forward, synthesis) + ahead.astype(jnp.float32)
    grad_input = dot("ik,nk->in", backward, moved_analysis) + behind.astype(jnp.float32)
    return (
        mixed_field.astype(jnp.bfloat16).reshape(shape),
        grad_input.astype(jnp.bfloat16).reshape(shape),
        grad_mixing,
    )


def solution(mesh):
    in_specs = (
        P("chan", "lat", None),
        P("lat"),
        P("lat"),
        P("lat", None),
        P("lat", "chan", None),
        P("chan", "lat", None),
    )
    out_specs = (P("chan", "lat", None), P("chan", "lat", None), P("lat", "chan", None))
    return jax.shard_map(
        per_device, mesh=mesh, in_specs=in_specs, out_specs=out_specs, check_vma=False
    )
```

```python
import functools
import math

import jax
import jax.numpy as jnp
import numpy as np
from jax import lax
from jax.experimental import pallas as pl
from jax.experimental.pallas import tpu as pltpu
from jax.sharding import PartitionSpec as P

NLAT = 512
NLON = 1440
MMAX = 192
LMAX = 192
HALO = 2
LAT = 32
CHAN = 8
MODES = MMAX // LAT
ROWS = NLAT // LAT
MESH = pl.DeviceIdType.MESH
VMEM_LIMIT = 58 * 1024 * 1024


def log_norms():
    return np.array(
        [
            0.5
            * (
                math.log((2.0 * m + 1.0) / (4.0 * math.pi))
                + math.lgamma(m + 0.5)
                - math.lgamma(m + 1.0)
                - 0.5 * math.log(math.pi)
            )
            for m in range(MMAX)
        ],
        np.float32,
    )


def fourier_table(shift):
    phase = 2.0 * math.pi / NLON * (np.outer(np.arange(NLON), np.arange(MMAX)) % NLON)
    table = np.zeros((NLON, 2, 256))
    places = np.concatenate([np.arange(128), np.arange(128, MMAX) + shift])
    table[:, 0, places] = np.cos(phase)
    table[:, 1, places] = -np.sin(phase)
    return table.reshape(NLON, 512)


def dense(a, b, dims=((1,), (0,))):
    return lax.dot_general(a, b, (dims, ((), ())), preferred_element_type=jnp.float32)


def iota(shape, axis):
    return lax.broadcasted_iota(jnp.int32, shape, axis)


def merge_lanes(a, b, c, d):
    lane = iota(a.shape, 1)
    return (
        jnp.where(lane < 96, a, b),
        jnp.where(lane < 64, b, c),
        jnp.where(lane < 32, c, d),
    )


def split_lanes(tiles):
    lane = iota(tiles[0].shape, 1)
    units = []
    for g in range(0, 9, 3):
        t0, t1, t2 = tiles[g : g + 3]
        units += [t0, jnp.where(lane < 64, t1, t0), jnp.where(lane < 32, t2, t1), t2]
    return units


def merge_rows(tiles):
    row = iota(tiles[0].shape, 0) % 8
    out = list(tiles[:8])
    for k in range(3):
        out[k] = jnp.where(row < 6, tiles[k], pltpu.roll(tiles[8], 6 - 2 * k, 0))
    return out


def split_rows(tiles):
    rows = tiles[0].shape[0]
    row = iota(tiles[0].shape, 0) % 8
    back = [pltpu.roll(tiles[k], rows - (6 - 2 * k), 0) for k in range(3)]
    return list(tiles) + [jnp.where(row < 2, back[0], jnp.where(row < 4, back[1], back[2]))]


def store_rows(out_ref, tiles):
    for p in range(4):
        pair = [tiles[2 * p + k].reshape(LAT, 8, 128) for k in range(2)]
        out_ref[:, 16 * p : 16 * p + 16, :] = jnp.concatenate(pair, axis=1).astype(jnp.bfloat16)


def load_rows(in_ref, live):
    tiles = []
    for p in range(4):
        pair = in_ref[:, 16 * p : 16 * p + 16, :].astype(jnp.float32)
        pair = jnp.where(live, pair, 0.0)
        tiles += [pair[:, :8].reshape(256, 128), pair[:, 8:].reshape(256, 128)]
    return tiles


def transform_kernel(fields, tables, loads, part):
    for f in range(2):
        loads[f].wait()

        def transform(b, carry):
            block = pl.ds(pl.multiple_of(b * 256, 256), 256)
            panel = dense(fields[f, block, :], tables[f][...])
            part[2 * f, block, :] = panel[:, :128]
            part[2 * f + 1, block, :] = panel[:, 256:384]
            for r in range(2):
                half = panel[:, 256 * r + 128 : 256 * r + 256]
                part[4 + r, block, :] = half if f == 0 else part[4 + r, block, :] + half
            return carry

        lax.fori_loop(0, 3, transform, 0)


def spread_kernel(out_ref, part, rows, link):
    def turn(i, carry):
        for k in range(3):
            a = part[2 * k, pl.ds(i, 48, stride=16), :]
            b = part[2 * k + 1, pl.ds(i, 48, stride=16), :]
            block = jnp.concatenate([a, b, a[:32]], axis=0).T
            if k < 2:
                rows[k, pl.ds(i, 128, stride=16), :] = block
            else:
                rows[0, pl.ds(2048 + i, 64, stride=16), :] = block[:64]
                rows[1, pl.ds(2048 + i, 64, stride=16), :] = block[64:]
        return carry

    lax.fori_loop(0, ROWS, turn, 0)

    def send(step, carry):
        d = wrap(link.lat + step, LAT)
        units = [
            rows[f, pl.ds(pl.multiple_of((d * 6 + m) * 16, 16), 16), :]
            for f in range(2)
            for m in range(MODES)
        ]
        for g in range(3):
            a, b, c, e = units[4 * g : 4 * g + 4]
            tiles = merge_lanes(a, pltpu.roll(b, 96, 1), pltpu.roll(c, 64, 1), pltpu.roll(e, 32, 1))
            for k in range(3):
                out_ref[d, 3 * g + k] = tiles[k].astype(jnp.bfloat16)
        link.start(step)
        return carry

    lax.fori_loop(0, LAT, send, 0)


def gather_kernel(in_ref, source_ref, grad_ref, part, rows, link):
    def receive(step, carry):
        d = link.arrive_one(step)
        tiles = [in_ref[d, k].astype(jnp.float32) for k in range(9)]
        units = split_lanes(tiles)
        for u in range(12):
            if u % 4:
                units[u] = pltpu.roll(units[u], 32 * (u % 4), 1)
            rows[u // 6, pl.ds(pl.multiple_of((d * 6 + u % 6) * 16, 16), 16), :] = units[u]
        return carry

    lax.fori_loop(0, LAT, receive, 0)

    def turn(i, carry):
        first = rows[0, pl.ds(i, MMAX, stride=16), :]
        second = rows[1, pl.ds(i, MMAX, stride=16), :]
        blocks = (
            first[:128], second[:128], jnp.concatenate([first[128:], second[128:]], axis=0)
        )
        for k in range(3):
            flat = blocks[k].T
            part[2 * k, pl.ds(i, 48, stride=16), :] = flat[:48]
            part[2 * k + 1, pl.ds(i, 48, stride=16), :] = flat[48:96]
        return carry

    lax.fori_loop(0, ROWS, turn, 0)
    for r in range(2):
        low = 256 * r
        half = part[4 + r, :768, :].astype(jnp.bfloat16)
        for f, ref in ((0, source_ref), (1, grad_ref)):
            ref[:, low : low + 128] = part[2 * f + r, :768, :].astype(jnp.bfloat16)
            ref[:, low + 128 : low + 256] = half


def recurrence(norm_ref, cosine_ref, log_sine_ref, table):
    lat = lax.axis_index("lat")
    order = (iota((8, NLAT), 0) + lat * MODES).astype(jnp.float32)
    cosine = jnp.broadcast_to(cosine_ref[...], (8, NLAT))
    sector = jnp.exp(norm_ref[lat][:, 0:1] + order * jnp.broadcast_to(log_sine_ref[...], (8, NLAT)))
    order_sq = order * order
    table[...] = jnp.zeros_like(table)

    def advance(degree_index, carry):
        previous, earlier = carry
        degree = jnp.full((8, NLAT), degree_index, jnp.int32).astype(jnp.float32)
        lower = degree - 1.0
        scale_a = jnp.sqrt(
            jnp.maximum(4.0 * degree * degree - 1.0, 0.0)
            / jnp.maximum(degree * degree - order_sq, 1.0)
        )
        scale_b = jnp.sqrt(
            jnp.maximum(lower * lower - order_sq, 0.0)
            / jnp.maximum(4.0 * lower * lower - 1.0, 1.0)
        )
        value = scale_a * (cosine * previous - scale_b * earlier)
        value = jnp.where(degree < order, 0.0, jnp.where(degree == order, sector, value))
        place = LMAX - 1 - degree_index
        row = place // 6 * 8 + place % 6
        for k in range(4):
            table[k, pl.ds(row, 8, stride=256), :] = value[:, 128 * k : 128 * k + 128]
        return value, previous

    zero = sector * 0.0
    lax.fori_loop(0, LMAX, advance, (zero, zero))


def finish_tables(quad_ref, band_ref, near_ref, far_ref, table):
    info = band_ref[...].reshape(NLAT, 128).astype(jnp.float32)
    relative = (iota((NLAT, NLAT), 1) - iota((NLAT, NLAT), 0)).astype(jnp.float32) - info[:, 0:1]
    band = jnp.zeros((NLAT, NLAT), jnp.float32)
    for k in range(4):
        keep = (relative == float(k)) & (info[:, 1:2] > float(k))
        band = band + jnp.where(keep, info[:, 2 + k : 3 + k], 0.0)
    band = band.astype(jnp.bfloat16)
    for m in range(MODES):
        own = jnp.concatenate([table[k, 256 * m : 256 * m + 256, :] for k in range(4)], axis=1)
        analysis = (own * quad_ref[...]).astype(jnp.bfloat16)
        banded = dense(analysis, band)
        synthesis = own * (1.0 / math.sqrt(LMAX))
        near_ref[m] = banded.astype(jnp.bfloat16)
        near_ref[MODES + m] = synthesis.astype(jnp.bfloat16)
        far_ref[m] = synthesis.T.astype(jnp.bfloat16)
        far_ref[MODES + m] = banded.T.astype(jnp.bfloat16)


def analysis_kernel(in_ref, table_ref, out_ref):
    tiles = [in_ref[:, k].reshape(NLAT, 128).astype(jnp.float32) for k in range(9)]
    units = split_lanes(tiles)
    units = [dense(table_ref[u], units[u].astype(jnp.bfloat16)) for u in range(12)]
    packed = []
    for g in range(3):
        packed += merge_lanes(*units[4 * g : 4 * g + 4])
    store_rows(out_ref, merge_rows(packed))


def synthesis_kernel(in_ref, table_ref, out_ref):
    live = iota((LAT, 16, 128), 0) + lax.axis_index("lat") < LAT
    units = split_lanes(split_rows(load_rows(in_ref, live)))
    units = [dense(table_ref[u], units[u].astype(jnp.bfloat16)) for u in range(12)]
    for g in range(3):
        tiles = merge_lanes(*units[4 * g : 4 * g + 4])
        for k in range(3):
            out_ref[:, 3 * g + k] = tiles[k].reshape(LAT, ROWS, 128).astype(jnp.bfloat16)


def widen(weight_ref, pick_ref, wide):
    def degree(l, carry):
        rows = []
        for e in range(CHAN):
            rows += [weight_ref[e, l], jnp.zeros((16, 384), jnp.bfloat16)]
        wide[l] = dense(jnp.concatenate(rows, axis=0), pick_ref[...]).astype(jnp.bfloat16)
        return carry

    lax.fori_loop(0, 6, degree, 0)


def mixing_kernel(in_ref, wide, pick_t_ref, out_ref, grad_ref, before, after):
    lat, chan = lax.axis_index("lat"), lax.axis_index("chan")
    slot = iota((LAT, 16, 128), 0)
    other = (2 * (slot % 4) + lax.rem(chan, 2)) * 4 + lax.div(chan, 2)
    units = split_lanes(split_rows(load_rows(in_ref, other + lat < LAT)))
    for u in range(12):
        if u % 4:
            units[u] = pltpu.roll(units[u], 32 * (u % 4), 1)
        f, m = u // 6, u % 6
        before[f, :, 32 * m : 32 * m + 32, :] = units[u].reshape(CHAN, 32, 128)
    after[...] = jnp.zeros_like(after)
    lane = iota((24, 128), 1)

    def degree(l, carry):
        left = []
        for f in range(2):
            columns = []
            for p in range(4):
                a = before[f, 2 * p, pl.ds(l, 24, stride=8), :]
                b = before[f, 2 * p + 1, pl.ds(l, 24, stride=8), :]
                first = jnp.where(lane < 64, a, pltpu.roll(b, 64, 1))
                second = jnp.where(lane < 64, pltpu.roll(a, 80, 1), pltpu.roll(b, 16, 1))
                columns.append(jnp.concatenate([first, second], axis=0))
            left.append(jnp.concatenate(columns, axis=1).astype(jnp.bfloat16))
        weight = wide[l]
        mixed = dense(left[0], weight)
        back = dense(left[1], weight, ((1,), (1,)))
        dense_back = dense(left[1], pick_t_ref[...]).astype(jnp.bfloat16)
        grad = dense(left[0], dense_back, ((0,), (0,)))
        for e in range(CHAN):
            grad_ref[e, l] = grad[64 * e : 64 * e + 48].astype(jnp.bfloat16)
            for f, value in ((0, mixed), (1, back)):
                tile = value[:, 128 * (e // 2) : 128 * (e // 2) + 128]
                first, second = tile[:24], tile[24:]
                if e % 2:
                    first = pltpu.roll(first, 64, 1)
                second = pltpu.roll(second, 112 if e % 2 else 48, 1)
                after[f, e, pl.ds(l, 24, stride=8), :] = jnp.where(lane < 48, first, second)
        return carry

    lax.fori_loop(0, 6, degree, 0)
    units = [after[u // 6, :, 32 * (u % 6) : 32 * (u % 6) + 32, :].reshape(256, 128) for u in range(12)]
    packed = []
    for g in range(3):
        a, b, c, d = units[4 * g : 4 * g + 4]
        packed += merge_lanes(a, pltpu.roll(b, 96, 1), pltpu.roll(c, 64, 1), pltpu.roll(d, 32, 1))
    store_rows(out_ref, merge_rows(packed))


def tail_kernel(
    forward_ref, backward_ref, ahead_ref, behind_ref, first_ref, second_ref, parts_ref,
    mixed_ref, input_ref, grad_ref
):
    for panel, table, extra, out in (
        (forward_ref, first_ref, ahead_ref, mixed_ref),
        (backward_ref, second_ref, behind_ref, input_ref),
    ):
        value = dense(panel[...], table[...]) + extra[...].astype(jnp.float32)
        out[...] = value.astype(jnp.bfloat16).reshape(out.shape)
    grad_ref[0] = jnp.sum(parts_ref[:, 0].astype(jnp.float32), axis=0)


def bf16(*shape):
    return jax.ShapeDtypeStruct(shape, jnp.bfloat16)


def legendre_inputs():
    theta = math.pi * (np.arange(NLAT, dtype=np.float64) + 0.5) / NLAT
    sine = np.sin(theta)
    norm = np.zeros((LAT, 8, 128), np.float32)
    norm[:, :MODES] = log_norms().reshape(LAT, MODES, 1)
    quadrature = math.sqrt(NLAT) * math.pi / NLAT * sine
    flat = [np.cos(theta), np.log(sine), quadrature]
    return [jnp.asarray(norm)] + [jnp.asarray(x.astype(np.float32)[None, :]) for x in flat]


def band_info(start_ref, width_ref, coef_ref, out_ref):
    row, lane = iota((ROWS, 128), 0), iota((ROWS, 128), 1)
    coef = coef_ref[...].astype(jnp.float32)
    total = pltpu.roll(jnp.concatenate([coef, jnp.zeros((ROWS, 124), jnp.float32)], axis=1), 2, 1)
    for i in range(ROWS):
        total = jnp.where((row == i) & (lane == 0), start_ref[i].astype(jnp.float32), total)
        total = jnp.where((row == i) & (lane == 1), width_ref[i].astype(jnp.float32), total)
    out_ref[...] = total.astype(jnp.bfloat16)


def wrap(value, size):
    return value - jnp.where(value >= size, size, 0)


def lat_to(step, lat, chan):
    other = wrap(lat + step, LAT)
    return other, chan, other, lat


def spectral_to(step, lat, chan):
    other = wrap(lat + step, LAT)
    group = 2 * lax.rem(lat, 4) + lax.rem(lax.div(lat, 4), 2)
    return other, group, other, chan * 4 + lax.div(lat, 8)


def spectral_from(step, lat, chan):
    part = lax.rem(step + lat, 4)
    group = lax.rem(lax.div(step, 4) + chan, CHAN)
    other = (2 * part + lax.rem(chan, 2)) * 4 + lax.div(chan, 2)
    return other, group, group * 4 + part, lat


def degree_owner(step, lat, chan):
    other = wrap(lat + LAT - step, LAT)
    group = 2 * lax.rem(lat, 4) + lax.rem(lax.div(lat, 4), 2)
    return other, group, other, 0


class Wire:
    def __init__(self, sends, receives, skip, source, target, sems):
        self.lat, self.chan = lax.axis_index("lat"), lax.axis_index("chan")
        self.sends, self.receives, self.skip = sends, receives, skip
        self.source, self.target = source, target
        self.send_sem, self.recv_sem, self.own_sem = sems

    def live(self, pair):
        if self.skip:
            return self.lat + pair[0] < LAT
        return pair[0] >= 0

    def own(self, pair):
        return (pair[0] == self.lat) & (pair[1] == self.chan) & self.live(pair)

    def far(self, pair):
        return jnp.logical_not((pair[0] == self.lat) & (pair[1] == self.chan)) & self.live(pair)

    def greet(self, barrier, total):
        def step_fn(step, count):
            source = self.receives(step, self.lat, self.chan)

            @pl.when(self.far(source))
            def _():
                pl.semaphore_signal(
                    barrier, inc=1, device_id={"lat": source[0], "chan": source[1]},
                    device_id_type=MESH,
                )

            return count + jnp.where(self.far(self.sends(step, self.lat, self.chan)), 1, 0)

        return lax.fori_loop(0, LAT, step_fn, total)

    def remote(self, pair, slot):
        return pltpu.make_async_remote_copy(
            src_ref=self.source.at[pair[2]],
            dst_ref=self.target.at[slot],
            send_sem=self.send_sem.at[pair[2]],
            recv_sem=self.recv_sem.at[slot],
            device_id={"lat": pair[0], "chan": pair[1]},
            device_id_type=MESH,
        )

    def local(self, pair):
        return pltpu.make_async_copy(
            self.source.at[pair[2]], self.target.at[pair[3]], self.own_sem
        )

    def start(self, step):
        pair = self.sends(step, self.lat, self.chan)

        @pl.when(self.own(pair))
        def _():
            self.local(pair).start()

        @pl.when(self.far(pair))
        def _():
            self.remote(pair, pair[3]).start()

    def start_all(self):
        def step_fn(step, carry):
            self.start(step)
            return carry

        lax.fori_loop(0, LAT, step_fn, 0)

    def arrive_one(self, step):
        target = self.sends(step, self.lat, self.chan)
        source = self.receives(step, self.lat, self.chan)

        @pl.when(self.own(target))
        def _():
            self.local(target).wait()

        @pl.when(self.far(source))
        def _():
            self.remote(source, source[2]).wait_recv()

        return source[2]

    def arrive(self):
        def step_fn(step, carry):
            self.arrive_one(step)
            return carry

        lax.fori_loop(0, LAT, step_fn, 0)

    def leave(self):
        def step_fn(step, carry):
            target = self.sends(step, self.lat, self.chan)

            @pl.when(self.far(target))
            def _():
                self.remote(target, target[3]).wait_send()

            return carry

        lax.fori_loop(0, LAT, step_fn, 0)


class Side:
    def __init__(self, parts, source, target, sems):
        self.lat, self.chan = lax.axis_index("lat"), lax.axis_index("chan")
        self.parts, self.source, self.target = parts, source, target
        self.send_sem, self.recv_sem, self.own_sem = sems

    def greet(self, barrier, total):
        def step_fn(step, count):
            pl.semaphore_signal(
                barrier, inc=1,
                device_id={"lat": self.lat, "chan": lax.rem(self.chan + step, CHAN)},
                device_id_type=MESH,
            )
            return count + 1

        return lax.fori_loop(1, CHAN, step_fn, total)

    def remote(self, step, incoming):
        other = lax.rem(self.chan + step, CHAN)
        slot = other if incoming else self.chan
        return pltpu.make_async_remote_copy(
            src_ref=self.source.at[other] if self.parts else self.source,
            dst_ref=self.target.at[slot],
            send_sem=self.send_sem.at[other],
            recv_sem=self.recv_sem.at[slot],
            device_id={"lat": self.lat, "chan": other},
            device_id_type=MESH,
        )

    def local(self):
        source = self.source.at[self.chan] if self.parts else self.source
        return pltpu.make_async_copy(source, self.target.at[self.chan], self.own_sem)

    def start(self):
        self.local().start()

        def step_fn(step, carry):
            self.remote(step, False).start()
            return carry

        lax.fori_loop(1, CHAN, step_fn, 0)

    def finish(self):
        self.local().wait()

        def step_fn(step, carry):
            self.remote(step, False).wait_send()
            self.remote(step, True).wait_recv()
            return carry

        lax.fori_loop(1, CHAN, step_fn, 0)


def lat_from(step, lat, chan):
    return lat_to(LAT - step, lat, chan)


def whole_to(step, lat, chan):
    other = wrap(lat + step, LAT)
    return other, chan, 0, lat


def whole_from(step, lat, chan):
    other = wrap(lat + LAT - step, LAT)
    return other, chan, other, lat


class Bulk(Wire):
    def remote(self, pair, slot):
        return pltpu.make_async_remote_copy(
            src_ref=self.source.at[pair[2]],
            dst_ref=self.target.at[slot],
            send_sem=self.send_sem,
            recv_sem=self.recv_sem,
            device_id={"lat": pair[0], "chan": pair[1]},
            device_id_type=MESH,
        )

    def local(self, pair):
        return pltpu.make_async_copy(
            self.source.at[pair[2]], self.target.at[pair[3]], self.recv_sem
        )

    def arrive(self):
        pltpu.make_async_copy(self.target, self.target, self.recv_sem).wait()

    def leave(self):
        sent = self.target.at[pl.ds(0, LAT - 1)]
        pltpu.make_async_copy(sent, sent, self.send_sem).wait()


class Whole(Bulk):
    def remote(self, pair, slot):
        return pltpu.make_async_remote_copy(
            src_ref=self.source,
            dst_ref=self.target.at[slot],
            send_sem=self.send_sem,
            recv_sem=self.recv_sem,
            device_id={"lat": pair[0], "chan": pair[1]},
            device_id_type=MESH,
        )

    def local(self, pair):
        return pltpu.make_async_copy(self.source, self.target.at[pair[3]], self.recv_sem)


class Halo:
    def __init__(self, source, target, send_sem, recv_sem):
        self.lat, self.chan = lax.axis_index("lat"), lax.axis_index("chan")
        self.source, self.target = source, target
        self.send_sem, self.recv_sem = send_sem, recv_sem
        self.up, self.down = self.lat < LAT - 1, self.lat > 0

    def copy(self, way):
        step = jnp.where(self.up, 1, -1) if way == 0 else jnp.where(self.down, -1, 1)
        other = self.lat + step
        return pltpu.make_async_remote_copy(
            src_ref=self.source.at[way],
            dst_ref=self.target.at[way],
            send_sem=self.send_sem.at[way],
            recv_sem=self.recv_sem.at[way],
            device_id={"lat": other, "chan": self.chan},
            device_id_type=MESH,
        )

    def start(self):
        pl.when(self.up)(lambda: self.copy(0).start())
        pl.when(self.down)(lambda: self.copy(1).start())

    def arrive(self):
        pl.when(self.down)(lambda: self.copy(0).wait_recv())
        pl.when(self.up)(lambda: self.copy(1).wait_recv())

    def leave(self):
        pl.when(self.up)(lambda: self.copy(0).wait_send())
        pl.when(self.down)(lambda: self.copy(1).wait_send())


CHUNKS = [(k * 128, min(128, NLON - k * 128)) for k in range(12)]
EDGES = (14, 15, 0, 1)


def edge_rows(f, field, part, out_ref):
    for k, (low, size) in enumerate(CHUNKS):
        slot = k % 4
        part[slot, :768, :size] = field[:, low : low + size].astype(jnp.float32)
        for r, i in enumerate(EDGES):
            row = part[slot, pl.ds(i, 48, stride=16), :]
            out_ref[r // 2, f, r % 2, :, low : low + size] = row[:, :size].astype(jnp.bfloat16)


def band_block(info, target, source, same):
    relative = (source - target).astype(jnp.float32) - info[:, 0:1]
    total = jnp.zeros(relative.shape, jnp.float32)
    for k in range(4):
        keep = (relative == float(k)) & (info[:, 1:2] > float(k)) & same
        total = total + jnp.where(keep, info[:, 2 + k : 3 + k], 0.0)
    return total


def halo_place(index):
    edge = index // 16
    return jnp.where(edge < 2, edge - HALO, edge + ROWS - HALO)


def residuals(fields, edges, bands, outs):
    lat = lax.axis_index("lat")
    own = bands[lat].astype(jnp.float32)
    below = bands[jnp.maximum(lat - 1, 0)].astype(jnp.float32)
    above = bands[jnp.minimum(lat + 1, LAT - 1)].astype(jnp.float32)
    own = jnp.concatenate([own] * 16, axis=0)
    near = [below[14:15], below[15:16], above[0:1], above[1:2]]
    near = jnp.concatenate([jnp.broadcast_to(x, (16, 128)) for x in near], axis=0)

    row, column = iota((256, 256), 0), iota((256, 256), 1)
    inner = band_block(own, row % 16, column % 16, row // 16 == column // 16)
    row, column = iota((256, 64), 0), iota((256, 64), 1)
    outer = band_block(own, row % 16, halo_place(column), row // 16 == column % 16)
    row, column = iota((64, 256), 0), iota((64, 256), 1)
    outer_back = band_block(near, halo_place(row), column % 16, row % 16 == column // 16)
    left = (
        (inner.astype(jnp.bfloat16), outer.astype(jnp.bfloat16)),
        (inner.T.astype(jnp.bfloat16), outer_back.T.astype(jnp.bfloat16)),
    )
    for low, size in ((0, 512), (512, 512), (1024, 416)):
        live = (lat > 0, lat < LAT - 1)
        for b in range(3):
            for f in range(2):
                rim = [
                    jnp.where(live[r // 2], edges[r // 2, f, r % 2, 16 * b : 16 * b + 16, low : low + size].astype(jnp.float32), 0.0)
                    for r in range(4)
                ]
                rim = jnp.concatenate(rim, axis=0).astype(jnp.bfloat16)
                rows = slice(256 * b, 256 * b + 256)
                value = dense(left[f][0], fields[f][rows, low : low + size]) + dense(left[f][1], rim)
                outs[f][rows, low : low + size] = value.astype(jnp.bfloat16)


def meet(links):
    barrier = pltpu.get_barrier_semaphore()
    total = jnp.int32(0)
    for link in links:
        total = link.greet(barrier, total)
    return lambda: pl.semaphore_wait(barrier, total)


def block_kernel(
    start_ref, width_ref, coef_ref, weight_ref, source_hbm, grad_hbm, lon_first, lon_second,
    norm_ref, cosine_ref, log_sine_ref, quad_ref, pick_ref, pick_t_ref,
    parts_ref, ahead_ref, behind_ref, forward_ref, backward_ref,
    part, rows, table, near, far, message, landing, info_ref, bands, spectral, received,
    weights, wide, before, after, reply, grads, answers, grids,
    fields, sums, edges, rim, field_sem, sum_sem, edge_send, edge_recv,
    info_send, info_recv, panel_send, panel_recv, *sems
):
    panels = Bulk(lat_to, lat_from, False, message, landing, (panel_send, panel_recv, None))
    grid_panels = Wire(lat_to, lat_from, False, message, grids, sems[12:15])
    degrees = Wire(spectral_to, spectral_from, True, spectral, received, sems[0:3])
    replies = Wire(spectral_from, degree_owner, True, reply, answers, sems[3:6])
    info = Whole(whole_to, whole_from, False, info_ref, bands, (info_send, info_recv, None))
    side = Side(False, weight_ref, weights, sems[6:9])
    grad_side = Side(True, grads, parts_ref, sems[9:12])
    halo = Halo(edges, rim, edge_send, edge_recv)
    loads = [
        pltpu.make_async_copy(ref, fields.at[f], field_sem.at[f])
        for f, ref in ((0, source_hbm), (1, grad_hbm))
    ]
    stores = [
        pltpu.make_async_copy(sums.at[f], ref, sum_sem.at[f])
        for f, ref in ((0, ahead_ref), (1, behind_ref))
    ]
    for load in loads:
        load.start()
    band_info(start_ref, width_ref, coef_ref, info_ref)
    met = meet([panels, degrees, replies, side])
    transform_kernel(fields, (lon_first, lon_second), loads, part)
    met()
    info.start_all()
    side.start()
    spread_kernel(message, part, rows, panels)
    for f in range(2):
        edge_rows(f, fields.at[f], part, edges)
    halo.start()
    recurrence(norm_ref, cosine_ref, log_sine_ref, table)
    info.arrive()
    finish_tables(quad_ref, bands, near, far, table)
    panels.arrive()
    analysis_kernel(landing, near, spectral)
    degrees.start_all()
    side.finish()
    widen(weights, pick_ref, wide)
    info.leave()
    panels.leave()
    halo.leave()
    degrees.arrive()
    mixing_kernel(received, wide, pick_t_ref, reply, grads, before, after)
    replies.start_all()
    degrees.leave()
    replies.arrive()
    synthesis_kernel(answers, far, message)
    grid_panels.start_all()
    grad_side.start()
    halo.arrive()
    residuals([fields.at[0], fields.at[1]], rim, bands, [sums.at[0], sums.at[1]])
    for store in stores:
        store.start()
    replies.leave()
    gather_kernel(grids, forward_ref, backward_ref, part, rows, grid_panels)
    grid_panels.leave()
    grad_side.finish()
    for store in stores:
        store.wait()


def link_sems(counts):
    out = []
    for count in counts:
        out += [pltpu.SemaphoreType.DMA((count,))] * 2 + [pltpu.SemaphoreType.DMA]
    return out


def linked(kernel, collective_id, shapes, out_spaces, scratch, spaces, arrays):
    def spec(space):
        return pl.BlockSpec(memory_space=space)

    return pl.pallas_call(
        kernel,
        out_shape=shapes,
        in_specs=[spec(space) for space in spaces],
        out_specs=[spec(space) for space in out_spaces],
        scratch_shapes=scratch,
        compiler_params=pltpu.CompilerParams(
            collective_id=collective_id, has_side_effects=True, vmem_limit_bytes=VMEM_LIMIT
        ),
    )(*arrays)


def dot(spec, a, b):
    return jnp.einsum(spec, a, b, preferred_element_type=jnp.float32)


def per_device(source_field, band_start, band_width, band_coef, mixing_weight, output_grad):
    channels = source_field.shape[0]
    plain, moved = fourier_table(0), fourier_table(64)
    scales = (1.0 / math.sqrt(NLON), 1.0 / math.sqrt(MMAX))
    analysis, moved_analysis, synthesis, moved_synthesis = [
        jnp.asarray((x * scale).astype(jnp.bfloat16))
        for x, scale in (
            (plain, scales[0]), (moved.T, scales[0]), (plain.T, scales[1]), (moved, scales[1])
        )
    ]
    flat = channels * ROWS

    vmem, anywhere = pltpu.VMEM, pl.ANY
    pick = np.zeros((CHAN, channels, CHAN, 64), np.float32)
    for e in range(CHAN):
        pick[e, :, e, :channels] = np.eye(channels)
    pick = pick.reshape(CHAN * channels, 512)

    def held(*shape):
        return vmem(shape, jnp.bfloat16)

    def panel(*shape):
        return vmem(shape, jnp.float32)

    grad_parts, ahead, behind, forward, backward = linked(
        block_kernel,
        1,
        [
            bf16(CHAN, 6, channels, CHAN * channels),
            bf16(flat, NLON),
            bf16(flat, NLON),
            bf16(flat, 512),
            bf16(flat, 512),
        ],
        [anywhere] * 3 + [vmem] * 2,
        [
            panel(6, flat + 16, 128),
            panel(2, MMAX * ROWS + 16, 128),
            panel(4, 2048 + 256, 128),
            held(12, 256, NLAT),
            held(12, NLAT, 256),
            held(LAT, 9, ROWS, 128),
            held(LAT, 9, ROWS, 128),
            held(ROWS, 128),
            held(LAT, ROWS, 128),
            held(LAT, 64, 128),
            held(LAT, 64, 128),
            held(CHAN, 6, channels, CHAN * channels),
            held(6, 512, 512),
            panel(2, CHAN, 192 + 8, 128),
            panel(2, CHAN, 192 + 8, 128),
            held(LAT, 64, 128),
            held(CHAN, 6, channels, CHAN * channels),
            held(LAT, 64, 128),
            held(LAT, 9, ROWS, 128),
            held(2, flat, NLON),
            held(2, flat, NLON),
            held(2, 2, 2, channels, NLON),
            held(2, 2, 2, channels, NLON),
        ]
        + [pltpu.SemaphoreType.DMA((2,))] * 4
        + [pltpu.SemaphoreType.DMA] * 4
        + link_sems([LAT, LAT, CHAN, CHAN, LAT]),
        [pltpu.SMEM] * 2 + [vmem] + [anywhere] * 3 + [vmem] * 8,
        [
            band_start,
            band_width,
            band_coef,
            mixing_weight,
            source_field.reshape(flat, NLON),
            output_grad.reshape(flat, NLON),
            analysis,
            moved_synthesis,
            *legendre_inputs(),
            jnp.asarray(pick.astype(jnp.bfloat16)),
            jnp.asarray(pick.T.astype(jnp.bfloat16)),
        ],
    )
    def rowwise(*block):
        return pl.BlockSpec(block, lambda i: (i,) + (0,) * (len(block) - 1))

    def fixed(*block):
        return pl.BlockSpec(block, lambda i: (0, 0))

    return pl.pallas_call(
        tail_kernel,
        grid=(6,),
        out_shape=[
            bf16(channels, ROWS, NLON),
            bf16(channels, ROWS, NLON),
            jax.ShapeDtypeStruct((6, channels, CHAN * channels), jnp.float32),
        ],
        in_specs=[rowwise(flat // 6, 512)] * 2
        + [rowwise(flat // 6, NLON)] * 2
        + [fixed(512, NLON)] * 2
        + [pl.BlockSpec((CHAN, 1, channels, CHAN * channels), lambda i: (0, i, 0, 0))],
        out_specs=[rowwise(channels // 6, ROWS, NLON)] * 2
        + [rowwise(1, channels, CHAN * channels)],
        compiler_params=pltpu.CompilerParams(vmem_limit_bytes=VMEM_LIMIT),
    )(forward, backward, ahead, behind, synthesis, moved_analysis, grad_parts)


def solution(mesh):
    in_specs = (
        P("chan", "lat", None),
        P("lat"),
        P("lat"),
        P("lat", None),
        P("lat", "chan", None),
        P("chan", "lat", None),
    )
    out_specs = (P("chan", "lat", None), P("chan", "lat", None), P("lat", "chan", None))
    return jax.shard_map(
        per_device, mesh=mesh, in_specs=in_specs, out_specs=out_specs, check_vma=False
    )
```

```python
import functools
import math

import jax
import jax.numpy as jnp
import numpy as np
from jax import lax
from jax.experimental import pallas as pl
from jax.experimental.pallas import tpu as pltpu
from jax.sharding import PartitionSpec as P

NLAT = 512
NLON = 1440
MMAX = 192
LMAX = 192
HALO = 2
LAT = 32
CHAN = 8
MODES = MMAX // LAT
ROWS = NLAT // LAT
MESH = pl.DeviceIdType.MESH
VMEM_LIMIT = 58 * 1024 * 1024


def log_norms():
    return np.array(
        [
            0.5
            * (
                math.log((2.0 * m + 1.0) / (4.0 * math.pi))
                + math.lgamma(m + 0.5)
                - math.lgamma(m + 1.0)
                - 0.5 * math.log(math.pi)
            )
            for m in range(MMAX)
        ],
        np.float32,
    )


def fourier_table(shift):
    phase = 2.0 * math.pi / NLON * (np.outer(np.arange(NLON), np.arange(MMAX)) % NLON)
    table = np.zeros((NLON, 2, 256))
    places = np.concatenate([np.arange(128), np.arange(128, MMAX) + shift])
    table[:, 0, places] = np.cos(phase)
    table[:, 1, places] = -np.sin(phase)
    return table.reshape(NLON, 512)


def dense(a, b, dims=((1,), (0,))):
    return lax.dot_general(a, b, (dims, ((), ())), preferred_element_type=jnp.float32)


def iota(shape, axis):
    return lax.broadcasted_iota(jnp.int32, shape, axis)


def merge_lanes(a, b, c, d):
    lane = iota(a.shape, 1)
    return (
        jnp.where(lane < 96, a, b),
        jnp.where(lane < 64, b, c),
        jnp.where(lane < 32, c, d),
    )


def split_lanes(tiles):
    lane = iota(tiles[0].shape, 1)
    units = []
    for g in range(0, 9, 3):
        t0, t1, t2 = tiles[g : g + 3]
        units += [t0, jnp.where(lane < 64, t1, t0), jnp.where(lane < 32, t2, t1), t2]
    return units


def merge_rows(tiles):
    row = iota(tiles[0].shape, 0) % 8
    out = list(tiles[:8])
    for k in range(3):
        out[k] = jnp.where(row < 6, tiles[k], pltpu.roll(tiles[8], 6 - 2 * k, 0))
    return out


def split_rows(tiles):
    rows = tiles[0].shape[0]
    row = iota(tiles[0].shape, 0) % 8
    back = [pltpu.roll(tiles[k], rows - (6 - 2 * k), 0) for k in range(3)]
    return list(tiles) + [jnp.where(row < 2, back[0], jnp.where(row < 4, back[1], back[2]))]


def store_rows(out_ref, tiles):
    for p in range(4):
        pair = [tiles[2 * p + k].reshape(LAT, 8, 128) for k in range(2)]
        out_ref[:, 16 * p : 16 * p + 16, :] = jnp.concatenate(pair, axis=1).astype(jnp.bfloat16)


def load_rows(in_ref, live):
    tiles = []
    for p in range(4):
        pair = in_ref[:, 16 * p : 16 * p + 16, :].astype(jnp.float32)
        pair = jnp.where(live, pair, 0.0)
        tiles += [pair[:, :8].reshape(256, 128), pair[:, 8:].reshape(256, 128)]
    return tiles


def transform_kernel(fields, tables, loads, part):
    for f in range(2):
        loads[f].wait()

        def transform(b, carry):
            block = pl.ds(pl.multiple_of(b * 256, 256), 256)
            panel = dense(fields[f, block, :], tables[f][...])
            part[2 * f, block, :] = panel[:, :128]
            part[2 * f + 1, block, :] = panel[:, 256:384]
            for r in range(2):
                half = panel[:, 256 * r + 128 : 256 * r + 256]
                part[4 + r, block, :] = half if f == 0 else part[4 + r, block, :] + half
            return carry

        lax.fori_loop(0, 3, transform, 0)


def spread_kernel(out_ref, part, rows, link):
    def turn(i, carry):
        for k in range(3):
            a = part[2 * k, pl.ds(i, 48, stride=16), :]
            b = part[2 * k + 1, pl.ds(i, 48, stride=16), :]
            block = jnp.concatenate([a, b, a[:32]], axis=0).T
            if k < 2:
                rows[k, pl.ds(i, 128, stride=16), :] = block
            else:
                rows[0, pl.ds(2048 + i, 64, stride=16), :] = block[:64]
                rows[1, pl.ds(2048 + i, 64, stride=16), :] = block[64:]
        return carry

    lax.fori_loop(0, ROWS, turn, 0)

    def send(step, carry):
        d = wrap(link.lat + step, LAT)
        units = [
            rows[f, pl.ds(pl.multiple_of((d * 6 + m) * 16, 16), 16), :]
            for f in range(2)
            for m in range(MODES)
        ]
        for g in range(3):
            a, b, c, e = units[4 * g : 4 * g + 4]
            tiles = merge_lanes(a, pltpu.roll(b, 96, 1), pltpu.roll(c, 64, 1), pltpu.roll(e, 32, 1))
            for k in range(3):
                out_ref[d, 3 * g + k] = tiles[k].astype(jnp.bfloat16)
        link.start(step)
        return carry

    lax.fori_loop(0, LAT, send, 0)


def gather_kernel(in_ref, source_ref, grad_ref, part, rows, link):
    def receive(step, carry):
        d = link.arrive_one(step)
        tiles = [in_ref[d, k].astype(jnp.float32) for k in range(9)]
        units = split_lanes(tiles)
        for u in range(12):
            if u % 4:
                units[u] = pltpu.roll(units[u], 32 * (u % 4), 1)
            rows[u // 6, pl.ds(pl.multiple_of((d * 6 + u % 6) * 16, 16), 16), :] = units[u]
        return carry

    lax.fori_loop(0, LAT, receive, 0)

    def turn(i, carry):
        first = rows[0, pl.ds(i, MMAX, stride=16), :]
        second = rows[1, pl.ds(i, MMAX, stride=16), :]
        blocks = (
            first[:128], second[:128], jnp.concatenate([first[128:], second[128:]], axis=0)
        )
        for k in range(3):
            flat = blocks[k].T
            part[2 * k, pl.ds(i, 48, stride=16), :] = flat[:48]
            part[2 * k + 1, pl.ds(i, 48, stride=16), :] = flat[48:96]
        return carry

    lax.fori_loop(0, ROWS, turn, 0)
    for r in range(2):
        low = 256 * r
        half = part[4 + r, :768, :].astype(jnp.bfloat16)
        for f, ref in ((0, source_ref), (1, grad_ref)):
            ref[:, low : low + 128] = part[2 * f + r, :768, :].astype(jnp.bfloat16)
            ref[:, low + 128 : low + 256] = half


def recurrence(norm_ref, cosine_ref, log_sine_ref, table):
    lat = lax.axis_index("lat")
    order = (iota((8, NLAT), 0) + lat * MODES).astype(jnp.float32)
    cosine = jnp.broadcast_to(cosine_ref[...], (8, NLAT))
    sector = jnp.exp(norm_ref[lat][:, 0:1] + order * jnp.broadcast_to(log_sine_ref[...], (8, NLAT)))
    order_sq = order * order
    table[...] = jnp.zeros_like(table)

    def advance(degree_index, carry):
        previous, earlier = carry
        degree = jnp.full((8, NLAT), degree_index, jnp.int32).astype(jnp.float32)
        lower = degree - 1.0
        scale_a = jnp.sqrt(
            jnp.maximum(4.0 * degree * degree - 1.0, 0.0)
            / jnp.maximum(degree * degree - order_sq, 1.0)
        )
        scale_b = jnp.sqrt(
            jnp.maximum(lower * lower - order_sq, 0.0)
            / jnp.maximum(4.0 * lower * lower - 1.0, 1.0)
        )
        value = scale_a * (cosine * previous - scale_b * earlier)
        value = jnp.where(degree < order, 0.0, jnp.where(degree == order, sector, value))
        place = LMAX - 1 - degree_index
        row = place // 6 * 8 + place % 6
        for k in range(4):
            table[k, pl.ds(row, 8, stride=256), :] = value[:, 128 * k : 128 * k + 128]
        return value, previous

    zero = sector * 0.0
    lax.fori_loop(0, LMAX, advance, (zero, zero))


def finish_tables(quad_ref, band_ref, near_ref, far_ref, table):
    info = band_ref[...].reshape(NLAT, 128).astype(jnp.float32)
    relative = (iota((NLAT, NLAT), 1) - iota((NLAT, NLAT), 0)).astype(jnp.float32) - info[:, 0:1]
    band = jnp.zeros((NLAT, NLAT), jnp.float32)
    for k in range(4):
        keep = (relative == float(k)) & (info[:, 1:2] > float(k))
        band = band + jnp.where(keep, info[:, 2 + k : 3 + k], 0.0)
    band = band.astype(jnp.bfloat16)
    for m in range(MODES):
        own = jnp.concatenate([table[k, 256 * m : 256 * m + 256, :] for k in range(4)], axis=1)
        analysis = (own * quad_ref[...]).astype(jnp.bfloat16)
        banded = dense(analysis, band)
        synthesis = own * (1.0 / math.sqrt(LMAX))
        near_ref[m] = banded.astype(jnp.bfloat16)
        near_ref[MODES + m] = synthesis.astype(jnp.bfloat16)
        far_ref[m] = synthesis.T.astype(jnp.bfloat16)
        far_ref[MODES + m] = banded.T.astype(jnp.bfloat16)


def analysis_kernel(in_ref, table_ref, out_ref):
    tiles = [in_ref[:, k].reshape(NLAT, 128).astype(jnp.float32) for k in range(9)]
    units = split_lanes(tiles)
    units = [dense(table_ref[u], units[u].astype(jnp.bfloat16)) for u in range(12)]
    packed = []
    for g in range(3):
        packed += merge_lanes(*units[4 * g : 4 * g + 4])
    store_rows(out_ref, merge_rows(packed))


def synthesis_kernel(in_ref, table_ref, out_ref):
    live = iota((LAT, 16, 128), 0) + lax.axis_index("lat") < LAT
    units = split_lanes(split_rows(load_rows(in_ref, live)))
    units = [dense(table_ref[u], units[u].astype(jnp.bfloat16)) for u in range(12)]
    for g in range(3):
        tiles = merge_lanes(*units[4 * g : 4 * g + 4])
        for k in range(3):
            out_ref[:, 3 * g + k] = tiles[k].reshape(LAT, ROWS, 128).astype(jnp.bfloat16)


def widen(weight_ref, pick_ref, wide):
    def degree(l, carry):
        rows = []
        for e in range(CHAN):
            rows += [weight_ref[e, l], jnp.zeros((16, 384), jnp.bfloat16)]
        wide[l] = dense(jnp.concatenate(rows, axis=0), pick_ref[...]).astype(jnp.bfloat16)
        return carry

    lax.fori_loop(0, 6, degree, 0)


def mixing_kernel(in_ref, wide, pick_t_ref, out_ref, grad_ref, before, after):
    lat, chan = lax.axis_index("lat"), lax.axis_index("chan")
    slot = iota((LAT, 16, 128), 0)
    other = (2 * (slot % 4) + lax.rem(chan, 2)) * 4 + lax.div(chan, 2)
    units = split_lanes(split_rows(load_rows(in_ref, other + lat < LAT)))
    for u in range(12):
        if u % 4:
            units[u] = pltpu.roll(units[u], 32 * (u % 4), 1)
        f, m = u // 6, u % 6
        before[f, :, 32 * m : 32 * m + 32, :] = units[u].reshape(CHAN, 32, 128)
    after[...] = jnp.zeros_like(after)
    lane = iota((24, 128), 1)

    def degree(l, carry):
        left = []
        for f in range(2):
            columns = []
            for p in range(4):
                a = before[f, 2 * p, pl.ds(l, 24, stride=8), :]
                b = before[f, 2 * p + 1, pl.ds(l, 24, stride=8), :]
                first = jnp.where(lane < 64, a, pltpu.roll(b, 64, 1))
                second = jnp.where(lane < 64, pltpu.roll(a, 80, 1), pltpu.roll(b, 16, 1))
                columns.append(jnp.concatenate([first, second], axis=0))
            left.append(jnp.concatenate(columns, axis=1).astype(jnp.bfloat16))
        weight = wide[l]
        mixed = dense(left[0], weight)
        back = dense(left[1], weight, ((1,), (1,)))
        dense_back = dense(left[1], pick_t_ref[...]).astype(jnp.bfloat16)
        grad = dense(left[0], dense_back, ((0,), (0,)))
        for e in range(CHAN):
            grad_ref[e, l] = grad[64 * e : 64 * e + 48].astype(jnp.bfloat16)
            for f, value in ((0, mixed), (1, back)):
                tile = value[:, 128 * (e // 2) : 128 * (e // 2) + 128]
                first, second = tile[:24], tile[24:]
                if e % 2:
                    first = pltpu.roll(first, 64, 1)
                second = pltpu.roll(second, 112 if e % 2 else 48, 1)
                after[f, e, pl.ds(l, 24, stride=8), :] = jnp.where(lane < 48, first, second)
        return carry

    lax.fori_loop(0, 6, degree, 0)
    units = [after[u // 6, :, 32 * (u % 6) : 32 * (u % 6) + 32, :].reshape(256, 128) for u in range(12)]
    packed = []
    for g in range(3):
        a, b, c, d = units[4 * g : 4 * g + 4]
        packed += merge_lanes(a, pltpu.roll(b, 96, 1), pltpu.roll(c, 64, 1), pltpu.roll(d, 32, 1))
    store_rows(out_ref, merge_rows(packed))


def tail_kernel(
    forward_ref, backward_ref, ahead_ref, behind_ref, first_ref, second_ref, parts_ref,
    mixed_ref, input_ref, grad_ref
):
    for panel, table, extra, out in (
        (forward_ref, first_ref, ahead_ref, mixed_ref),
        (backward_ref, second_ref, behind_ref, input_ref),
    ):
        value = dense(panel[...], table[...]) + extra[...].astype(jnp.float32)
        out[...] = value.astype(jnp.bfloat16).reshape(out.shape)
    grad_ref[...] = jnp.sum(parts_ref[...].astype(jnp.float32), axis=0)


def bf16(*shape):
    return jax.ShapeDtypeStruct(shape, jnp.bfloat16)


def legendre_inputs():
    theta = math.pi * (np.arange(NLAT, dtype=np.float64) + 0.5) / NLAT
    sine = np.sin(theta)
    norm = np.zeros((LAT, 8, 128), np.float32)
    norm[:, :MODES] = log_norms().reshape(LAT, MODES, 1)
    quadrature = math.sqrt(NLAT) * math.pi / NLAT * sine
    flat = [np.cos(theta), np.log(sine), quadrature]
    return [jnp.asarray(norm)] + [jnp.asarray(x.astype(np.float32)[None, :]) for x in flat]


def band_info(start_ref, width_ref, coef_ref, out_ref):
    row, lane = iota((ROWS, 128), 0), iota((ROWS, 128), 1)
    coef = coef_ref[...].astype(jnp.float32)
    total = pltpu.roll(jnp.concatenate([coef, jnp.zeros((ROWS, 124), jnp.float32)], axis=1), 2, 1)
    for i in range(ROWS):
        total = jnp.where((row == i) & (lane == 0), start_ref[i].astype(jnp.float32), total)
        total = jnp.where((row == i) & (lane == 1), width_ref[i].astype(jnp.float32), total)
    out_ref[...] = total.astype(jnp.bfloat16)


def wrap(value, size):
    return value - jnp.where(value >= size, size, 0)


def lat_to(step, lat, chan):
    other = wrap(lat + step, LAT)
    return other, chan, other, lat


def spectral_maps():
    lat, chan = lax.axis_index("lat"), lax.axis_index("chan")
    low = lax.rem(lat, 4)
    group = 2 * low + lax.rem(lax.div(lat, 4), 2)
    slot = chan * 4 + lax.div(lat, 8)
    base = lax.rem(chan, 2) * 4 + lax.div(chan, 2)

    def spectral_to(step, lat, chan):
        other = wrap(lat + step[0] * 4 + step[1], LAT)
        return other, group, other, slot

    def spectral_from(step, lat, chan):
        part = wrap(low + step[1], 4)
        near = wrap(chan + step[0], CHAN)
        return part * 8 + base, near, near * 4 + part, lat

    def degree_owner(step, lat, chan):
        other = wrap(lat + LAT - step[0] * 4 - step[1], LAT)
        return other, group, other, 0

    return spectral_to, spectral_from, degree_owner


class Wire:
    def __init__(self, sends, receives, skip, source, target, sems):
        self.lat, self.chan = lax.axis_index("lat"), lax.axis_index("chan")
        self.sends, self.receives, self.skip = sends, receives, skip
        self.source, self.target = source, target
        self.send_sem, self.recv_sem, self.own_sem = sems

    def each(self, body, carry):
        if not self.skip:
            return lax.fori_loop(0, LAT, body, carry)

        def four(outer, carry):
            for inner in range(4):
                carry = body((outer, inner), carry)
            return carry

        return lax.fori_loop(0, LAT // 4, four, carry)

    def live(self, pair):
        if self.skip:
            return self.lat + pair[0] < LAT
        return pair[0] >= 0

    def own(self, pair):
        return (pair[0] == self.lat) & (pair[1] == self.chan) & self.live(pair)

    def far(self, pair):
        return jnp.logical_not((pair[0] == self.lat) & (pair[1] == self.chan)) & self.live(pair)

    def greet(self, barrier, total):
        def step_fn(step, count):
            source = self.receives(step, self.lat, self.chan)

            @pl.when(self.far(source))
            def _():
                pl.semaphore_signal(
                    barrier, inc=1, device_id={"lat": source[0], "chan": source[1]},
                    device_id_type=MESH,
                )

            return count + jnp.where(self.far(self.sends(step, self.lat, self.chan)), 1, 0)

        return self.each(step_fn, total)

    def remote(self, pair, slot):
        return pltpu.make_async_remote_copy(
            src_ref=self.source.at[pair[2]],
            dst_ref=self.target.at[slot],
            send_sem=self.send_sem.at[pair[2]],
            recv_sem=self.recv_sem.at[slot],
            device_id={"lat": pair[0], "chan": pair[1]},
            device_id_type=MESH,
        )

    def local(self, pair):
        return pltpu.make_async_copy(
            self.source.at[pair[2]], self.target.at[pair[3]], self.own_sem
        )

    def start(self, step):
        pair = self.sends(step, self.lat, self.chan)

        @pl.when(self.own(pair))
        def _():
            self.local(pair).start()

        @pl.when(self.far(pair))
        def _():
            self.remote(pair, pair[3]).start()

    def start_all(self):
        def step_fn(step, carry):
            self.start(step)
            return carry

        self.each(step_fn, 0)

    def arrive_one(self, step):
        target = self.sends(step, self.lat, self.chan)
        source = self.receives(step, self.lat, self.chan)

        @pl.when(self.own(target))
        def _():
            self.local(target).wait()

        @pl.when(self.far(source))
        def _():
            self.remote(source, source[2]).wait_recv()

        return source[2]

    def arrive(self):
        def step_fn(step, carry):
            self.arrive_one(step)
            return carry

        self.each(step_fn, 0)

    def leave(self):
        def step_fn(step, carry):
            target = self.sends(step, self.lat, self.chan)

            @pl.when(self.far(target))
            def _():
                self.remote(target, target[3]).wait_send()

            return carry

        self.each(step_fn, 0)


class Side:
    def __init__(self, parts, source, target, sems):
        self.lat, self.chan = lax.axis_index("lat"), lax.axis_index("chan")
        self.parts, self.source, self.target = parts, source, target
        self.send_sem, self.recv_sem, self.own_sem = sems

    def greet(self, barrier, total):
        def step_fn(step, count):
            pl.semaphore_signal(
                barrier, inc=1,
                device_id={"lat": self.lat, "chan": lax.rem(self.chan + step, CHAN)},
                device_id_type=MESH,
            )
            return count + 1

        return lax.fori_loop(1, CHAN, step_fn, total)

    def remote(self, step, incoming):
        other = lax.rem(self.chan + step, CHAN)
        slot = other if incoming else self.chan
        return pltpu.make_async_remote_copy(
            src_ref=self.source.at[other] if self.parts else self.source,
            dst_ref=self.target.at[slot],
            send_sem=self.send_sem.at[other],
            recv_sem=self.recv_sem.at[slot],
            device_id={"lat": self.lat, "chan": other},
            device_id_type=MESH,
        )

    def local(self):
        source = self.source.at[self.chan] if self.parts else self.source
        return pltpu.make_async_copy(source, self.target.at[self.chan], self.own_sem)

    def start(self):
        self.local().start()

        def step_fn(step, carry):
            self.remote(step, False).start()
            return carry

        lax.fori_loop(1, CHAN, step_fn, 0)

    def finish(self):
        self.local().wait()

        def step_fn(step, carry):
            self.remote(step, False).wait_send()
            self.remote(step, True).wait_recv()
            return carry

        lax.fori_loop(1, CHAN, step_fn, 0)


def lat_from(step, lat, chan):
    return lat_to(LAT - step, lat, chan)


def whole_to(step, lat, chan):
    other = wrap(lat + step, LAT)
    return other, chan, 0, lat


def whole_from(step, lat, chan):
    other = wrap(lat + LAT - step, LAT)
    return other, chan, other, lat


class Bulk(Wire):
    def remote(self, pair, slot):
        return pltpu.make_async_remote_copy(
            src_ref=self.source.at[pair[2]],
            dst_ref=self.target.at[slot],
            send_sem=self.send_sem,
            recv_sem=self.recv_sem,
            device_id={"lat": pair[0], "chan": pair[1]},
            device_id_type=MESH,
        )

    def local(self, pair):
        return pltpu.make_async_copy(
            self.source.at[pair[2]], self.target.at[pair[3]], self.recv_sem
        )

    def arrive(self):
        pltpu.make_async_copy(self.target, self.target, self.recv_sem).wait()

    def leave(self):
        sent = self.target.at[pl.ds(0, LAT - 1)]
        pltpu.make_async_copy(sent, sent, self.send_sem).wait()


class Whole(Bulk):
    def remote(self, pair, slot):
        return pltpu.make_async_remote_copy(
            src_ref=self.source,
            dst_ref=self.target.at[slot],
            send_sem=self.send_sem,
            recv_sem=self.recv_sem,
            device_id={"lat": pair[0], "chan": pair[1]},
            device_id_type=MESH,
        )

    def local(self, pair):
        return pltpu.make_async_copy(self.source, self.target.at[pair[3]], self.recv_sem)


class Halo:
    def __init__(self, source, target, send_sem, recv_sem):
        self.lat, self.chan = lax.axis_index("lat"), lax.axis_index("chan")
        self.source, self.target = source, target
        self.send_sem, self.recv_sem = send_sem, recv_sem
        self.up, self.down = self.lat < LAT - 1, self.lat > 0

    def copy(self, way):
        step = jnp.where(self.up, 1, -1) if way == 0 else jnp.where(self.down, -1, 1)
        other = self.lat + step
        return pltpu.make_async_remote_copy(
            src_ref=self.source.at[way],
            dst_ref=self.target.at[way],
            send_sem=self.send_sem.at[way],
            recv_sem=self.recv_sem.at[way],
            device_id={"lat": other, "chan": self.chan},
            device_id_type=MESH,
        )

    def start(self):
        pl.when(self.up)(lambda: self.copy(0).start())
        pl.when(self.down)(lambda: self.copy(1).start())

    def arrive(self):
        pl.when(self.down)(lambda: self.copy(0).wait_recv())
        pl.when(self.up)(lambda: self.copy(1).wait_recv())

    def leave(self):
        pl.when(self.up)(lambda: self.copy(0).wait_send())
        pl.when(self.down)(lambda: self.copy(1).wait_send())


CHUNKS = [(k * 128, min(128, NLON - k * 128)) for k in range(12)]
EDGES = (14, 15, 0, 1)


def edge_rows(f, field, part, out_ref):
    for k, (low, size) in enumerate(CHUNKS):
        slot = k % 4
        part[slot, :768, :size] = field[:, low : low + size].astype(jnp.float32)
        for r, i in enumerate(EDGES):
            row = part[slot, pl.ds(i, 48, stride=16), :]
            out_ref[r // 2, f, r % 2, :, low : low + size] = row[:, :size].astype(jnp.bfloat16)


def band_block(info, target, source, same):
    relative = (source - target).astype(jnp.float32) - info[:, 0:1]
    total = jnp.zeros(relative.shape, jnp.float32)
    for k in range(4):
        keep = (relative == float(k)) & (info[:, 1:2] > float(k)) & same
        total = total + jnp.where(keep, info[:, 2 + k : 3 + k], 0.0)
    return total


def halo_place(index):
    edge = index // 16
    return jnp.where(edge < 2, edge - HALO, edge + ROWS - HALO)


def residuals(fields, edges, bands, outs):
    lat = lax.axis_index("lat")
    own = bands[lat].astype(jnp.float32)
    below = bands[jnp.maximum(lat - 1, 0)].astype(jnp.float32)
    above = bands[jnp.minimum(lat + 1, LAT - 1)].astype(jnp.float32)
    own = jnp.concatenate([own] * 16, axis=0)
    near = [below[14:15], below[15:16], above[0:1], above[1:2]]
    near = jnp.concatenate([jnp.broadcast_to(x, (16, 128)) for x in near], axis=0)

    row, column = iota((256, 256), 0), iota((256, 256), 1)
    inner = band_block(own, row % 16, column % 16, row // 16 == column // 16)
    row, column = iota((256, 64), 0), iota((256, 64), 1)
    outer = band_block(own, row % 16, halo_place(column), row // 16 == column % 16)
    row, column = iota((64, 256), 0), iota((64, 256), 1)
    outer_back = band_block(near, halo_place(row), column % 16, row % 16 == column // 16)
    left = (
        (inner.astype(jnp.bfloat16), outer.astype(jnp.bfloat16)),
        (inner.T.astype(jnp.bfloat16), outer_back.T.astype(jnp.bfloat16)),
    )
    for low, size in ((0, 512), (512, 512), (1024, 416)):
        live = (lat > 0, lat < LAT - 1)
        for b in range(3):
            for f in range(2):
                rim = [
                    jnp.where(live[r // 2], edges[r // 2, f, r % 2, 16 * b : 16 * b + 16, low : low + size].astype(jnp.float32), 0.0)
                    for r in range(4)
                ]
                rim = jnp.concatenate(rim, axis=0).astype(jnp.bfloat16)
                rows = slice(256 * b, 256 * b + 256)
                value = dense(left[f][0], fields[f][rows, low : low + size]) + dense(left[f][1], rim)
                outs[f][rows, low : low + size] = value.astype(jnp.bfloat16)


def meet(links):
    barrier = pltpu.get_barrier_semaphore()
    total = jnp.int32(0)
    for link in links:
        total = link.greet(barrier, total)
    return lambda: pl.semaphore_wait(barrier, total)


def block_kernel(
    start_ref, width_ref, coef_ref, weight_ref, source_hbm, grad_hbm, lon_first, lon_second,
    norm_ref, cosine_ref, log_sine_ref, quad_ref, pick_ref, pick_t_ref,
    parts_ref, ahead_ref, behind_ref, forward_ref, backward_ref,
    part, rows, table, near, far, message, landing, info_ref, bands, spectral, received,
    weights, wide, before, after, reply, grads, answers, grids,
    fields, sums, edges, rim, field_sem, sum_sem, edge_send, edge_recv,
    info_send, info_recv, panel_send, panel_recv, *sems
):
    panels = Bulk(lat_to, lat_from, False, message, landing, (panel_send, panel_recv, None))
    grid_panels = Wire(lat_to, lat_from, False, message, grids, sems[12:15])
    spectral_to, spectral_from, degree_owner = spectral_maps()
    degrees = Wire(spectral_to, spectral_from, True, spectral, received, sems[0:3])
    replies = Wire(spectral_from, degree_owner, True, reply, answers, sems[3:6])
    info = Whole(whole_to, whole_from, False, info_ref, bands, (info_send, info_recv, None))
    side = Side(False, weight_ref, weights, sems[6:9])
    grad_side = Side(True, grads, parts_ref, sems[9:12])
    halo = Halo(edges, rim, edge_send, edge_recv)
    loads = [
        pltpu.make_async_copy(ref, fields.at[f], field_sem.at[f])
        for f, ref in ((0, source_hbm), (1, grad_hbm))
    ]
    stores = [
        pltpu.make_async_copy(sums.at[f], ref, sum_sem.at[f])
        for f, ref in ((0, ahead_ref), (1, behind_ref))
    ]
    for load in loads:
        load.start()
    band_info(start_ref, width_ref, coef_ref, info_ref)
    met = meet([panels, degrees, replies, side])
    transform_kernel(fields, (lon_first, lon_second), loads, part)
    met()
    info.start_all()
    side.start()
    spread_kernel(message, part, rows, panels)
    for f in range(2):
        edge_rows(f, fields.at[f], part, edges)
    halo.start()
    recurrence(norm_ref, cosine_ref, log_sine_ref, table)
    info.arrive()
    finish_tables(quad_ref, bands, near, far, table)
    panels.arrive()
    analysis_kernel(landing, near, spectral)
    degrees.start_all()
    side.finish()
    widen(weights, pick_ref, wide)
    info.leave()
    panels.leave()
    halo.leave()
    degrees.arrive()
    mixing_kernel(received, wide, pick_t_ref, reply, grads, before, after)
    replies.start_all()
    degrees.leave()
    replies.arrive()
    synthesis_kernel(answers, far, message)
    grid_panels.start_all()
    grad_side.start()
    halo.arrive()
    residuals([fields.at[0], fields.at[1]], rim, bands, [sums.at[0], sums.at[1]])
    for store in stores:
        store.start()
    replies.leave()
    gather_kernel(grids, forward_ref, backward_ref, part, rows, grid_panels)
    grid_panels.leave()
    grad_side.finish()
    for store in stores:
        store.wait()


def link_sems(counts):
    out = []
    for count in counts:
        out += [pltpu.SemaphoreType.DMA((count,))] * 2 + [pltpu.SemaphoreType.DMA]
    return out


def linked(kernel, collective_id, shapes, out_spaces, scratch, spaces, arrays):
    def spec(space):
        return pl.BlockSpec(memory_space=space)

    return pl.pallas_call(
        kernel,
        out_shape=shapes,
        in_specs=[spec(space) for space in spaces],
        out_specs=[spec(space) for space in out_spaces],
        scratch_shapes=scratch,
        compiler_params=pltpu.CompilerParams(
            collective_id=collective_id, has_side_effects=True, vmem_limit_bytes=VMEM_LIMIT
        ),
    )(*arrays)


def dot(spec, a, b):
    return jnp.einsum(spec, a, b, preferred_element_type=jnp.float32)


def per_device(source_field, band_start, band_width, band_coef, mixing_weight, output_grad):
    channels = source_field.shape[0]
    plain, moved = fourier_table(0), fourier_table(64)
    scales = (1.0 / math.sqrt(NLON), 1.0 / math.sqrt(MMAX))
    analysis, moved_analysis, synthesis, moved_synthesis = [
        jnp.asarray((x * scale).astype(jnp.bfloat16))
        for x, scale in (
            (plain, scales[0]), (moved.T, scales[0]), (plain.T, scales[1]), (moved, scales[1])
        )
    ]
    flat = channels * ROWS

    vmem, anywhere = pltpu.VMEM, pl.ANY
    pick = np.zeros((CHAN, channels, CHAN, 64), np.float32)
    for e in range(CHAN):
        pick[e, :, e, :channels] = np.eye(channels)
    pick = pick.reshape(CHAN * channels, 512)

    def held(*shape):
        return vmem(shape, jnp.bfloat16)

    def panel(*shape):
        return vmem(shape, jnp.float32)

    grad_parts, ahead, behind, forward, backward = linked(
        block_kernel,
        1,
        [
            bf16(CHAN, 6, channels, CHAN * channels),
            bf16(flat, NLON),
            bf16(flat, NLON),
            bf16(flat, 512),
            bf16(flat, 512),
        ],
        [anywhere] * 3 + [vmem] * 2,
        [
            panel(6, flat + 16, 128),
            panel(2, MMAX * ROWS + 16, 128),
            panel(4, 2048 + 256, 128),
            held(12, 256, NLAT),
            held(12, NLAT, 256),
            held(LAT, 9, ROWS, 128),
            held(LAT, 9, ROWS, 128),
            held(ROWS, 128),
            held(LAT, ROWS, 128),
            held(LAT, 64, 128),
            held(LAT, 64, 128),
            held(CHAN, 6, channels, CHAN * channels),
            held(6, 512, 512),
            panel(2, CHAN, 192 + 8, 128),
            panel(2, CHAN, 192 + 8, 128),
            held(LAT, 64, 128),
            held(CHAN, 6, channels, CHAN * channels),
            held(LAT, 64, 128),
            held(LAT, 9, ROWS, 128),
            held(2, flat, NLON),
            held(2, flat, NLON),
            held(2, 2, 2, channels, NLON),
            held(2, 2, 2, channels, NLON),
        ]
        + [pltpu.SemaphoreType.DMA((2,))] * 4
        + [pltpu.SemaphoreType.DMA] * 4
        + link_sems([LAT, LAT, CHAN, CHAN, LAT]),
        [pltpu.SMEM] * 2 + [vmem] + [anywhere] * 3 + [vmem] * 8,
        [
            band_start,
            band_width,
            band_coef,
            mixing_weight,
            source_field.reshape(flat, NLON),
            output_grad.reshape(flat, NLON),
            analysis,
            moved_synthesis,
            *legendre_inputs(),
            jnp.asarray(pick.astype(jnp.bfloat16)),
            jnp.asarray(pick.T.astype(jnp.bfloat16)),
        ],
    )
    def rowwise(*block):
        return pl.BlockSpec(block, lambda i: (i,) + (0,) * (len(block) - 1))

    def fixed(*block):
        return pl.BlockSpec(block, lambda i: (0, 0))

    return pl.pallas_call(
        tail_kernel,
        grid=(3,),
        out_shape=[
            bf16(channels, ROWS, NLON),
            bf16(channels, ROWS, NLON),
            jax.ShapeDtypeStruct((6, channels, CHAN * channels), jnp.float32),
        ],
        in_specs=[rowwise(flat // 3, 512)] * 2
        + [rowwise(flat // 3, NLON)] * 2
        + [fixed(512, NLON)] * 2
        + [pl.BlockSpec((CHAN, 2, channels, CHAN * channels), lambda i: (0, i, 0, 0))],
        out_specs=[rowwise(channels // 3, ROWS, NLON)] * 2
        + [rowwise(2, channels, CHAN * channels)],
        compiler_params=pltpu.CompilerParams(vmem_limit_bytes=VMEM_LIMIT),
    )(forward, backward, ahead, behind, synthesis, moved_analysis, grad_parts)


def solution(mesh):
    in_specs = (
        P("chan", "lat", None),
        P("lat"),
        P("lat"),
        P("lat", None),
        P("lat", "chan", None),
        P("chan", "lat", None),
    )
    out_specs = (P("chan", "lat", None), P("chan", "lat", None), P("lat", "chan", None))
    return jax.shard_map(
        per_device, mesh=mesh, in_specs=in_specs, out_specs=out_specs, check_vma=False
    )
```

```python
import functools
import math

import jax
import jax.numpy as jnp
import numpy as np
from jax import lax
from jax.experimental import pallas as pl
from jax.experimental.pallas import tpu as pltpu
from jax.sharding import PartitionSpec as P

NLAT = 512
NLON = 1440
MMAX = 192
LMAX = 192
HALO = 2
LAT = 32
CHAN = 8
MODES = MMAX // LAT
ROWS = NLAT // LAT
MESH = pl.DeviceIdType.MESH
VMEM_LIMIT = 58 * 1024 * 1024


def log_norms():
    return np.array(
        [
            0.5
            * (
                math.log((2.0 * m + 1.0) / (4.0 * math.pi))
                + math.lgamma(m + 0.5)
                - math.lgamma(m + 1.0)
                - 0.5 * math.log(math.pi)
            )
            for m in range(MMAX)
        ],
        np.float32,
    )


def fourier_table(shift):
    phase = 2.0 * math.pi / NLON * (np.outer(np.arange(NLON), np.arange(MMAX)) % NLON)
    table = np.zeros((NLON, 2, 256))
    places = np.concatenate([np.arange(128), np.arange(128, MMAX) + shift])
    table[:, 0, places] = np.cos(phase)
    table[:, 1, places] = -np.sin(phase)
    return table.reshape(NLON, 512)


def dense(a, b, dims=((1,), (0,))):
    return lax.dot_general(a, b, (dims, ((), ())), preferred_element_type=jnp.float32)


def iota(shape, axis):
    return lax.broadcasted_iota(jnp.int32, shape, axis)


def merge_lanes(a, b, c, d):
    lane = iota(a.shape, 1)
    return (
        jnp.where(lane < 96, a, b),
        jnp.where(lane < 64, b, c),
        jnp.where(lane < 32, c, d),
    )


def split_lanes(tiles):
    lane = iota(tiles[0].shape, 1)
    units = []
    for g in range(0, 9, 3):
        t0, t1, t2 = tiles[g : g + 3]
        units += [t0, jnp.where(lane < 64, t1, t0), jnp.where(lane < 32, t2, t1), t2]
    return units


def merge_rows(tiles):
    row = iota(tiles[0].shape, 0) % 8
    out = list(tiles[:8])
    for k in range(3):
        out[k] = jnp.where(row < 6, tiles[k], pltpu.roll(tiles[8], 6 - 2 * k, 0))
    return out


def split_rows(tiles):
    rows = tiles[0].shape[0]
    row = iota(tiles[0].shape, 0) % 8
    back = [pltpu.roll(tiles[k], rows - (6 - 2 * k), 0) for k in range(3)]
    return list(tiles) + [jnp.where(row < 2, back[0], jnp.where(row < 4, back[1], back[2]))]


def store_rows(out_ref, tiles):
    for p in range(4):
        pair = [tiles[2 * p + k].reshape(LAT, 8, 128) for k in range(2)]
        out_ref[:, 16 * p : 16 * p + 16, :] = jnp.concatenate(pair, axis=1).astype(jnp.bfloat16)


def load_rows(in_ref, live):
    tiles = []
    for p in range(4):
        pair = in_ref[:, 16 * p : 16 * p + 16, :].astype(jnp.float32)
        pair = jnp.where(live, pair, 0.0)
        tiles += [pair[:, :8].reshape(256, 128), pair[:, 8:].reshape(256, 128)]
    return tiles


def transform_kernel(fields, tables, loads, part):
    for f in range(2):
        loads[f].wait()

        def transform(b, carry):
            block = pl.ds(pl.multiple_of(b * 256, 256), 256)
            panel = dense(fields[f, block, :], tables[f][...])
            part[2 * f, block, :] = panel[:, :128]
            part[2 * f + 1, block, :] = panel[:, 256:384]
            for r in range(2):
                half = panel[:, 256 * r + 128 : 256 * r + 256]
                part[4 + r, block, :] = half if f == 0 else part[4 + r, block, :] + half
            return carry

        lax.fori_loop(0, 3, transform, 0)


def spread_kernel(out_ref, part, rows, link):
    def turn(i, carry):
        for k in range(3):
            a = part[2 * k, pl.ds(i, 48, stride=16), :]
            b = part[2 * k + 1, pl.ds(i, 48, stride=16), :]
            block = jnp.concatenate([a, b, a[:32]], axis=0).T
            if k < 2:
                rows[k, pl.ds(i, 128, stride=16), :] = block
            else:
                rows[0, pl.ds(2048 + i, 64, stride=16), :] = block[:64]
                rows[1, pl.ds(2048 + i, 64, stride=16), :] = block[64:]
        return carry

    lax.fori_loop(0, ROWS, turn, 0)

    def send(step, carry):
        d = wrap(link.lat + step, LAT)
        units = [
            rows[f, pl.ds(pl.multiple_of((d * 6 + m) * 16, 16), 16), :]
            for f in range(2)
            for m in range(MODES)
        ]
        for g in range(3):
            a, b, c, e = units[4 * g : 4 * g + 4]
            tiles = merge_lanes(a, pltpu.roll(b, 96, 1), pltpu.roll(c, 64, 1), pltpu.roll(e, 32, 1))
            for k in range(3):
                out_ref[d, 3 * g + k] = tiles[k].astype(jnp.bfloat16)
        link.start(step)
        return carry

    lax.fori_loop(0, LAT, send, 0)


def gather_kernel(in_ref, source_ref, grad_ref, part, rows, link):
    def receive(step, carry):
        d = link.arrive_one(step)
        tiles = [in_ref[d, k].astype(jnp.float32) for k in range(9)]
        units = split_lanes(tiles)
        for u in range(12):
            if u % 4:
                units[u] = pltpu.roll(units[u], 32 * (u % 4), 1)
            rows[u // 6, pl.ds(pl.multiple_of((d * 6 + u % 6) * 16, 16), 16), :] = units[u]
        return carry

    lax.fori_loop(0, LAT, receive, 0)

    def turn(i, carry):
        first = rows[0, pl.ds(i, MMAX, stride=16), :]
        second = rows[1, pl.ds(i, MMAX, stride=16), :]
        blocks = (
            first[:128], second[:128], jnp.concatenate([first[128:], second[128:]], axis=0)
        )
        for k in range(3):
            flat = blocks[k].T
            part[2 * k, pl.ds(i, 48, stride=16), :] = flat[:48]
            part[2 * k + 1, pl.ds(i, 48, stride=16), :] = flat[48:96]
        return carry

    lax.fori_loop(0, ROWS, turn, 0)
    for r in range(2):
        low = 256 * r
        half = part[4 + r, :768, :].astype(jnp.bfloat16)
        for f, ref in ((0, source_ref), (1, grad_ref)):
            ref[:, low : low + 128] = part[2 * f + r, :768, :].astype(jnp.bfloat16)
            ref[:, low + 128 : low + 256] = half


def recurrence(norm_ref, cosine_ref, log_sine_ref, table):
    lat = lax.axis_index("lat")
    order = (iota((8, NLAT), 0) + lat * MODES).astype(jnp.float32)
    cosine = jnp.broadcast_to(cosine_ref[...], (8, NLAT))
    sector = jnp.exp(norm_ref[lat][:, 0:1] + order * jnp.broadcast_to(log_sine_ref[...], (8, NLAT)))
    order_sq = order * order
    table[...] = jnp.zeros_like(table)

    def advance(degree_index, carry):
        previous, earlier = carry
        degree = jnp.full((8, NLAT), degree_index, jnp.int32).astype(jnp.float32)
        lower = degree - 1.0
        scale_a = jnp.sqrt(
            jnp.maximum(4.0 * degree * degree - 1.0, 0.0)
            / jnp.maximum(degree * degree - order_sq, 1.0)
        )
        scale_b = jnp.sqrt(
            jnp.maximum(lower * lower - order_sq, 0.0)
            / jnp.maximum(4.0 * lower * lower - 1.0, 1.0)
        )
        value = scale_a * (cosine * previous - scale_b * earlier)
        value = jnp.where(degree < order, 0.0, jnp.where(degree == order, sector, value))
        place = LMAX - 1 - degree_index
        row = place // 6 * 8 + place % 6
        for k in range(4):
            table[k, pl.ds(row, 8, stride=256), :] = value[:, 128 * k : 128 * k + 128]
        return value, previous

    zero = sector * 0.0
    lax.fori_loop(0, LMAX, advance, (zero, zero))


def finish_tables(quad_ref, band_ref, near_ref, far_ref, table):
    info = band_ref[...].reshape(NLAT, 128).astype(jnp.float32)
    relative = (iota((NLAT, NLAT), 1) - iota((NLAT, NLAT), 0)).astype(jnp.float32) - info[:, 0:1]
    band = jnp.zeros((NLAT, NLAT), jnp.float32)
    for k in range(4):
        keep = (relative == float(k)) & (info[:, 1:2] > float(k))
        band = band + jnp.where(keep, info[:, 2 + k : 3 + k], 0.0)
    band = band.astype(jnp.bfloat16)
    for m in range(MODES):
        own = jnp.concatenate([table[k, 256 * m : 256 * m + 256, :] for k in range(4)], axis=1)
        analysis = (own * quad_ref[...]).astype(jnp.bfloat16)
        banded = dense(analysis, band)
        synthesis = own * (1.0 / math.sqrt(LMAX))
        near_ref[m] = banded.astype(jnp.bfloat16)
        near_ref[MODES + m] = synthesis.astype(jnp.bfloat16)
        far_ref[m] = synthesis.T.astype(jnp.bfloat16)
        far_ref[MODES + m] = banded.T.astype(jnp.bfloat16)


def analysis_kernel(in_ref, table_ref, out_ref):
    tiles = [in_ref[:, k].reshape(NLAT, 128).astype(jnp.float32) for k in range(9)]
    units = split_lanes(tiles)
    units = [dense(table_ref[u], units[u].astype(jnp.bfloat16)) for u in range(12)]
    packed = []
    for g in range(3):
        packed += merge_lanes(*units[4 * g : 4 * g + 4])
    store_rows(out_ref, merge_rows(packed))


def synthesis_kernel(in_ref, table_ref, out_ref):
    live = iota((LAT, 16, 128), 0) + lax.axis_index("lat") < LAT
    units = split_lanes(split_rows(load_rows(in_ref, live)))
    units = [dense(table_ref[u], units[u].astype(jnp.bfloat16)) for u in range(12)]
    for g in range(3):
        tiles = merge_lanes(*units[4 * g : 4 * g + 4])
        for k in range(3):
            out_ref[:, 3 * g + k] = tiles[k].reshape(LAT, ROWS, 128).astype(jnp.bfloat16)


def widen(weight_ref, pick_ref, wide):
    def degree(l, carry):
        rows = []
        for e in range(CHAN):
            rows += [weight_ref[e, l], jnp.zeros((16, 384), jnp.bfloat16)]
        wide[l] = dense(jnp.concatenate(rows, axis=0), pick_ref[...]).astype(jnp.bfloat16)
        return carry

    lax.fori_loop(0, 6, degree, 0)


def mixing_kernel(in_ref, wide, pick_t_ref, out_ref, grad_ref, before, after):
    lat, chan = lax.axis_index("lat"), lax.axis_index("chan")
    slot = iota((LAT, 16, 128), 0)
    other = (2 * (slot % 4) + lax.rem(chan, 2)) * 4 + lax.div(chan, 2)
    units = split_lanes(split_rows(load_rows(in_ref, other + lat < LAT)))
    for u in range(12):
        if u % 4:
            units[u] = pltpu.roll(units[u], 32 * (u % 4), 1)
        f, m = u // 6, u % 6
        before[f, :, 32 * m : 32 * m + 32, :] = units[u].reshape(CHAN, 32, 128)
    after[...] = jnp.zeros_like(after)
    lane = iota((24, 128), 1)

    def degree(l, carry):
        left = []
        for f in range(2):
            columns = []
            for p in range(4):
                a = before[f, 2 * p, pl.ds(l, 24, stride=8), :]
                b = before[f, 2 * p + 1, pl.ds(l, 24, stride=8), :]
                first = jnp.where(lane < 64, a, pltpu.roll(b, 64, 1))
                second = jnp.where(lane < 64, pltpu.roll(a, 80, 1), pltpu.roll(b, 16, 1))
                columns.append(jnp.concatenate([first, second], axis=0))
            left.append(jnp.concatenate(columns, axis=1).astype(jnp.bfloat16))
        weight = wide[l]
        mixed = dense(left[0], weight)
        back = dense(left[1], weight, ((1,), (1,)))
        dense_back = dense(left[1], pick_t_ref[...]).astype(jnp.bfloat16)
        grad = dense(left[0], dense_back, ((0,), (0,)))
        for e in range(CHAN):
            grad_ref[e, l] = grad[64 * e : 64 * e + 48].astype(jnp.bfloat16)
            for f, value in ((0, mixed), (1, back)):
                tile = value[:, 128 * (e // 2) : 128 * (e // 2) + 128]
                first, second = tile[:24], tile[24:]
                if e % 2:
                    first = pltpu.roll(first, 64, 1)
                second = pltpu.roll(second, 112 if e % 2 else 48, 1)
                after[f, e, pl.ds(l, 24, stride=8), :] = jnp.where(lane < 48, first, second)
        return carry

    lax.fori_loop(0, 6, degree, 0)
    units = [after[u // 6, :, 32 * (u % 6) : 32 * (u % 6) + 32, :].reshape(256, 128) for u in range(12)]
    packed = []
    for g in range(3):
        a, b, c, d = units[4 * g : 4 * g + 4]
        packed += merge_lanes(a, pltpu.roll(b, 96, 1), pltpu.roll(c, 64, 1), pltpu.roll(d, 32, 1))
    store_rows(out_ref, merge_rows(packed))


def tail_kernel(
    forward_ref, backward_ref, ahead_ref, behind_ref, first_ref, second_ref, parts_ref,
    mixed_ref, input_ref, grad_ref
):
    for panel, table, extra, out in (
        (forward_ref, first_ref, ahead_ref, mixed_ref),
        (backward_ref, second_ref, behind_ref, input_ref),
    ):
        value = dense(panel[...], table[...]) + extra[...].astype(jnp.float32)
        out[...] = value.astype(jnp.bfloat16).reshape(out.shape)
    grad_ref[...] = jnp.sum(parts_ref[...].astype(jnp.float32), axis=0)


def bf16(*shape):
    return jax.ShapeDtypeStruct(shape, jnp.bfloat16)


def legendre_inputs():
    theta = math.pi * (np.arange(NLAT, dtype=np.float64) + 0.5) / NLAT
    sine = np.sin(theta)
    norm = np.zeros((LAT, 8, 128), np.float32)
    norm[:, :MODES] = log_norms().reshape(LAT, MODES, 1)
    quadrature = math.sqrt(NLAT) * math.pi / NLAT * sine
    flat = [np.cos(theta), np.log(sine), quadrature]
    return [jnp.asarray(norm)] + [jnp.asarray(x.astype(np.float32)[None, :]) for x in flat]


def band_info(start_ref, width_ref, coef_ref, out_ref):
    row, lane = iota((ROWS, 128), 0), iota((ROWS, 128), 1)
    coef = coef_ref[...].astype(jnp.float32)
    total = pltpu.roll(jnp.concatenate([coef, jnp.zeros((ROWS, 124), jnp.float32)], axis=1), 2, 1)
    for i in range(ROWS):
        total = jnp.where((row == i) & (lane == 0), start_ref[i].astype(jnp.float32), total)
        total = jnp.where((row == i) & (lane == 1), width_ref[i].astype(jnp.float32), total)
    out_ref[...] = total.astype(jnp.bfloat16)


def wrap(value, size):
    return value - jnp.where(value >= size, size, 0)


def lat_to(step, lat, chan):
    other = wrap(lat + step, LAT)
    return other, chan, other, lat


def spectral_maps():
    lat, chan = lax.axis_index("lat"), lax.axis_index("chan")
    low = lax.rem(lat, 4)
    group = 2 * low + lax.rem(lax.div(lat, 4), 2)
    slot = chan * 4 + lax.div(lat, 8)
    base = lax.rem(chan, 2) * 4 + lax.div(chan, 2)

    def spectral_to(step, lat, chan):
        other = wrap(lat + step[0] * 4 + step[1], LAT)
        return other, group, other, slot

    def spectral_from(step, lat, chan):
        part = wrap(low + step[1], 4)
        near = wrap(chan + step[0], CHAN)
        return part * 8 + base, near, near * 4 + part, lat

    def degree_owner(step, lat, chan):
        other = wrap(lat + LAT - step[0] * 4 - step[1], LAT)
        return other, group, other, 0

    return spectral_to, spectral_from, degree_owner


class Wire:
    def __init__(self, sends, receives, skip, source, target, sems):
        self.lat, self.chan = lax.axis_index("lat"), lax.axis_index("chan")
        self.sends, self.receives, self.skip = sends, receives, skip
        self.source, self.target = source, target
        self.send_sem, self.recv_sem, self.own_sem = sems

    def each(self, body, carry):
        if not self.skip:
            return lax.fori_loop(0, LAT, body, carry)

        def four(outer, carry):
            for inner in range(4):
                carry = body((outer, inner), carry)
            return carry

        return lax.fori_loop(0, LAT // 4, four, carry)

    def live(self, pair):
        if self.skip:
            return self.lat + pair[0] < LAT
        return pair[0] >= 0

    def own(self, pair):
        return (pair[0] == self.lat) & (pair[1] == self.chan) & self.live(pair)

    def far(self, pair):
        return jnp.logical_not((pair[0] == self.lat) & (pair[1] == self.chan)) & self.live(pair)

    def greet(self, barrier, total):
        def step_fn(step, count):
            source = self.receives(step, self.lat, self.chan)

            @pl.when(self.far(source))
            def _():
                pl.semaphore_signal(
                    barrier, inc=1, device_id={"lat": source[0], "chan": source[1]},
                    device_id_type=MESH,
                )

            return count + jnp.where(self.far(self.sends(step, self.lat, self.chan)), 1, 0)

        return self.each(step_fn, total)

    def remote(self, pair, slot):
        return pltpu.make_async_remote_copy(
            src_ref=self.source.at[pair[2]],
            dst_ref=self.target.at[slot],
            send_sem=self.send_sem.at[pair[2]],
            recv_sem=self.recv_sem.at[slot],
            device_id={"lat": pair[0], "chan": pair[1]},
            device_id_type=MESH,
        )

    def local(self, pair):
        return pltpu.make_async_copy(
            self.source.at[pair[2]], self.target.at[pair[3]], self.own_sem
        )

    def start(self, step):
        pair = self.sends(step, self.lat, self.chan)

        @pl.when(self.own(pair))
        def _():
            self.local(pair).start()

        @pl.when(self.far(pair))
        def _():
            self.remote(pair, pair[3]).start()

    def start_all(self):
        def step_fn(step, carry):
            self.start(step)
            return carry

        self.each(step_fn, 0)

    def arrive_one(self, step):
        target = self.sends(step, self.lat, self.chan)
        source = self.receives(step, self.lat, self.chan)

        @pl.when(self.own(target))
        def _():
            self.local(target).wait()

        @pl.when(self.far(source))
        def _():
            self.remote(source, source[2]).wait_recv()

        return source[2]

    def arrive(self):
        def step_fn(step, carry):
            self.arrive_one(step)
            return carry

        self.each(step_fn, 0)

    def leave(self):
        def step_fn(step, carry):
            target = self.sends(step, self.lat, self.chan)

            @pl.when(self.far(target))
            def _():
                self.remote(target, target[3]).wait_send()

            return carry

        self.each(step_fn, 0)


class Side:
    def __init__(self, parts, source, target, sems):
        self.lat, self.chan = lax.axis_index("lat"), lax.axis_index("chan")
        self.parts, self.source, self.target = parts, source, target
        self.send_sem, self.recv_sem, self.own_sem = sems

    def greet(self, barrier, total):
        def step_fn(step, count):
            pl.semaphore_signal(
                barrier, inc=1,
                device_id={"lat": self.lat, "chan": lax.rem(self.chan + step, CHAN)},
                device_id_type=MESH,
            )
            return count + 1

        return lax.fori_loop(1, CHAN, step_fn, total)

    def remote(self, step, incoming):
        other = lax.rem(self.chan + step, CHAN)
        slot = other if incoming else self.chan
        return pltpu.make_async_remote_copy(
            src_ref=self.source.at[other] if self.parts else self.source,
            dst_ref=self.target.at[slot],
            send_sem=self.send_sem.at[other],
            recv_sem=self.recv_sem.at[slot],
            device_id={"lat": self.lat, "chan": other},
            device_id_type=MESH,
        )

    def local(self):
        source = self.source.at[self.chan] if self.parts else self.source
        return pltpu.make_async_copy(source, self.target.at[self.chan], self.own_sem)

    def start(self):
        self.local().start()

        def step_fn(step, carry):
            self.remote(step, False).start()
            return carry

        lax.fori_loop(1, CHAN, step_fn, 0)

    def finish(self):
        self.local().wait()

        def step_fn(step, carry):
            self.remote(step, False).wait_send()
            self.remote(step, True).wait_recv()
            return carry

        lax.fori_loop(1, CHAN, step_fn, 0)


def lat_from(step, lat, chan):
    return lat_to(LAT - step, lat, chan)


def whole_to(step, lat, chan):
    other = wrap(lat + step, LAT)
    return other, chan, 0, lat


def whole_from(step, lat, chan):
    other = wrap(lat + LAT - step, LAT)
    return other, chan, other, lat


class Bulk(Wire):
    def remote(self, pair, slot):
        return pltpu.make_async_remote_copy(
            src_ref=self.source.at[pair[2]],
            dst_ref=self.target.at[slot],
            send_sem=self.send_sem,
            recv_sem=self.recv_sem,
            device_id={"lat": pair[0], "chan": pair[1]},
            device_id_type=MESH,
        )

    def local(self, pair):
        return pltpu.make_async_copy(
            self.source.at[pair[2]], self.target.at[pair[3]], self.recv_sem
        )

    def arrive(self):
        pltpu.make_async_copy(self.target, self.target, self.recv_sem).wait()

    def leave(self):
        sent = self.target.at[pl.ds(0, LAT - 1)]
        pltpu.make_async_copy(sent, sent, self.send_sem).wait()


class Whole(Bulk):
    def remote(self, pair, slot):
        return pltpu.make_async_remote_copy(
            src_ref=self.source,
            dst_ref=self.target.at[slot],
            send_sem=self.send_sem,
            recv_sem=self.recv_sem,
            device_id={"lat": pair[0], "chan": pair[1]},
            device_id_type=MESH,
        )

    def local(self, pair):
        return pltpu.make_async_copy(self.source, self.target.at[pair[3]], self.recv_sem)


class Halo:
    def __init__(self, source, target, send_sem, recv_sem):
        self.lat, self.chan = lax.axis_index("lat"), lax.axis_index("chan")
        self.source, self.target = source, target
        self.send_sem, self.recv_sem = send_sem, recv_sem
        self.up, self.down = self.lat < LAT - 1, self.lat > 0

    def copy(self, way):
        step = jnp.where(self.up, 1, -1) if way == 0 else jnp.where(self.down, -1, 1)
        other = self.lat + step
        return pltpu.make_async_remote_copy(
            src_ref=self.source.at[way],
            dst_ref=self.target.at[way],
            send_sem=self.send_sem.at[way],
            recv_sem=self.recv_sem.at[way],
            device_id={"lat": other, "chan": self.chan},
            device_id_type=MESH,
        )

    def start(self):
        pl.when(self.up)(lambda: self.copy(0).start())
        pl.when(self.down)(lambda: self.copy(1).start())

    def arrive(self):
        pl.when(self.down)(lambda: self.copy(0).wait_recv())
        pl.when(self.up)(lambda: self.copy(1).wait_recv())

    def leave(self):
        pl.when(self.up)(lambda: self.copy(0).wait_send())
        pl.when(self.down)(lambda: self.copy(1).wait_send())


CHUNKS = [(k * 128, min(128, NLON - k * 128)) for k in range(12)]
EDGES = (14, 15, 0, 1)


def edge_rows(f, field, part, out_ref):
    for k, (low, size) in enumerate(CHUNKS):
        slot = k % 4
        part[slot, :768, :size] = field[:, low : low + size].astype(jnp.float32)
        for r, i in enumerate(EDGES):
            row = part[slot, pl.ds(i, 48, stride=16), :]
            out_ref[r // 2, f, r % 2, :, low : low + size] = row[:, :size].astype(jnp.bfloat16)


def band_block(info, target, source, same):
    relative = (source - target).astype(jnp.float32) - info[:, 0:1]
    total = jnp.zeros(relative.shape, jnp.float32)
    for k in range(4):
        keep = (relative == float(k)) & (info[:, 1:2] > float(k)) & same
        total = total + jnp.where(keep, info[:, 2 + k : 3 + k], 0.0)
    return total


def halo_place(index):
    edge = index // 16
    return jnp.where(edge < 2, edge - HALO, edge + ROWS - HALO)


def residuals(fields, edges, bands, outs):
    lat = lax.axis_index("lat")
    own = bands[lat].astype(jnp.float32)
    below = bands[jnp.maximum(lat - 1, 0)].astype(jnp.float32)
    above = bands[jnp.minimum(lat + 1, LAT - 1)].astype(jnp.float32)
    own = jnp.concatenate([own] * 16, axis=0)
    near = [below[14:15], below[15:16], above[0:1], above[1:2]]
    near = jnp.concatenate([jnp.broadcast_to(x, (16, 128)) for x in near], axis=0)

    row, column = iota((256, 256), 0), iota((256, 256), 1)
    inner = band_block(own, row % 16, column % 16, row // 16 == column // 16)
    row, column = iota((256, 64), 0), iota((256, 64), 1)
    outer = band_block(own, row % 16, halo_place(column), row // 16 == column % 16)
    row, column = iota((64, 256), 0), iota((64, 256), 1)
    outer_back = band_block(near, halo_place(row), column % 16, row % 16 == column // 16)
    left = (
        (inner.astype(jnp.bfloat16), outer.astype(jnp.bfloat16)),
        (inner.T.astype(jnp.bfloat16), outer_back.T.astype(jnp.bfloat16)),
    )
    for low, size in ((0, 512), (512, 512), (1024, 416)):
        live = (lat > 0, lat < LAT - 1)
        for b in range(3):
            for f in range(2):
                rim = [
                    jnp.where(live[r // 2], edges[r // 2, f, r % 2, 16 * b : 16 * b + 16, low : low + size].astype(jnp.float32), 0.0)
                    for r in range(4)
                ]
                rim = jnp.concatenate(rim, axis=0).astype(jnp.bfloat16)
                rows = slice(256 * b, 256 * b + 256)
                value = dense(left[f][0], fields[f][rows, low : low + size]) + dense(left[f][1], rim)
                outs[f][rows, low : low + size] = value.astype(jnp.bfloat16)


def meet(links):
    barrier = pltpu.get_barrier_semaphore()
    total = jnp.int32(0)
    for link in links:
        total = link.greet(barrier, total)
    return lambda: pl.semaphore_wait(barrier, total)


def block_kernel(
    start_ref, width_ref, coef_ref, weight_ref, source_hbm, grad_hbm, lon_first, lon_second,
    norm_ref, cosine_ref, log_sine_ref, quad_ref, pick_ref, pick_t_ref,
    parts_ref, ahead_ref, behind_ref, forward_ref, backward_ref,
    part, rows, table, near, far, message, landing, info_ref, bands, spectral, received,
    weights, wide, before, after, reply, grads, answers, grids,
    fields, sums, edges, rim, field_sem, sum_sem, edge_send, edge_recv,
    info_send, info_recv, panel_send, panel_recv, *sems
):
    panels = Bulk(lat_to, lat_from, False, message, landing, (panel_send, panel_recv, None))
    grid_panels = Wire(lat_to, lat_from, False, message, grids, sems[12:15])
    spectral_to, spectral_from, degree_owner = spectral_maps()
    degrees = Wire(spectral_to, spectral_from, True, spectral, received, sems[0:3])
    replies = Wire(spectral_from, degree_owner, True, reply, answers, sems[3:6])
    info = Whole(whole_to, whole_from, False, info_ref, bands, (info_send, info_recv, None))
    side = Side(False, weight_ref, weights, sems[6:9])
    grad_side = Side(True, grads, parts_ref, sems[9:12])
    halo = Halo(edges, rim, edge_send, edge_recv)
    loads = [
        pltpu.make_async_copy(ref, fields.at[f], field_sem.at[f])
        for f, ref in ((0, source_hbm), (1, grad_hbm))
    ]
    stores = [
        pltpu.make_async_copy(sums.at[f], ref, sum_sem.at[f])
        for f, ref in ((0, ahead_ref), (1, behind_ref))
    ]
    for load in loads:
        load.start()
    band_info(start_ref, width_ref, coef_ref, info_ref)
    met = meet([panels, degrees, replies, side])
    transform_kernel(fields, (lon_first, lon_second), loads, part)
    met()
    info.start_all()
    spread_kernel(message, part, rows, panels)
    side.start()
    for f in range(2):
        edge_rows(f, fields.at[f], part, edges)
    halo.start()
    recurrence(norm_ref, cosine_ref, log_sine_ref, table)
    info.arrive()
    finish_tables(quad_ref, bands, near, far, table)
    panels.arrive()
    analysis_kernel(landing, near, spectral)
    degrees.start_all()
    side.finish()
    widen(weights, pick_ref, wide)
    info.leave()
    panels.leave()
    halo.leave()
    degrees.arrive()
    mixing_kernel(received, wide, pick_t_ref, reply, grads, before, after)
    replies.start_all()
    degrees.leave()
    replies.arrive()
    synthesis_kernel(answers, far, message)
    grid_panels.start_all()
    grad_side.start()
    halo.arrive()
    residuals([fields.at[0], fields.at[1]], rim, bands, [sums.at[0], sums.at[1]])
    for store in stores:
        store.start()
    replies.leave()
    gather_kernel(grids, forward_ref, backward_ref, part, rows, grid_panels)
    grid_panels.leave()
    grad_side.finish()
    for store in stores:
        store.wait()


def link_sems(counts):
    out = []
    for count in counts:
        out += [pltpu.SemaphoreType.DMA((count,))] * 2 + [pltpu.SemaphoreType.DMA]
    return out


def linked(kernel, collective_id, shapes, out_spaces, scratch, spaces, arrays):
    def spec(space):
        return pl.BlockSpec(memory_space=space)

    return pl.pallas_call(
        kernel,
        out_shape=shapes,
        in_specs=[spec(space) for space in spaces],
        out_specs=[spec(space) for space in out_spaces],
        scratch_shapes=scratch,
        compiler_params=pltpu.CompilerParams(
            collective_id=collective_id, has_side_effects=True, vmem_limit_bytes=VMEM_LIMIT
        ),
    )(*arrays)


def dot(spec, a, b):
    return jnp.einsum(spec, a, b, preferred_element_type=jnp.float32)


def per_device(source_field, band_start, band_width, band_coef, mixing_weight, output_grad):
    channels = source_field.shape[0]
    plain, moved = fourier_table(0), fourier_table(64)
    scales = (1.0 / math.sqrt(NLON), 1.0 / math.sqrt(MMAX))
    analysis, moved_analysis, synthesis, moved_synthesis = [
        jnp.asarray((x * scale).astype(jnp.bfloat16))
        for x, scale in (
            (plain, scales[0]), (moved.T, scales[0]), (plain.T, scales[1]), (moved, scales[1])
        )
    ]
    flat = channels * ROWS

    vmem, anywhere = pltpu.VMEM, pl.ANY
    pick = np.zeros((CHAN, channels, CHAN, 64), np.float32)
    for e in range(CHAN):
        pick[e, :, e, :channels] = np.eye(channels)
    pick = pick.reshape(CHAN * channels, 512)

    def held(*shape):
        return vmem(shape, jnp.bfloat16)

    def panel(*shape):
        return vmem(shape, jnp.float32)

    grad_parts, ahead, behind, forward, backward = linked(
        block_kernel,
        1,
        [
            bf16(CHAN, 6, channels, CHAN * channels),
            bf16(flat, NLON),
            bf16(flat, NLON),
            bf16(flat, 512),
            bf16(flat, 512),
        ],
        [anywhere] * 3 + [vmem] * 2,
        [
            panel(6, flat + 16, 128),
            panel(2, MMAX * ROWS + 16, 128),
            panel(4, 2048 + 256, 128),
            held(12, 256, NLAT),
            held(12, NLAT, 256),
            held(LAT, 9, ROWS, 128),
            held(LAT, 9, ROWS, 128),
            held(ROWS, 128),
            held(LAT, ROWS, 128),
            held(LAT, 64, 128),
            held(LAT, 64, 128),
            held(CHAN, 6, channels, CHAN * channels),
            held(6, 512, 512),
            panel(2, CHAN, 192 + 8, 128),
            panel(2, CHAN, 192 + 8, 128),
            held(LAT, 64, 128),
            held(CHAN, 6, channels, CHAN * channels),
            held(LAT, 64, 128),
            held(LAT, 9, ROWS, 128),
            held(2, flat, NLON),
            held(2, flat, NLON),
            held(2, 2, 2, channels, NLON),
            held(2, 2, 2, channels, NLON),
        ]
        + [pltpu.SemaphoreType.DMA((2,))] * 4
        + [pltpu.SemaphoreType.DMA] * 4
        + link_sems([LAT, LAT, CHAN, CHAN, LAT]),
        [pltpu.SMEM] * 2 + [vmem] + [anywhere] * 3 + [vmem] * 8,
        [
            band_start,
            band_width,
            band_coef,
            mixing_weight,
            source_field.reshape(flat, NLON),
            output_grad.reshape(flat, NLON),
            analysis,
            moved_synthesis,
            *legendre_inputs(),
            jnp.asarray(pick.astype(jnp.bfloat16)),
            jnp.asarray(pick.T.astype(jnp.bfloat16)),
        ],
    )
    def rowwise(*block):
        return pl.BlockSpec(block, lambda i: (i,) + (0,) * (len(block) - 1))

    def fixed(*block):
        return pl.BlockSpec(block, lambda i: (0, 0))

    return pl.pallas_call(
        tail_kernel,
        grid=(3,),
        out_shape=[
            bf16(channels, ROWS, NLON),
            bf16(channels, ROWS, NLON),
            jax.ShapeDtypeStruct((6, channels, CHAN * channels), jnp.float32),
        ],
        in_specs=[rowwise(flat // 3, 512)] * 2
        + [rowwise(flat // 3, NLON)] * 2
        + [fixed(512, NLON)] * 2
        + [pl.BlockSpec((CHAN, 2, channels, CHAN * channels), lambda i: (0, i, 0, 0))],
        out_specs=[rowwise(channels // 3, ROWS, NLON)] * 2
        + [rowwise(2, channels, CHAN * channels)],
        compiler_params=pltpu.CompilerParams(vmem_limit_bytes=VMEM_LIMIT),
    )(forward, backward, ahead, behind, synthesis, moved_analysis, grad_parts)


def solution(mesh):
    in_specs = (
        P("chan", "lat", None),
        P("lat"),
        P("lat"),
        P("lat", None),
        P("lat", "chan", None),
        P("chan", "lat", None),
    )
    out_specs = (P("chan", "lat", None), P("chan", "lat", None), P("lat", "chan", None))
    return jax.shard_map(
        per_device, mesh=mesh, in_specs=in_specs, out_specs=out_specs, check_vma=False
    )
```
